256 devices in a mesh: tm: 8 (over x, core), row: 4 (over z_hi), col: 8 (over z_lo, y).
Axes of the slice: x: 4, y: 4, z: 8 (z_hi: 4, z_lo: 2; z = z_hi * 2 + z_lo), core: 2. Of those that a mesh axis runs over, the one named last changes fastest.
Arguments:
- records: bfloat16 [384, 2, 16, 2048], P('tm', None, None, ('row', 'col')), may hold values from -6 to 6
- offsets: int32 [8, 8], replicated, may hold values from 0 to 3
Outputs:
- cthree: bfloat16 [2, 16, 2048, 2048], P(None, 'tm', 'row', 'col')
The draws below stay inside these ranges and needn't reach their ends.
All inputs are finite; a program needn't handle non-finite values.
Results may differ from the reference program's by a relative error of at most 0.017.
Values may be sent and summed in bfloat16 or wider, within the bound.
No kernel may reach another device: no remote copies, remote signals or barrier semaphores. Data moves between devices by JAX's collectives and lax.ppermute only.
A program may use at most 128 MiB of HBM per device.

```python
import math
import jax
import jax.numpy as jnp
from jax import lax

S = 2048
F = 16
REC_DEV = 48
BLOCK = 256
NOFF = 4
RECORDS = 384
NB = 8
N_TM = 8


def place_ends(drawn, own_key, smallest, largest):
    longest = drawn.shape.index(max(drawn.shape))
    spots = []
    for shift in (0, 1):
        where = [jax.random.randint(jax.random.fold_in(own_key, axis), (), 0, length) for axis, length in enumerate(drawn.shape)]
        where[longest] = (where[longest] + shift) % drawn.shape[longest]
        spots.append(tuple(where))
    return drawn.at[spots[0]].set(smallest).at[spots[1]].set(largest)


def block_levels(stream_key, shape, split, smallest, largest):
    factor_of = 1.0
    for dim, blocks in split:
        steps = jax.random.uniform(jax.random.fold_in(jax.random.fold_in(stream_key, 6), dim), (blocks,), jnp.float32, smallest / len(split), largest / len(split))
        factor_of = factor_of * jnp.repeat(jnp.exp(steps), shape[dim] // blocks).reshape((-1,) + (1,) * (len(shape) - 1 - dim))
    return factor_of


def noise(rng, shape, width, limit, pieces=(), kind=jnp.bfloat16):
    factor_of = block_levels(rng, shape, pieces, -0.22, 0.18) if pieces else 1.0
    values = jax.random.normal(rng, shape, jnp.float32) * width * factor_of
    return jnp.minimum(jnp.maximum(values, -limit), limit).astype(kind)


def setup_inputs(seed: int = 0) -> dict:
    keys = jax.random.split(jax.random.key(seed), 3)
    records = noise(keys[0], (RECORDS, 2, F, S), 1.0, 6.0, ((0, 8), (3, 32)))
    offsets = place_ends(jax.random.randint(keys[1], (NB, NB), 0, NOFF), jax.random.fold_in(keys[1], 1), 0, NOFF - 1).astype(jnp.int32)
    return dict(records=records, offsets=offsets)


def lag_kernels(bins, count):
    freq = jnp.arange(bins, dtype=jnp.int32)
    lag = jnp.minimum(freq, bins - freq)
    starts = jnp.arange(count, dtype=jnp.int32)[:, None] + 2
    inside = (lag[None, :] >= starts) & (lag[None, :] < starts + 3)
    weights = jnp.where(inside, jnp.float32(1.0), jnp.float32(0.1))
    phase = (freq[:, None, None] - freq[None, :, None]) * freq[None, None, :] % bins
    cosines = jnp.cos(phase.astype(jnp.float32) * jnp.float32(2.0 * math.pi / bins))
    return jnp.einsum('ot,fgt->ofg', weights, cosines, precision=lax.Precision.HIGHEST) / jnp.float32(bins)

def gram_bin(xbin):
    grouped = xbin.reshape(N_TM, REC_DEV, 2, S)
    total = jnp.zeros((2, S, S), jnp.float32)
    for group in range(N_TM):
        piece = grouped[group]
        left = jnp.concatenate([piece[:, 0], piece[:, 1]], axis=0)
        right_imag = jnp.concatenate([piece[:, 1], -piece[:, 0]], axis=0)
        real_part = jnp.dot(left.T, left, preferred_element_type=jnp.float32)
        imag_part = jnp.dot(left.T, right_imag, preferred_element_type=jnp.float32)
        term = jnp.stack([real_part, imag_part]) / jnp.float32(math.sqrt(RECORDS))
        rounded = lax.optimization_barrier(term.astype(jnp.bfloat16))
        total = total + rounded.astype(jnp.float32)
    return total

def reference(records, offsets):
    gram = lax.map(gram_bin, jnp.moveaxis(records, 2, 0))
    gram = jnp.moveaxis(gram, 0, 1)
    lagged = lag_kernels(F, NOFF)
    symmetric = (offsets + offsets.T) % NOFF
    blocks = jnp.moveaxis(gram.reshape(2, F, NB, BLOCK, S), 2, 0)

    def window_block(args):
        block, block_index = args
        shift_cols = jnp.repeat(symmetric[block_index], BLOCK)
        result = jnp.zeros_like(block)
        for offset in range(NOFF):
            term = jnp.einsum('fg,cgab->cfab', lagged[offset], block, precision=lax.Precision.HIGHEST)
            result = result + jnp.where(shift_cols[None, None, None, :] == offset, term, jnp.float32(0.0))
        return result.astype(jnp.bfloat16)
    windowed = lax.map(window_block, (blocks, jnp.arange(NB, dtype=jnp.int32)))
    windowed = jnp.moveaxis(windowed, 0, 2).reshape(2, F, S, S)

    def square_bin(matrix):
        left = jnp.concatenate([matrix[0], matrix[1]], axis=1)
        right_real = jnp.concatenate([matrix[0], -matrix[1]], axis=0)
        right_imag = jnp.concatenate([matrix[1], matrix[0]], axis=0)
        real_part = jnp.dot(left, right_real, preferred_element_type=jnp.float32)
        imag_part = jnp.dot(left, right_imag, preferred_element_type=jnp.float32)
        return (jnp.stack([real_part, imag_part]) / jnp.float32(math.sqrt(S))).astype(jnp.bfloat16)
    cthree = lax.map(square_bin, jnp.moveaxis(windowed, 1, 0))
    return jnp.moveaxis(cthree, 0, 1)
```

```python
import math

import jax
import jax.numpy as jnp
import numpy as np
from jax import lax
from jax.experimental import pallas as pl
from jax.experimental.pallas import tpu as pltpu
from jax.sharding import Mesh, PartitionSpec as P

S = 2048
F = 16
RECORDS = 384
BLOCK = 256
HALF = 128
NOFF = 4
NB = 8
REC_DEV = 48
GROUP = 4
NK = GROUP * REC_DEV
KK = 2 * NK
Z = ("zh", "zl")
VMEM_LIMIT = 48 * 1024 * 1024


def lag_profile():
    lag = np.minimum(np.arange(F), F - np.arange(F))
    rows = []
    for offset in range(NOFF):
        inside = (lag >= offset + 2) & (lag < offset + 5)
        weights = np.where(inside, 1.0, 0.1)
        step = np.arange(F // 2 + 1)
        angles = 2.0 * np.pi * (step[:, None] * np.arange(F)[None, :] % F) / F
        rows.append(np.cos(angles) @ weights / F)
    return [[float(value) for value in row] for row in rows]


LAG_PROFILE = lag_profile()


def home_shift(diff):
    return jnp.where(diff <= 4, -(diff // 2), (9 - diff) // 2)


HOME = [0, 0, -1, -1, -2, 2, 1, 1]


def pack_kernel(y_ref, out_ref):
    for part in range(GROUP):
        rows = jnp.concatenate([y_ref[x * GROUP + part] for x in range(GROUP)], axis=0)
        turned = rows.astype(jnp.float32).T.astype(jnp.bfloat16)
        both = jnp.concatenate([turned[:64], turned[64:]], axis=1)
        out_ref[part * 64 : (part + 1) * 64, :] = both


def gram_kernel(*refs):
    own = refs[0:5]
    other = refs[5:10]
    out_ref = refs[10]
    core = lax.axis_index("core")
    rows = pl.ds(pl.multiple_of(core * HALF, HALF), HALF)
    lane = lax.broadcasted_iota(jnp.int32, (HALF, KK), 1)
    sign = jnp.where(lane < NK, -1.0, 1.0).astype(jnp.float32)

    def quarter(value):
        turned = pltpu.roll(value.astype(jnp.float32), NK, 1) * sign
        return turned.astype(jnp.bfloat16)

    lefts = {}
    for index in range(5):
        first = own[index][rows, :]
        second = other[index][rows, :]
        top = jnp.concatenate([first, second], axis=1)
        bottom = jnp.concatenate([quarter(first), quarter(second)], axis=1)
        lefts[index] = jnp.concatenate([top, bottom], axis=0)
    place = {0: 0, -1: 1, 1: 2, -2: 3, 2: 4}
    scale = jnp.float32(1.0 / math.sqrt(RECORDS))
    for diff in range(NB):
        a = HOME[diff]
        b = (a + diff + 3) % NB - 3
        right_own = own[place[b]][...]
        right_other = other[place[b]][...]
        right = jnp.concatenate([right_own, right_other], axis=1)
        both = lax.dot_general(
            lefts[place[a]], right, (((1,), (1,)), ((), ())), preferred_element_type=jnp.float32
        )
        tile = ((both[:HALF] + both[HALF:]) * scale).astype(jnp.bfloat16)
        out_ref[2 * diff] = tile[:, :HALF]
        out_ref[2 * diff + 1] = tile[:, HALF:]


def window_kernel(offsets_ref, in_ref, out_ref):
    piece = lax.axis_index("x") * GROUP + lax.axis_index("y")
    plane = lax.axis_index("zh") * 2 + lax.axis_index("zl")
    diff = piece // 2
    a = (plane + home_shift(diff) + NB) % NB
    b = (a + diff) % NB
    shift = (offsets_ref[a, b] + offsets_ref[b, a]) % NOFF
    coefs = []
    for step in range(F // 2 + 1):
        value = jnp.float32(LAG_PROFILE[0][step])
        for offset in range(1, NOFF):
            value = jnp.where(shift == offset, jnp.float32(LAG_PROFILE[offset][step]), value)
        coefs.append(value)

    def chunk(index, carry):
        rows = pl.ds(pl.multiple_of(index * 16, 16), 16)
        data = [in_ref[g, rows, :].astype(jnp.float32) for g in range(F)]
        for f in range(F):
            total = coefs[0] * data[f] + coefs[F // 2] * data[(f + F // 2) % F]
            for step in range(1, F // 2):
                total = total + coefs[step] * (data[(f + step) % F] + data[(f - step) % F])
            out_ref[f, rows, :] = total.astype(jnp.bfloat16)
        return carry

    lax.fori_loop(0, HALF // 16, chunk, 0)


def square_kernel(g_ref, out_ref, left_ref):
    core = lax.axis_index("core")
    zh = lax.axis_index("zh")
    zl = lax.axis_index("zl")
    y = lax.axis_index("y")
    i = 2 * zh + core

    def block(a, diff):
        plane = (a - home_shift(diff) + NB) % NB
        halves = [
            jnp.concatenate([g_ref[h, plane, 2 * diff], g_ref[h, plane, 2 * diff + 1]], axis=1)
            for h in range(2)
        ]
        return jnp.concatenate(halves, axis=0)

    for step in range(NB):
        columns = pl.ds(step * BLOCK, BLOCK)
        left_ref[:BLOCK, columns] = block(i, jnp.int32(step))
        k = (i + step) % NB
        across = block(k, jnp.int32((NB - step) % NB))
        left_ref[BLOCK:, columns] = across.astype(jnp.float32).T.astype(jnp.bfloat16)

    scale = jnp.float32(0.5 / math.sqrt(S))
    aside = jnp.where(core == y // 2, 0, 2)

    def panel(m, carry):
        j = 4 * zl + (y + m + aside) % GROUP
        downs = []
        acrosses = []
        for step in range(NB):
            k = (i + step) % NB
            downs.append(block(k, (j - k + NB) % NB))
            acrosses.append(block(j, (k - j + NB) % NB))
        down = jnp.concatenate(downs, axis=0)
        across = jnp.concatenate(acrosses, axis=1)
        first = jnp.dot(left_ref[...], down, preferred_element_type=jnp.float32)
        second = lax.dot_general(
            left_ref[...], across, (((1,), (1,)), ((), ())), preferred_element_type=jnp.float32
        )
        out_ref[m, 0] = ((second[:BLOCK] + first[BLOCK:]) * scale).astype(jnp.bfloat16)
        out_ref[m, 1] = ((first[:BLOCK] - second[BLOCK:]) * scale).astype(jnp.bfloat16)
        return carry

    lax.fori_loop(0, GROUP, panel, 0)


def join_kernel(r0, r1, r2, r3, out_ref):
    core = lax.axis_index("core")
    y = lax.axis_index("y")
    for m, ref in enumerate((r0, r1, r2, r3)):
        source = (y - m + GROUP) % GROUP
        half = jnp.where(source // 2 == core, core, 1 - core)
        rows = pl.ds(pl.multiple_of(half * BLOCK, BLOCK), BLOCK)
        for part in range(2):
            out_ref[part, source % 2, rows, :] = ref[part]


def call(kernel, out_shape, *args, scratch=(), smem_first=False):
    specs = [pl.BlockSpec(memory_space=pltpu.VMEM)] * len(args)
    if smem_first:
        specs[0] = pl.BlockSpec(memory_space=pltpu.SMEM)
    return pl.pallas_call(
        kernel,
        out_shape=jax.ShapeDtypeStruct(out_shape, jnp.bfloat16),
        in_specs=specs,
        out_specs=pl.BlockSpec(memory_space=pltpu.VMEM),
        scratch_shapes=list(scratch),
        compiler_params=pltpu.CompilerParams(vmem_limit_bytes=VMEM_LIMIT),
    )(*args)


def along_z(value, step):
    return lax.ppermute(value, Z, [(z, (z + step) % NB) for z in range(NB)])


def other_core(value):
    return lax.ppermute(value, "core", [(0, 1), (1, 0)])


def panel_moves(m):
    moves = []
    for core in range(2):
        for y in range(GROUP):
            if core == y // 2:
                target = (core, (y + m) % GROUP)
            else:
                target = (1 - core, (y + m + 2) % GROUP)
            moves.append((core * GROUP + y, target[0] * GROUP + target[1]))
    return moves


def on_device(records, offsets):
    outgoing = records.transpose(2, 0, 1, 3).reshape(F, REC_DEV, 2 * 64)
    arrived = lax.all_to_all(outgoing, ("x", "y"), 0, 0, tiled=True)
    here = call(pack_kernel, (BLOCK, KK), arrived)
    below = along_z(here, 1)
    above = along_z(here, -1)
    below2 = along_z(below, 1)
    above2 = along_z(above, -1)
    own = [here, below, above, below2, above2]
    other = [other_core(value) for value in own]
    strip = call(gram_kernel, (F, HALF, HALF), *own, *other)
    bins = lax.all_to_all(strip, ("x", "y"), 0, 0, tiled=True)
    windowed = call(window_kernel, (F, HALF, HALF), offsets, bins, smem_first=True)
    pieces = lax.all_to_all(windowed, ("x", "y"), 0, 0, tiled=True)
    whole = lax.all_gather(pieces, ("core",) + Z, axis=0, tiled=False)
    whole = whole.reshape(2, NB, F, HALF, HALF)
    panels = call(
        square_kernel,
        (GROUP, 2, BLOCK, BLOCK),
        whole,
        scratch=[pltpu.VMEM((2 * BLOCK, S), jnp.bfloat16)],
    )
    arrived = [lax.ppermute(panels[m], ("core", "y"), panel_moves(m)) for m in range(GROUP)]
    return call(join_kernel, (2, 2, 2 * BLOCK, BLOCK), *arrived)


def solution(mesh):
    fine = Mesh(mesh.devices.reshape(4, 2, 4, 2, 4), ("x", "core", "zh", "zl", "y"))
    return jax.shard_map(
        on_device,
        mesh=fine,
        in_specs=(P(("x", "core"), None, None, ("zh", "zl", "y")), P()),
        out_specs=P(None, ("x", "core"), "zh", ("zl", "y")),
        check_vma=False,
    )
```

```python
import math

import jax
import jax.numpy as jnp
import numpy as np
from jax import lax
from jax.experimental import pallas as pl
from jax.experimental.pallas import tpu as pltpu
from jax.sharding import Mesh, PartitionSpec as P

S = 2048
F = 16
RECORDS = 384
BLOCK = 256
HALF = 128
NOFF = 4
NB = 8
REC_DEV = 48
GROUP = 4
Z = ("zh", "zl")
VMEM_LIMIT = 24 * 1024 * 1024


def lag_profile():
    lag = np.minimum(np.arange(F), F - np.arange(F))
    rows = []
    for offset in range(NOFF):
        inside = (lag >= offset + 2) & (lag < offset + 5)
        weights = np.where(inside, 1.0, 0.1)
        step = np.arange(F // 2 + 1)
        angles = 2.0 * np.pi * (step[:, None] * np.arange(F)[None, :] % F) / F
        rows.append(np.cos(angles) @ weights / F)
    return [[float(value) for value in row] for row in rows]


LAG_PROFILE = lag_profile()


def home_shift(diff):
    return jnp.where(diff <= 4, -(diff // 2), (9 - diff) // 2)


HOME = [0, 0, -1, -1, -2, 2, 1, 1]

PIECES = [(0, True, True), (0, True, False)]
for _step in range(1, NB // 2):
    PIECES += [
        (_step, True, True),
        (_step, True, False),
        (_step, False, False),
        (_step, False, True),
    ]
PIECES += [(NB // 2, True, True), (NB // 2, False, False)]
NPIECES = len(PIECES)


def pack_kernel(y_ref, out_ref):
    for part in range(GROUP):
        rows = jnp.concatenate([y_ref[line * GROUP + part] for line in range(2 * GROUP)], axis=0)
        turned = rows.astype(jnp.float32).T.astype(jnp.bfloat16)
        stations = slice(part * 64, (part + 1) * 64)
        out_ref[stations, :RECORDS] = turned[:64]
        out_ref[stations, RECORDS:] = turned[64:]


def gram_kernel(here_ref, near_ref, near_swap_ref, far_ref, far_swap_ref, out_ref):
    core = lax.axis_index("core")
    rows = pl.ds(pl.multiple_of(core * HALF, HALF), HALF)
    planes = {
        0: (here_ref, here_ref),
        -1: (near_ref, near_swap_ref),
        1: (near_swap_ref, near_ref),
        -2: (far_ref, far_swap_ref),
        2: (far_swap_ref, far_ref),
    }
    lefts = {}
    rights = {}
    for plane, (first, second) in planes.items():
        if first is second:
            rights[plane] = first[...]
            top = first[rows, :]
        else:
            rights[plane] = jnp.where(core == 0, first[...], second[...])
            top = jnp.where(core == 0, first[rows, :], second[rows, :])
        bottom = jnp.concatenate([-top[:, RECORDS:], top[:, :RECORDS]], axis=1)
        lefts[plane] = jnp.concatenate([top, bottom], axis=0)
    scale = jnp.float32(1.0 / math.sqrt(RECORDS))
    for diff in range(NB):
        a = HOME[diff]
        b = (a + diff + 3) % NB - 3
        both = lax.dot_general(
            lefts[a], rights[b], (((1,), (1,)), ((), ())), preferred_element_type=jnp.float32
        )
        tile = ((both[:HALF] + both[HALF:]) * scale).astype(jnp.bfloat16)
        out_ref[2 * diff] = tile[:, :HALF]
        out_ref[2 * diff + 1] = tile[:, HALF:]


def window_kernel(offsets_ref, in_ref, out_ref):
    piece = lax.axis_index("x") * GROUP + lax.axis_index("y")
    plane = lax.axis_index("zh") * 2 + lax.axis_index("zl")
    diff = piece // 2
    a = (plane + home_shift(diff) + NB) % NB
    b = (a + diff) % NB
    shift = (offsets_ref[a, b] + offsets_ref[b, a]) % NOFF
    coefs = []
    for step in range(F // 2 + 1):
        value = jnp.float32(LAG_PROFILE[0][step])
        for offset in range(1, NOFF):
            value = jnp.where(shift == offset, jnp.float32(LAG_PROFILE[offset][step]), value)
        coefs.append(value)

    def chunk(index, carry):
        rows = pl.ds(pl.multiple_of(index * 16, 16), 16)
        data = [in_ref[g, rows, :].astype(jnp.float32) for g in range(F)]
        for f in range(F):
            total = coefs[0] * data[f] + coefs[F // 2] * data[(f + F // 2) % F]
            for step in range(1, F // 2):
                total = total + coefs[step] * (data[(f + step) % F] + data[(f - step) % F])
            out_ref[f, rows, :] = total.astype(jnp.bfloat16)
        return carry

    lax.fori_loop(0, HALF // 16, chunk, 0)


def square_kernel(*refs):
    pieces = refs[:NPIECES]
    out_ref, g_ref, left_ref, sems = refs[NPIECES:]
    core = lax.axis_index("core")
    zh = lax.axis_index("zh")
    zl = lax.axis_index("zl")
    y = lax.axis_index("y")
    here = 2 * zh + zl
    i = 2 * zh + core
    away = jnp.where(core == 0, -1, 1)
    copies = []
    for index, (step, carried, own) in enumerate(PIECES):
        plane = (here + (away if carried else -away) * step + NB) % NB
        half = core if own else 1 - core
        copy = pltpu.make_async_copy(pieces[index], g_ref.at[half, plane], sems.at[index])
        copy.start()
        copies.append(copy)
    for (step, _, _), copy in zip(PIECES, copies):
        if step < NB // 2:
            copy.wait()

    def block(a, diff):
        plane = (a - home_shift(diff) + NB) % NB
        halves = [
            jnp.concatenate([g_ref[h, plane, 2 * diff], g_ref[h, plane, 2 * diff + 1]], axis=1)
            for h in range(2)
        ]
        return jnp.concatenate(halves, axis=0)

    for step in range(NB):
        columns = pl.ds(step * BLOCK, BLOCK)
        left_ref[:BLOCK, columns] = block(i, jnp.int32(step))
        k = (i + step) % NB
        across = block(k, jnp.int32((NB - step) % NB))
        left_ref[BLOCK:, columns] = across.astype(jnp.float32).T.astype(jnp.bfloat16)

    for (step, _, _), copy in zip(PIECES, copies):
        if step == NB // 2:
            copy.wait()
    scale = jnp.float32(0.5 / math.sqrt(S))
    aside = jnp.where(core == y // 2, 0, 2)

    def panel(m, carry):
        j = 4 * zl + (y + m + aside) % GROUP
        downs = []
        acrosses = []
        for step in range(NB):
            k = (i + step) % NB
            downs.append(block(k, (j - k + NB) % NB))
            acrosses.append(block(j, (k - j + NB) % NB))
        down = jnp.concatenate(downs, axis=0)
        across = jnp.concatenate(acrosses, axis=1)
        first = jnp.dot(left_ref[...], down, preferred_element_type=jnp.float32)
        second = lax.dot_general(
            left_ref[...], across, (((1,), (1,)), ((), ())), preferred_element_type=jnp.float32
        )
        out_ref[m, 0] = ((second[:BLOCK] + first[BLOCK:]) * scale).astype(jnp.bfloat16)
        out_ref[m, 1] = ((first[:BLOCK] - second[BLOCK:]) * scale).astype(jnp.bfloat16)
        return carry

    lax.fori_loop(0, GROUP, panel, 0)


def join_kernel(r0, r1, r2, r3, out_ref):
    core = lax.axis_index("core")
    y = lax.axis_index("y")
    for m, ref in enumerate((r0, r1, r2, r3)):
        source = (y - m + GROUP) % GROUP
        half = jnp.where(source // 2 == core, core, 1 - core)
        rows = pl.ds(pl.multiple_of(half * BLOCK, BLOCK), BLOCK)
        for part in range(2):
            out_ref[part, source % 2, rows, :] = ref[part]


def call(kernel, out_shape, *args, scratch=(), smem_first=False, space=pltpu.VMEM):
    specs = [pl.BlockSpec(memory_space=space)] * len(args)
    if smem_first:
        specs[0] = pl.BlockSpec(memory_space=pltpu.SMEM)
    return pl.pallas_call(
        kernel,
        out_shape=jax.ShapeDtypeStruct(out_shape, jnp.bfloat16),
        in_specs=specs,
        out_specs=pl.BlockSpec(memory_space=pltpu.VMEM),
        scratch_shapes=list(scratch),
        compiler_params=pltpu.CompilerParams(vmem_limit_bytes=VMEM_LIMIT),
    )(*args)


def carry(value):
    moves = [(z, (z + 1) % NB) for z in range(NB)]
    moves += [(NB + z, NB + (z - 1) % NB) for z in range(NB)]
    return lax.ppermute(value, ("core",) + Z, moves)


def other_core(value):
    return lax.ppermute(value, "core", [(0, 1), (1, 0)])


def panel_moves(m):
    moves = []
    for core in range(2):
        for y in range(GROUP):
            if core == y // 2:
                target = (core, (y + m) % GROUP)
            else:
                target = (1 - core, (y + m + 2) % GROUP)
            moves.append((core * GROUP + y, target[0] * GROUP + target[1]))
    return moves


def on_device(records, offsets):
    outgoing = records.transpose(2, 0, 1, 3).reshape(GROUP, 1, GROUP, REC_DEV, 2 * 64)
    outgoing = jnp.broadcast_to(outgoing, (GROUP, 2, GROUP, REC_DEV, 2 * 64))
    outgoing = outgoing.reshape(2 * F, REC_DEV, 2 * 64)
    arrived = lax.all_to_all(outgoing, ("x", "core", "y"), 0, 0, tiled=True)
    here = call(pack_kernel, (BLOCK, 2 * RECORDS), arrived)
    near = carry(here)
    far = carry(near)
    near_swap = other_core(near)
    far_swap = other_core(far)
    strip = call(gram_kernel, (F, HALF, HALF), here, near, near_swap, far, far_swap)
    bins = lax.all_to_all(strip, ("x", "y"), 0, 0, tiled=True)
    windowed = call(window_kernel, (F, HALF, HALF), offsets, bins, smem_first=True)
    own = {0: lax.all_to_all(windowed, ("x", "y"), 0, 0, tiled=True)}
    other = {0: other_core(own[0])}
    pieces = {(0, True, True): own[0], (0, True, False): other[0]}
    for step in range(1, NB // 2 + 1):
        own[step] = carry(own[step - 1])
        pieces[(step, True, True)] = own[step]
        if step < NB // 2:
            other[step] = carry(other[step - 1])
            pieces[(step, True, False)] = other[step]
        pieces[(step, False, False)] = other_core(own[step])
        if step < NB // 2:
            pieces[(step, False, True)] = other_core(other[step])
    panels = call(
        square_kernel,
        (GROUP, 2, BLOCK, BLOCK),
        *[pieces[key] for key in PIECES],
        scratch=[
            pltpu.VMEM((2, NB, F, HALF, HALF), jnp.bfloat16),
            pltpu.VMEM((2 * BLOCK, S), jnp.bfloat16),
            pltpu.SemaphoreType.DMA((NPIECES,)),
        ],
        space=pl.ANY,
    )
    arrived = [lax.ppermute(panels[m], ("core", "y"), panel_moves(m)) for m in range(GROUP)]
    return call(join_kernel, (2, 2, 2 * BLOCK, BLOCK), *arrived)


def solution(mesh):
    fine = Mesh(mesh.devices.reshape(4, 2, 4, 2, 4), ("x", "core", "zh", "zl", "y"))
    return jax.shard_map(
        on_device,
        mesh=fine,
        in_specs=(P(("x", "core"), None, None, ("zh", "zl", "y")), P()),
        out_specs=P(None, ("x", "core"), "zh", ("zl", "y")),
        check_vma=False,
    )
```

```python
import functools
import math

import jax
import jax.numpy as jnp
import numpy as np
from jax import lax
from jax.experimental import pallas as pl
from jax.experimental.pallas import tpu as pltpu
from jax.sharding import Mesh, PartitionSpec as P

S = 2048
F = 16
RECORDS = 384
BLOCK = 256
HALF = 128
NOFF = 4
NB = 8
REC_DEV = 48
GROUP = 4
NK = GROUP * REC_DEV
KK = 2 * NK
NEAR_DIFFS = (0, 1, 7, 2, 6)
FAR_DIFFS = (3, 5, 4)
Z = ("zh", "zl")


def lag_profile():
    lag = np.minimum(np.arange(F), F - np.arange(F))
    rows = []
    for offset in range(NOFF):
        inside = (lag >= offset + 2) & (lag < offset + 5)
        weights = np.where(inside, 1.0, 0.1)
        step = np.arange(F // 2 + 1)
        angles = 2.0 * np.pi * (step[:, None] * np.arange(F)[None, :] % F) / F
        rows.append(np.cos(angles) @ weights / F)
    return [[float(value) for value in row] for row in rows]


LAG_PROFILE = lag_profile()


def home_shift(diff):
    return jnp.where(diff <= 4, -(diff // 2), (9 - diff) // 2)


HOME = [0, 0, -1, -1, -2, 2, 1, 1]

PIECES = [(0, True, True), (0, True, False)]
for _step in range(1, NB // 2):
    PIECES += [
        (_step, True, True),
        (_step, True, False),
        (_step, False, False),
        (_step, False, True),
    ]
PIECES += [(NB // 2, True, True), (NB // 2, False, False)]
NPIECES = len(PIECES)


def pack_kernel(y_ref, out_ref):
    for part in range(GROUP):
        rows = jnp.concatenate([y_ref[line * GROUP + part] for line in range(GROUP)], axis=0)
        turned = rows.astype(jnp.float32).T.astype(jnp.bfloat16)
        both = jnp.concatenate([turned[:64], turned[64:]], axis=1)
        out_ref[part * 64 : (part + 1) * 64, :] = both


def gram_kernel(diffs, planes, *refs):
    rights = {plane: ref[...] for plane, ref in zip(planes, refs)}
    mine_ref, theirs_ref = refs[len(planes) :]
    first_core = lax.axis_index("core") == 0
    lane = lax.broadcasted_iota(jnp.int32, (BLOCK, KK), 1)
    sign = jnp.where(lane < NK, -1.0, 1.0).astype(jnp.float32)
    scale = jnp.float32(1.0 / math.sqrt(RECORDS))
    lefts = {}
    for plane in sorted({HOME[diff] for diff in diffs}):
        top = rights[plane]
        bottom = (pltpu.roll(top.astype(jnp.float32), NK, 1) * sign).astype(jnp.bfloat16)
        lefts[plane] = jnp.concatenate([top, bottom], axis=0)
    for index, diff in enumerate(diffs):
        a = HOME[diff]
        b = (a + diff + 3) % NB - 3
        both = lax.dot_general(
            lefts[a], rights[b], (((1,), (1,)), ((), ())), preferred_element_type=jnp.float32
        )
        tile = (both[:BLOCK] + both[BLOCK:]) * scale
        mine = jnp.where(first_core, tile[:HALF], tile[HALF:])
        theirs = jnp.where(first_core, tile[HALF:], tile[:HALF]).astype(jnp.bfloat16)
        for side in range(2):
            columns = slice(side * HALF, (side + 1) * HALF)
            mine_ref[2 * index + side] = mine[:, columns]
            theirs_ref[2 * index + side] = theirs[:, columns]


def add_kernel(near_ref, near_other_ref, far_ref, far_other_ref, out_ref):
    for diffs, mine_ref, other_ref in (
        (NEAR_DIFFS, near_ref, near_other_ref),
        (FAR_DIFFS, far_ref, far_other_ref),
    ):
        for index, diff in enumerate(diffs):
            for side in range(2):
                total = mine_ref[2 * index + side] + other_ref[2 * index + side].astype(jnp.float32)
                out_ref[2 * diff + side] = total.astype(jnp.bfloat16)


def window_kernel(offsets_ref, in_ref, out_ref):
    piece = lax.axis_index("x") * GROUP + lax.axis_index("y")
    plane = lax.axis_index("zh") * 2 + lax.axis_index("zl")
    diff = piece // 2
    a = (plane + home_shift(diff) + NB) % NB
    b = (a + diff) % NB
    shift = (offsets_ref[a, b] + offsets_ref[b, a]) % NOFF
    coefs = []
    for step in range(F // 2 + 1):
        value = jnp.float32(LAG_PROFILE[0][step])
        for offset in range(1, NOFF):
            value = jnp.where(shift == offset, jnp.float32(LAG_PROFILE[offset][step]), value)
        coefs.append(value)

    def chunk(index, carry):
        rows = pl.ds(pl.multiple_of(index * 16, 16), 16)
        data = [in_ref[g, rows, :].astype(jnp.float32) for g in range(F)]
        for f in range(F):
            total = coefs[0] * data[f] + coefs[F // 2] * data[(f + F // 2) % F]
            for step in range(1, F // 2):
                total = total + coefs[step] * (data[(f + step) % F] + data[(f - step) % F])
            out_ref[f, rows, :] = total.astype(jnp.bfloat16)
        return carry

    lax.fori_loop(0, HALF // 16, chunk, 0)


def place():
    core = lax.axis_index("core")
    zh = lax.axis_index("zh")
    zl = lax.axis_index("zl")
    return core, 2 * zh + zl, 2 * zh + core, 4 * zl


def copy_in(entry, piece_ref, g_ref, sem):
    step, carried, own = entry
    core, here, _, _ = place()
    away = jnp.where(core == 0, -1, 1)
    plane = (here + (away if carried else -away) * step + NB) % NB
    half = core if own else 1 - core
    return pltpu.make_async_copy(piece_ref, g_ref.at[half, plane], sem)


def read_block(g_ref, a, diff):
    plane = (a - home_shift(diff) + NB) % NB
    halves = [
        jnp.concatenate([g_ref[h, plane, 2 * diff], g_ref[h, plane, 2 * diff + 1]], axis=1)
        for h in range(2)
    ]
    return jnp.concatenate(halves, axis=0)


def prepare_kernel(*refs):
    pieces = refs[: NPIECES - 2]
    g_ref, left_ref, sems = refs[NPIECES - 2 :]
    _, _, i, _ = place()
    copies = []
    for index, piece_ref in enumerate(pieces):
        copy = copy_in(PIECES[index], piece_ref, g_ref, sems.at[index])
        copy.start()
        copies.append(copy)
    for copy in copies:
        copy.wait()
    for step in range(NB):
        columns = pl.ds(step * BLOCK, BLOCK)
        left_ref[:BLOCK, columns] = read_block(g_ref, i, jnp.int32(step))
        k = (i + step) % NB
        across = read_block(g_ref, k, jnp.int32((NB - step) % NB))
        left_ref[BLOCK:, columns] = across.astype(jnp.float32).T.astype(jnp.bfloat16)


def panel(m, g_ref, left_ref, out_ref):
    core, _, i, first = place()
    y = lax.axis_index("y")
    aside = jnp.where(core == y // 2, 0, 2)
    j = first + (y + m + aside) % GROUP
    downs = []
    acrosses = []
    for step in range(NB):
        k = (i + step) % NB
        downs.append(read_block(g_ref, k, (j - k + NB) % NB))
        acrosses.append(read_block(g_ref, j, (k - j + NB) % NB))
    down = jnp.concatenate(downs, axis=0)
    across = jnp.concatenate(acrosses, axis=1)
    first = jnp.dot(left_ref[...], down, preferred_element_type=jnp.float32)
    second = lax.dot_general(
        left_ref[...], across, (((1,), (1,)), ((), ())), preferred_element_type=jnp.float32
    )
    scale = jnp.float32(0.5 / math.sqrt(S))
    out_ref[0] = ((second[:BLOCK] + first[BLOCK:]) * scale).astype(jnp.bfloat16)
    out_ref[1] = ((first[:BLOCK] - second[BLOCK:]) * scale).astype(jnp.bfloat16)


def first_panels_kernel(old_ref, left_ref, last_ref, last_swap_ref, g_ref, out1_ref, out3_ref, sems):
    del old_ref
    copies = [
        copy_in(PIECES[-2], last_ref, g_ref, sems.at[0]),
        copy_in(PIECES[-1], last_swap_ref, g_ref, sems.at[1]),
    ]
    for copy in copies:
        copy.start()
    for copy in copies:
        copy.wait()
    panel(1, g_ref, left_ref, out1_ref)
    panel(3, g_ref, left_ref, out3_ref)


def last_panels_kernel(g_ref, left_ref, out2_ref, out0_ref):
    panel(2, g_ref, left_ref, out2_ref)
    panel(0, g_ref, left_ref, out0_ref)


def join_kernel(moved, *refs):
    pieces = refs[: len(moved)]
    out_ref, sems = refs[-2:]
    core = lax.axis_index("core")
    y = lax.axis_index("y")
    copies = []
    for index, m in enumerate(moved):
        source = (y - m + GROUP) % GROUP
        half = jnp.where(source // 2 == core, core, 1 - core)
        rows = pl.ds(pl.multiple_of(half * BLOCK, BLOCK), BLOCK)
        copies.append(
            pltpu.make_async_copy(
                pieces[index], out_ref.at[:, source % 2, rows, :], sems.at[index]
            )
        )
    for copy in copies:
        copy.start()
    for copy in copies:
        copy.wait()


def call(kernel, shapes, *args, spaces=None, out_space=pltpu.VMEM, scratch=(), aliases=None, flops=0, mib=16):
    shapes = [shape if isinstance(shape, jax.ShapeDtypeStruct) else bf16(shape) for shape in shapes]
    spaces = spaces or [pltpu.VMEM] * len(args)
    moved = sum(arg.size * arg.dtype.itemsize for arg in args)
    moved += sum(math.prod(shape.shape) * shape.dtype.itemsize for shape in shapes)
    results = pl.pallas_call(
        kernel,
        out_shape=shapes,
        in_specs=[pl.BlockSpec(memory_space=space) for space in spaces],
        out_specs=[pl.BlockSpec(memory_space=out_space)] * len(shapes),
        scratch_shapes=list(scratch),
        input_output_aliases=aliases or {},
        cost_estimate=pl.CostEstimate(flops=flops, bytes_accessed=moved, transcendentals=0),
        compiler_params=pltpu.CompilerParams(vmem_limit_bytes=mib * 1024 * 1024),
    )(*args)
    return results[0] if len(shapes) == 1 else results


def bf16(shape):
    return jax.ShapeDtypeStruct(shape, jnp.bfloat16)


def along_z(value, step):
    return lax.ppermute(value, Z, [(z, (z + step) % NB) for z in range(NB)])


def carry(value):
    moves = [(z, (z + 1) % NB) for z in range(NB)]
    moves += [(NB + z, NB + (z - 1) % NB) for z in range(NB)]
    return lax.ppermute(value, ("core",) + Z, moves)


def other_core(value):
    return lax.ppermute(value, "core", [(0, 1), (1, 0)])


def panel_moves(m):
    moves = []
    for core in range(2):
        for y in range(GROUP):
            if core == y // 2:
                target = (core, (y + m) % GROUP)
            else:
                target = (1 - core, (y + m + 2) % GROUP)
            moves.append((core * GROUP + y, target[0] * GROUP + target[1]))
    return moves


def partial_gram(diffs, planes, values):
    count = 2 * len(diffs)
    shapes = [jax.ShapeDtypeStruct((count, HALF, HALF), jnp.float32), bf16((count, HALF, HALF))]
    return call(functools.partial(gram_kernel, diffs, planes), shapes, *values, flops=count * 2 * BLOCK * BLOCK * KK)


def on_device(records, offsets):
    outgoing = records.transpose(2, 0, 1, 3).reshape(F, REC_DEV, 2 * 64)
    arrived = lax.all_to_all(outgoing, ("x", "y"), 0, 0, tiled=True)
    here = call(pack_kernel, [(BLOCK, KK)], arrived)
    below = along_z(here, 1)
    above = along_z(here, -1)
    below2 = along_z(below, 1)
    above2 = along_z(above, -1)
    near, near_theirs = partial_gram(NEAR_DIFFS, (0, -1, 1), (here, below, above))
    near_other = other_core(near_theirs)
    far, far_theirs = partial_gram(FAR_DIFFS, (-1, 2, -2), (below, above2, below2))
    far_other = other_core(far_theirs)
    strip = call(add_kernel, [(F, HALF, HALF)], near, near_other, far, far_other)
    bins = lax.all_to_all(strip, ("x", "y"), 0, 0, tiled=True)
    windowed = call(window_kernel, [(F, HALF, HALF)], offsets, bins, spaces=[pltpu.SMEM, pltpu.VMEM])
    mine = lax.all_to_all(windowed, ("x", "y"), 0, 0, tiled=True)
    own = {}
    other = {}
    own[0], other[0] = lax.optimization_barrier((mine, other_core(mine)))
    pieces = {(0, True, True): own[0], (0, True, False): other[0]}
    for step in range(1, NB // 2 + 1):
        own[step] = carry(own[step - 1])
        pieces[(step, True, True)] = own[step]
        if step < NB // 2:
            other[step] = carry(other[step - 1])
            pieces[(step, True, False)] = other[step]
        pieces[(step, False, False)] = other_core(own[step])
        if step < NB // 2:
            pieces[(step, False, True)] = other_core(other[step])
    pieces = [pieces[key] for key in PIECES]
    whole_shape = (2, NB, F, HALF, HALF)
    whole, left = call(
        prepare_kernel,
        [whole_shape, (2 * BLOCK, S)],
        *pieces[:-2],
        spaces=[pl.ANY] * (NPIECES - 2),
        scratch=[pltpu.SemaphoreType.DMA((NPIECES - 2,))],
    )
    tile = (2, BLOCK, BLOCK)
    panel_flops = 2 * 2 * 2 * (2 * BLOCK) * BLOCK * S
    whole, panel1, panel3 = call(
        first_panels_kernel,
        [whole_shape, tile, tile],
        whole,
        left,
        *pieces[-2:],
        spaces=[pltpu.VMEM, pltpu.VMEM, pl.ANY, pl.ANY],
        scratch=[pltpu.SemaphoreType.DMA((2,))],
        aliases={0: 0},
        flops=panel_flops,
    )
    panel2, panel0 = call(last_panels_kernel, [tile, tile], whole, left, flops=panel_flops)
    panels = [panel0, panel1, panel2, panel3]
    arrived = [lax.ppermute(panels[m], ("core", "y"), panel_moves(m)) for m in range(GROUP)]
    out_shape = (2, 2, 2 * BLOCK, BLOCK)
    joined = call(
        functools.partial(join_kernel, (1, 3)),
        [out_shape],
        arrived[1],
        arrived[3],
        spaces=[pl.ANY] * 2,
        out_space=pl.ANY,
        scratch=[pltpu.SemaphoreType.DMA((2,))],
    )
    return call(
        functools.partial(join_kernel, (2, 0)),
        [out_shape],
        arrived[2],
        arrived[0],
        joined,
        spaces=[pl.ANY] * 3,
        out_space=pl.ANY,
        scratch=[pltpu.SemaphoreType.DMA((2,))],
        aliases={2: 0},
    )


def solution(mesh):
    fine = Mesh(mesh.devices.reshape(4, 2, 4, 2, 4), ("x", "core", "zh", "zl", "y"))
    return jax.shard_map(
        on_device,
        mesh=fine,
        in_specs=(P(("x", "core"), None, None, ("zh", "zl", "y")), P()),
        out_specs=P(None, ("x", "core"), "zh", ("zl", "y")),
        check_vma=False,
    )
```

```python
import functools
import math

import jax
import jax.numpy as jnp
import numpy as np
from jax import lax
from jax.experimental import pallas as pl
from jax.experimental.pallas import tpu as pltpu
from jax.sharding import Mesh, PartitionSpec as P

S = 2048
F = 16
RECORDS = 384
BLOCK = 256
HALF = 128
NOFF = 4
NB = 8
REC_DEV = 48
GROUP = 4
NK = GROUP * REC_DEV
KK = 2 * NK
NEAR_DIFFS = (0, 1, 7, 2, 6)
FAR_DIFFS = (3, 5, 4)
PANELS = ((2, 0, 1), (3,),)
Z = ("zh", "zl")


def lag_profile():
    lag = np.minimum(np.arange(F), F - np.arange(F))
    rows = []
    for offset in range(NOFF):
        inside = (lag >= offset + 2) & (lag < offset + 5)
        weights = np.where(inside, 1.0, 0.1)
        step = np.arange(F // 2 + 1)
        angles = 2.0 * np.pi * (step[:, None] * np.arange(F)[None, :] % F) / F
        rows.append(np.cos(angles) @ weights / F)
    return [[float(value) for value in row] for row in rows]


LAG_PROFILE = lag_profile()


def home_shift(diff):
    return jnp.where(diff <= 4, -(diff // 2), (9 - diff) // 2)


HOME = [0, 0, -1, -1, -2, 2, 1, 1]

PIECES = [(0, True, True), (0, True, False)]
for _step in range(1, NB // 2):
    PIECES += [
        (_step, True, True),
        (_step, True, False),
        (_step, False, False),
        (_step, False, True),
    ]
PIECES += [(NB // 2, True, True), (NB // 2, False, False)]
NPIECES = len(PIECES)


def pack_kernel(y_ref, out_ref):
    for part in range(GROUP):
        rows = jnp.concatenate([y_ref[line * GROUP + part] for line in range(GROUP)], axis=0)
        turned = rows.astype(jnp.float32).T.astype(jnp.bfloat16)
        both = jnp.concatenate([turned[:64], turned[64:]], axis=1)
        out_ref[part * 64 : (part + 1) * 64, :] = both


def write_coefs(offsets_ref, coefs_ref):
    piece = lax.axis_index("x") * GROUP + lax.axis_index("y")
    plane = lax.axis_index("zh") * 2 + lax.axis_index("zl")
    diff = piece // 2
    a = (plane + home_shift(diff) + NB) % NB
    b = (a + diff) % NB
    shift = (offsets_ref[a, b] + offsets_ref[b, a]) % NOFF
    for step in range(F // 2 + 1):
        value = jnp.float32(LAG_PROFILE[0][step])
        for offset in range(1, NOFF):
            value = jnp.where(shift == offset, jnp.float32(LAG_PROFILE[offset][step]), value)
        coefs_ref[step : step + 1, :] = jnp.full((1, HALF), value, jnp.float32)


def gram_kernel(diffs, planes, *refs):
    if len(refs) > len(planes) + 2:
        write_coefs(refs[len(planes)], refs[-1])
        refs = refs[: len(planes)] + refs[len(planes) + 1 : -1]
    rights = {plane: ref[...] for plane, ref in zip(planes, refs)}
    mine_ref, theirs_ref = refs[len(planes) :]
    first_core = lax.axis_index("core") == 0
    lane = lax.broadcasted_iota(jnp.int32, (BLOCK, KK), 1)
    sign = jnp.where(lane < NK, -1.0, 1.0).astype(jnp.float32)
    scale = jnp.float32(1.0 / math.sqrt(RECORDS))
    lefts = {}
    for plane in sorted({HOME[diff] for diff in diffs}):
        top = rights[plane]
        bottom = (pltpu.roll(top.astype(jnp.float32), NK, 1) * sign).astype(jnp.bfloat16)
        lefts[plane] = jnp.concatenate([top, bottom], axis=0)
    for index, diff in enumerate(diffs):
        a = HOME[diff]
        b = (a + diff + 3) % NB - 3
        both = lax.dot_general(
            lefts[a], rights[b], (((1,), (1,)), ((), ())), preferred_element_type=jnp.float32
        )
        tile = (both[:BLOCK] + both[BLOCK:]) * scale
        mine = jnp.where(first_core, tile[:HALF], tile[HALF:])
        theirs = jnp.where(first_core, tile[HALF:], tile[:HALF]).astype(jnp.bfloat16)
        for side in range(2):
            columns = slice(side * HALF, (side + 1) * HALF)
            mine_ref[2 * index + side] = mine[:, columns]
            theirs_ref[2 * index + side] = theirs[:, columns]


def add_kernel(near_ref, near_other_ref, far_ref, far_other_ref, out_ref):
    for diffs, mine_ref, other_ref in (
        (NEAR_DIFFS, near_ref, near_other_ref),
        (FAR_DIFFS, far_ref, far_other_ref),
    ):
        for index, diff in enumerate(diffs):
            for side in range(2):
                total = mine_ref[2 * index + side] + other_ref[2 * index + side].astype(jnp.float32)
                out_ref[2 * diff + side] = total.astype(jnp.bfloat16)


def window_kernel(coefs_ref, in_ref, out_ref):
    coefs = [coefs_ref[step : step + 1, :] for step in range(F // 2 + 1)]

    def chunk(index, carry):
        rows = pl.ds(pl.multiple_of(index * 16, 16), 16)
        data = [in_ref[g, rows, :].astype(jnp.float32) for g in range(F)]
        for f in range(F):
            total = coefs[0] * data[f] + coefs[F // 2] * data[(f + F // 2) % F]
            for step in range(1, F // 2):
                total = total + coefs[step] * (data[(f + step) % F] + data[(f - step) % F])
            out_ref[f, rows, :] = total.astype(jnp.bfloat16)
        return carry

    lax.fori_loop(0, HALF // 16, chunk, 0)


def place():
    core = lax.axis_index("core")
    zh = lax.axis_index("zh")
    zl = lax.axis_index("zl")
    return core, 2 * zh + zl, 2 * zh + core, 4 * zl


def copy_in(entry, piece_ref, g_ref, sem):
    step, carried, own = entry
    core, here, _, _ = place()
    away = jnp.where(core == 0, -1, 1)
    plane = (here + (away if carried else -away) * step + NB) % NB
    half = core if own else 1 - core
    return pltpu.make_async_copy(piece_ref, g_ref.at[half, plane], sem)


def read_block(g_ref, a, diff):
    plane = (a - home_shift(diff) + NB) % NB
    halves = [
        jnp.concatenate([g_ref[h, plane, 2 * diff], g_ref[h, plane, 2 * diff + 1]], axis=1)
        for h in range(2)
    ]
    return jnp.concatenate(halves, axis=0)


def prepare_kernel(*refs):
    pieces = refs[: NPIECES - 2]
    g_ref, left_ref, sems = refs[NPIECES - 2 :]
    _, _, i, _ = place()
    copies = []
    for index, piece_ref in enumerate(pieces):
        copy = copy_in(PIECES[index], piece_ref, g_ref, sems.at[index])
        copy.start()
        copies.append(copy)
    for copy in copies:
        copy.wait()
    for step in range(NB):
        columns = pl.ds(step * BLOCK, BLOCK)
        left_ref[:BLOCK, columns] = read_block(g_ref, i, jnp.int32(step))
        k = (i + step) % NB
        across = read_block(g_ref, k, jnp.int32((NB - step) % NB))
        left_ref[BLOCK:, columns] = across.astype(jnp.float32).T.astype(jnp.bfloat16)


def panel(m, g_ref, left_ref, out_ref):
    core, _, i, first = place()
    y = lax.axis_index("y")
    aside = jnp.where(core == y // 2, 0, 2)
    j = first + (y + m + aside) % GROUP
    downs = []
    acrosses = []
    for step in range(NB):
        k = (i + step) % NB
        downs.append(read_block(g_ref, k, (j - k + NB) % NB))
        acrosses.append(read_block(g_ref, j, (k - j + NB) % NB))
    down = jnp.concatenate(downs, axis=0)
    across = jnp.concatenate(acrosses, axis=1)
    first = jnp.dot(left_ref[...], down, preferred_element_type=jnp.float32)
    second = lax.dot_general(
        left_ref[...], across, (((1,), (1,)), ((), ())), preferred_element_type=jnp.float32
    )
    scale = jnp.float32(0.5 / math.sqrt(S))
    out_ref[0] = ((second[:BLOCK] + first[BLOCK:]) * scale).astype(jnp.bfloat16)
    out_ref[1] = ((first[:BLOCK] - second[BLOCK:]) * scale).astype(jnp.bfloat16)


def panels_kernel(order, first, *refs):
    if first:
        left_ref, last_ref, last_swap_ref, g_ref = refs[1:5]
        out_refs = refs[5:-1]
        sems = refs[-1]
        copies = [
            copy_in(PIECES[-2], last_ref, g_ref, sems.at[0]),
            copy_in(PIECES[-1], last_swap_ref, g_ref, sems.at[1]),
        ]
        for copy in copies:
            copy.start()
        for copy in copies:
            copy.wait()
    else:
        left_ref, g_ref = refs[:2]
        out_refs = refs[2:]
    for m, out_ref in zip(order, out_refs):
        panel(m, g_ref, left_ref, out_ref)


def join_kernel(moved, *refs):
    pieces = refs[: len(moved)]
    out_ref, sems = refs[-2:]
    core = lax.axis_index("core")
    y = lax.axis_index("y")
    copies = []
    for index, m in enumerate(moved):
        source = (y - m + GROUP) % GROUP
        half = jnp.where(source // 2 == core, core, 1 - core)
        rows = pl.ds(pl.multiple_of(half * BLOCK, BLOCK), BLOCK)
        copies.append(
            pltpu.make_async_copy(
                pieces[index], out_ref.at[:, source % 2, rows, :], sems.at[index]
            )
        )
    for copy in copies:
        copy.start()
    for copy in copies:
        copy.wait()


def call(kernel, shapes, *args, spaces=None, out_space=pltpu.VMEM, scratch=(), aliases=None, flops=0, mib=16):
    shapes = [shape if isinstance(shape, jax.ShapeDtypeStruct) else bf16(shape) for shape in shapes]
    spaces = spaces or [pltpu.VMEM] * len(args)
    moved = sum(arg.size * arg.dtype.itemsize for arg in args)
    moved += sum(math.prod(shape.shape) * shape.dtype.itemsize for shape in shapes)
    results = pl.pallas_call(
        kernel,
        out_shape=shapes,
        in_specs=[pl.BlockSpec(memory_space=space) for space in spaces],
        out_specs=[pl.BlockSpec(memory_space=out_space)] * len(shapes),
        scratch_shapes=list(scratch),
        input_output_aliases=aliases or {},
        cost_estimate=pl.CostEstimate(flops=flops, bytes_accessed=moved, transcendentals=0),
        compiler_params=pltpu.CompilerParams(vmem_limit_bytes=mib * 1024 * 1024),
    )(*args)
    return results[0] if len(shapes) == 1 else results


def bf16(shape):
    return jax.ShapeDtypeStruct(shape, jnp.bfloat16)


def along_z(value, step):
    return lax.ppermute(value, Z, [(z, (z + step) % NB) for z in range(NB)])


def carry(value):
    moves = [(z, (z + 1) % NB) for z in range(NB)]
    moves += [(NB + z, NB + (z - 1) % NB) for z in range(NB)]
    return lax.ppermute(value, ("core",) + Z, moves)


def other_core(value):
    return lax.ppermute(value, "core", [(0, 1), (1, 0)])


def panel_moves(m):
    moves = []
    for core in range(2):
        for y in range(GROUP):
            if core == y // 2:
                target = (core, (y + m) % GROUP)
            else:
                target = (1 - core, (y + m + 2) % GROUP)
            moves.append((core * GROUP + y, target[0] * GROUP + target[1]))
    return moves


def partial_gram(diffs, planes, values, offsets=None):
    count = 2 * len(diffs)
    shapes = [jax.ShapeDtypeStruct((count, HALF, HALF), jnp.float32), bf16((count, HALF, HALF))]
    spaces = [pltpu.VMEM] * len(values)
    if offsets is not None:
        shapes.append(jax.ShapeDtypeStruct((F, HALF), jnp.float32))
        values = (*values, offsets)
        spaces.append(pltpu.SMEM)
    return call(
        functools.partial(gram_kernel, diffs, planes),
        shapes,
        *values,
        spaces=spaces,
        flops=count * 2 * BLOCK * BLOCK * KK,
    )


def on_device(records, offsets):
    outgoing = records.transpose(2, 0, 1, 3).reshape(F, REC_DEV, 2 * 64)
    arrived = lax.all_to_all(outgoing, ("x", "y"), 0, 0, tiled=True)
    here = call(pack_kernel, [(BLOCK, KK)], arrived)
    below = along_z(here, 1)
    above = along_z(here, -1)
    below2 = along_z(below, 1)
    above2 = along_z(above, -1)
    near, near_theirs, coefs = partial_gram(NEAR_DIFFS, (0, -1, 1), (here, below, above), offsets)
    near_other = other_core(near_theirs)
    far, far_theirs = partial_gram(FAR_DIFFS, (-1, 2, -2), (below, above2, below2))
    far_other = other_core(far_theirs)
    strip = call(add_kernel, [(F, HALF, HALF)], near, near_other, far, far_other)
    bins = lax.all_to_all(strip, ("x", "y"), 0, 0, tiled=True)
    windowed = call(window_kernel, [(F, HALF, HALF)], coefs, bins)
    mine = lax.all_to_all(windowed, ("x", "y"), 0, 0, tiled=True)
    own = {}
    other = {}
    own[0], other[0] = lax.optimization_barrier((mine, other_core(mine)))
    pieces = {(0, True, True): own[0], (0, True, False): other[0]}
    for step in range(1, NB // 2 + 1):
        own[step] = carry(own[step - 1])
        pieces[(step, True, True)] = own[step]
        if step < NB // 2:
            other[step] = carry(other[step - 1])
            pieces[(step, True, False)] = other[step]
        pieces[(step, False, False)] = other_core(own[step])
        if step < NB // 2:
            pieces[(step, False, True)] = other_core(other[step])
    pieces = [pieces[key] for key in PIECES]
    whole_shape = (2, NB, F, HALF, HALF)
    whole, left = call(
        prepare_kernel,
        [whole_shape, (2 * BLOCK, S)],
        *pieces[:-2],
        spaces=[pl.ANY] * (NPIECES - 2),
        scratch=[pltpu.SemaphoreType.DMA((NPIECES - 2,))],
    )
    tile = (2, BLOCK, BLOCK)
    panel_flops = 2 * 2 * (2 * BLOCK) * BLOCK * S
    out_shape = (2, 2, 2 * BLOCK, BLOCK)
    joined = []
    for order in PANELS:
        first = order is PANELS[0]
        kernel = functools.partial(panels_kernel, order, first)
        shapes = [tile] * len(order)
        flops = panel_flops * len(order)
        if first:
            whole, *panels = call(
                kernel,
                [whole_shape] + shapes,
                whole,
                left,
                *pieces[-2:],
                spaces=[pltpu.VMEM, pltpu.VMEM, pl.ANY, pl.ANY],
                scratch=[pltpu.SemaphoreType.DMA((2,))],
                aliases={0: 0},
                flops=flops,
            )
        else:
            panels = call(kernel, shapes, left, whole, flops=flops)
            panels = panels if len(order) > 1 else [panels]
        arrived = [
            lax.ppermute(value, ("core", "y"), panel_moves(m)) for m, value in zip(order, panels)
        ]
        joined = [
            call(
                functools.partial(join_kernel, order),
                [out_shape],
                *arrived,
                *joined,
                spaces=[pl.ANY] * (len(arrived) + len(joined)),
                out_space=pl.ANY,
                scratch=[pltpu.SemaphoreType.DMA((len(order),))],
                aliases={len(order): 0} if joined else None,
            )
        ]
    return joined[0]


def solution(mesh):
    fine = Mesh(mesh.devices.reshape(4, 2, 4, 2, 4), ("x", "core", "zh", "zl", "y"))
    return jax.shard_map(
        on_device,
        mesh=fine,
        in_specs=(P(("x", "core"), None, None, ("zh", "zl", "y")), P()),
        out_specs=P(None, ("x", "core"), "zh", ("zl", "y")),
        check_vma=False,
    )
```

```python
import functools
import math

import jax
import jax.numpy as jnp
import numpy as np
from jax import lax
from jax.experimental import pallas as pl
from jax.experimental.pallas import tpu as pltpu
from jax.sharding import Mesh, PartitionSpec as P

S = 2048
F = 16
RECORDS = 384
BLOCK = 256
HALF = 128
NOFF = 4
NB = 8
REC_DEV = 48
GROUP = 4
NK = GROUP * REC_DEV
KK = 2 * NK
NEAR_DIFFS = (0, 1, 7, 2, 6)
FAR_DIFFS = (3, 5, 4)
PANELS = ((2,), (0,), (1,), (3,))
Z = ("zh", "zl")


def lag_profile():
    lag = np.minimum(np.arange(F), F - np.arange(F))
    rows = []
    for offset in range(NOFF):
        inside = (lag >= offset + 2) & (lag < offset + 5)
        weights = np.where(inside, 1.0, 0.1)
        step = np.arange(F // 2 + 1)
        angles = 2.0 * np.pi * (step[:, None] * np.arange(F)[None, :] % F) / F
        rows.append(np.cos(angles) @ weights / F)
    return [[float(value) for value in row] for row in rows]


LAG_PROFILE = lag_profile()


def home_shift(diff):
    return jnp.where(diff <= 4, -(diff // 2), (9 - diff) // 2)


HOME = [0, 0, -1, -1, -2, 2, 1, 1]

PIECES = [(0, True, True), (0, True, False)]
for _step in range(1, NB // 2):
    PIECES += [
        (_step, True, True),
        (_step, True, False),
        (_step, False, False),
        (_step, False, True),
    ]
PIECES += [(NB // 2, True, True), (NB // 2, False, False)]
NPIECES = len(PIECES)


def pack_kernel(y_ref, out_ref):
    for part in range(GROUP):
        rows = jnp.concatenate([y_ref[line * GROUP + part] for line in range(GROUP)], axis=0)
        turned = rows.astype(jnp.float32).T.astype(jnp.bfloat16)
        both = jnp.concatenate([turned[:64], turned[64:]], axis=1)
        out_ref[part * 64 : (part + 1) * 64, :] = both


def write_coefs(offsets_ref, coefs_ref):
    piece = lax.axis_index("x") * GROUP + lax.axis_index("y")
    plane = lax.axis_index("zh") * 2 + lax.axis_index("zl")
    diff = piece // 2
    a = (plane + home_shift(diff) + NB) % NB
    b = (a + diff) % NB
    shift = (offsets_ref[a, b] + offsets_ref[b, a]) % NOFF
    for step in range(F // 2 + 1):
        value = jnp.float32(LAG_PROFILE[0][step])
        for offset in range(1, NOFF):
            value = jnp.where(shift == offset, jnp.float32(LAG_PROFILE[offset][step]), value)
        coefs_ref[step : step + 1, :] = jnp.full((1, HALF), value, jnp.float32)


def gram_kernel(diffs, planes, *refs):
    if len(refs) > len(planes) + 2:
        write_coefs(refs[len(planes)], refs[-1])
        refs = refs[: len(planes)] + refs[len(planes) + 1 : -1]
    rights = {plane: ref[...] for plane, ref in zip(planes, refs)}
    mine_ref, theirs_ref = refs[len(planes) :]
    first_core = lax.axis_index("core") == 0
    lane = lax.broadcasted_iota(jnp.int32, (BLOCK, KK), 1)
    sign = jnp.where(lane < NK, -1.0, 1.0).astype(jnp.float32)
    scale = jnp.float32(1.0 / math.sqrt(RECORDS))
    lefts = {}
    for plane in sorted({HOME[diff] for diff in diffs}):
        top = rights[plane]
        bottom = (pltpu.roll(top.astype(jnp.float32), NK, 1) * sign).astype(jnp.bfloat16)
        lefts[plane] = jnp.concatenate([top, bottom], axis=0)
    for index, diff in enumerate(diffs):
        a = HOME[diff]
        b = (a + diff + 3) % NB - 3
        both = lax.dot_general(
            lefts[a], rights[b], (((1,), (1,)), ((), ())), preferred_element_type=jnp.float32
        )
        tile = (both[:BLOCK] + both[BLOCK:]) * scale
        mine = jnp.where(first_core, tile[:HALF], tile[HALF:])
        theirs = jnp.where(first_core, tile[HALF:], tile[:HALF]).astype(jnp.bfloat16)
        for side in range(2):
            columns = slice(side * HALF, (side + 1) * HALF)
            mine_ref[2 * index + side] = mine[:, columns]
            theirs_ref[2 * index + side] = theirs[:, columns]


def add_kernel(near_ref, near_other_ref, far_ref, far_other_ref, out_ref):
    for diffs, mine_ref, other_ref in (
        (NEAR_DIFFS, near_ref, near_other_ref),
        (FAR_DIFFS, far_ref, far_other_ref),
    ):
        for index, diff in enumerate(diffs):
            for side in range(2):
                total = mine_ref[2 * index + side] + other_ref[2 * index + side].astype(jnp.float32)
                out_ref[2 * diff + side] = total.astype(jnp.bfloat16)


def window_kernel(coefs_ref, in_ref, out_ref):
    coefs = [coefs_ref[step : step + 1, :] for step in range(F // 2 + 1)]

    def chunk(index, carry):
        rows = pl.ds(pl.multiple_of(index * 16, 16), 16)
        data = [in_ref[g, rows, :].astype(jnp.float32) for g in range(F)]
        for f in range(F):
            total = coefs[0] * data[f] + coefs[F // 2] * data[(f + F // 2) % F]
            for step in range(1, F // 2):
                total = total + coefs[step] * (data[(f + step) % F] + data[(f - step) % F])
            out_ref[f, rows, :] = total.astype(jnp.bfloat16)
        return carry

    lax.fori_loop(0, HALF // 16, chunk, 0)


def place():
    core = lax.axis_index("core")
    zh = lax.axis_index("zh")
    zl = lax.axis_index("zl")
    return core, 2 * zh + zl, 2 * zh + core, 4 * zl


def copy_in(entry, piece_ref, g_ref, sem):
    step, carried, own = entry
    core, here, _, _ = place()
    away = jnp.where(core == 0, -1, 1)
    plane = (here + (away if carried else -away) * step + NB) % NB
    half = core if own else 1 - core
    return pltpu.make_async_copy(piece_ref, g_ref.at[half, plane], sem)


def read_block(g_ref, a, diff):
    plane = (a - home_shift(diff) + NB) % NB
    halves = [
        jnp.concatenate([g_ref[h, plane, 2 * diff], g_ref[h, plane, 2 * diff + 1]], axis=1)
        for h in range(2)
    ]
    return jnp.concatenate(halves, axis=0)


def prepare_kernel(*refs):
    pieces = refs[: NPIECES - 2]
    g_ref, left_ref, sems = refs[NPIECES - 2 :]
    _, _, i, _ = place()
    copies = []
    for index, piece_ref in enumerate(pieces):
        copy = copy_in(PIECES[index], piece_ref, g_ref, sems.at[index])
        copy.start()
        copies.append(copy)
    for copy in copies:
        copy.wait()
    for step in range(NB):
        columns = pl.ds(step * BLOCK, BLOCK)
        left_ref[:BLOCK, columns] = read_block(g_ref, i, jnp.int32(step))
        k = (i + step) % NB
        across = read_block(g_ref, k, jnp.int32((NB - step) % NB))
        left_ref[BLOCK:, columns] = across.astype(jnp.float32).T.astype(jnp.bfloat16)


def panel(m, g_ref, left_ref, out_ref):
    core, _, i, first = place()
    y = lax.axis_index("y")
    aside = jnp.where(core == y // 2, 0, 2)
    j = first + (y + m + aside) % GROUP
    downs = []
    acrosses = []
    for step in range(NB):
        k = (i + step) % NB
        downs.append(read_block(g_ref, k, (j - k + NB) % NB))
        acrosses.append(read_block(g_ref, j, (k - j + NB) % NB))
    down = jnp.concatenate(downs, axis=0)
    across = jnp.concatenate(acrosses, axis=1)
    first = jnp.dot(left_ref[...], down, preferred_element_type=jnp.float32)
    second = lax.dot_general(
        left_ref[...], across, (((1,), (1,)), ((), ())), preferred_element_type=jnp.float32
    )
    scale = jnp.float32(0.5 / math.sqrt(S))
    out_ref[0] = ((second[:BLOCK] + first[BLOCK:]) * scale).astype(jnp.bfloat16)
    out_ref[1] = ((first[:BLOCK] - second[BLOCK:]) * scale).astype(jnp.bfloat16)


def panels_kernel(order, first, *refs):
    if first:
        left_ref, last_ref, last_swap_ref, g_ref = refs[1:5]
        out_refs = refs[5:-1]
        sems = refs[-1]
        copies = [
            copy_in(PIECES[-2], last_ref, g_ref, sems.at[0]),
            copy_in(PIECES[-1], last_swap_ref, g_ref, sems.at[1]),
        ]
        for copy in copies:
            copy.start()
        for copy in copies:
            copy.wait()
    else:
        left_ref, g_ref = refs[:2]
        out_refs = refs[2:]
    for m, out_ref in zip(order, out_refs):
        panel(m, g_ref, left_ref, out_ref)


def join_kernel(moved, *refs):
    pieces = refs[: len(moved)]
    out_ref, sems = refs[-2:]
    core = lax.axis_index("core")
    y = lax.axis_index("y")
    copies = []
    for index, m in enumerate(moved):
        source = (y - m + GROUP) % GROUP
        half = jnp.where(source // 2 == core, core, 1 - core)
        rows = pl.ds(pl.multiple_of(half * BLOCK, BLOCK), BLOCK)
        copies.append(
            pltpu.make_async_copy(
                pieces[index], out_ref.at[:, source % 2, rows, :], sems.at[index]
            )
        )
    for copy in copies:
        copy.start()
    for copy in copies:
        copy.wait()


def call(kernel, shapes, *args, spaces=None, out_space=pltpu.VMEM, scratch=(), aliases=None, flops=0, mib=16):
    shapes = [shape if isinstance(shape, jax.ShapeDtypeStruct) else bf16(shape) for shape in shapes]
    spaces = spaces or [pltpu.VMEM] * len(args)
    cost = None
    if flops is not None:
        moved = sum(arg.size * arg.dtype.itemsize for arg in args)
        moved += sum(math.prod(shape.shape) * shape.dtype.itemsize for shape in shapes)
        cost = pl.CostEstimate(flops=flops, bytes_accessed=moved, transcendentals=0)
    results = pl.pallas_call(
        kernel,
        out_shape=shapes,
        in_specs=[pl.BlockSpec(memory_space=space) for space in spaces],
        out_specs=[pl.BlockSpec(memory_space=out_space)] * len(shapes),
        scratch_shapes=list(scratch),
        input_output_aliases=aliases or {},
        cost_estimate=cost,
        compiler_params=pltpu.CompilerParams(vmem_limit_bytes=mib * 1024 * 1024),
    )(*args)
    return results[0] if len(shapes) == 1 else results


def bf16(shape):
    return jax.ShapeDtypeStruct(shape, jnp.bfloat16)


def along_z(value, step):
    return lax.ppermute(value, Z, [(z, (z + step) % NB) for z in range(NB)])


def carry(value):
    moves = [(z, (z + 1) % NB) for z in range(NB)]
    moves += [(NB + z, NB + (z - 1) % NB) for z in range(NB)]
    return lax.ppermute(value, ("core",) + Z, moves)


def other_core(value):
    return lax.ppermute(value, "core", [(0, 1), (1, 0)])


def panel_moves(m):
    moves = []
    for core in range(2):
        for y in range(GROUP):
            if core == y // 2:
                target = (core, (y + m) % GROUP)
            else:
                target = (1 - core, (y + m + 2) % GROUP)
            moves.append((core * GROUP + y, target[0] * GROUP + target[1]))
    return moves


def partial_gram(diffs, planes, values, offsets=None):
    count = 2 * len(diffs)
    shapes = [jax.ShapeDtypeStruct((count, HALF, HALF), jnp.float32), bf16((count, HALF, HALF))]
    spaces = [pltpu.VMEM] * len(values)
    if offsets is not None:
        shapes.append(jax.ShapeDtypeStruct((F, HALF), jnp.float32))
        values = (*values, offsets)
        spaces.append(pltpu.SMEM)
    return call(
        functools.partial(gram_kernel, diffs, planes),
        shapes,
        *values,
        spaces=spaces,
        flops=count * 2 * BLOCK * BLOCK * KK,
    )


def on_device(records, offsets):
    outgoing = records.transpose(2, 0, 1, 3).reshape(F, REC_DEV, 2 * 64)
    arrived = lax.all_to_all(outgoing, ("x", "y"), 0, 0, tiled=True)
    here = call(pack_kernel, [(BLOCK, KK)], arrived)
    below = along_z(here, 1)
    above = along_z(here, -1)
    below2 = along_z(below, 1)
    above2 = along_z(above, -1)
    near, near_theirs, coefs = partial_gram(NEAR_DIFFS, (0, -1, 1), (here, below, above), offsets)
    near_other = other_core(near_theirs)
    far, far_theirs = partial_gram(FAR_DIFFS, (-1, 2, -2), (below, above2, below2))
    far_other = other_core(far_theirs)
    strip = call(add_kernel, [(F, HALF, HALF)], near, near_other, far, far_other)
    bins = lax.all_to_all(strip, ("x", "y"), 0, 0, tiled=True)
    windowed = call(window_kernel, [(F, HALF, HALF)], coefs, bins)
    mine = lax.all_to_all(windowed, ("x", "y"), 0, 0, tiled=True)
    own = {}
    other = {}
    own[0], other[0] = mine, other_core(mine)
    pieces = {(0, True, True): own[0], (0, True, False): other[0]}
    for step in range(1, NB // 2 + 1):
        own[step] = carry(own[step - 1])
        pieces[(step, True, True)] = own[step]
        if step < NB // 2:
            other[step] = carry(other[step - 1])
            pieces[(step, True, False)] = other[step]
        pieces[(step, False, False)] = other_core(own[step])
        if step < NB // 2:
            pieces[(step, False, True)] = other_core(other[step])
    pieces = [pieces[key] for key in PIECES]
    whole_shape = (2, NB, F, HALF, HALF)
    whole, left = call(
        prepare_kernel,
        [whole_shape, (2 * BLOCK, S)],
        *pieces[:-2],
        spaces=[pl.ANY] * (NPIECES - 2),
        scratch=[pltpu.SemaphoreType.DMA((NPIECES - 2,))],
    )
    tile = (2, BLOCK, BLOCK)
    out_shape = (2, 2, 2 * BLOCK, BLOCK)
    joined = []
    for order in PANELS:
        first = order is PANELS[0]
        kernel = functools.partial(panels_kernel, order, first)
        shapes = [tile] * len(order)
        if first:
            whole, *panels = call(
                kernel,
                [whole_shape] + shapes,
                whole,
                left,
                *pieces[-2:],
                spaces=[pltpu.VMEM, pltpu.VMEM, pl.ANY, pl.ANY],
                scratch=[pltpu.SemaphoreType.DMA((2,))],
                aliases={0: 0},
                flops=None,
            )
        else:
            panels = call(kernel, shapes, left, whole, flops=None)
            panels = panels if len(order) > 1 else [panels]
        arrived = [
            lax.ppermute(value, ("core", "y"), panel_moves(m)) for m, value in zip(order, panels)
        ]
        joined = [
            call(
                functools.partial(join_kernel, order),
                [out_shape],
                *arrived,
                *joined,
                spaces=[pl.ANY] * (len(arrived) + len(joined)),
                out_space=pl.ANY,
                scratch=[pltpu.SemaphoreType.DMA((len(order),))],
                aliases={len(order): 0} if joined else None,
            )
        ]
    return joined[0]


def solution(mesh):
    fine = Mesh(mesh.devices.reshape(4, 2, 4, 2, 4), ("x", "core", "zh", "zl", "y"))
    return jax.shard_map(
        on_device,
        mesh=fine,
        in_specs=(P(("x", "core"), None, None, ("zh", "zl", "y")), P()),
        out_specs=P(None, ("x", "core"), "zh", ("zl", "y")),
        check_vma=False,
    )
```

```python
import functools
import math

import jax
import jax.numpy as jnp
import numpy as np
from jax import lax
from jax.experimental import pallas as pl
from jax.experimental.pallas import tpu as pltpu
from jax.sharding import Mesh, PartitionSpec as P

S = 2048
F = 16
RECORDS = 384
BLOCK = 256
HALF = 128
NOFF = 4
NB = 8
REC_DEV = 48
GROUP = 4
NK = GROUP * REC_DEV
KK = 2 * NK
NEAR_DIFFS = (0, 1, 7, 2, 6)
FAR_DIFFS = (3, 5, 4)
PANELS = ((2, 0), (1,), (3,))
Z = ("zh", "zl")


def lag_profile():
    lag = np.minimum(np.arange(F), F - np.arange(F))
    rows = []
    for offset in range(NOFF):
        inside = (lag >= offset + 2) & (lag < offset + 5)
        weights = np.where(inside, 1.0, 0.1)
        step = np.arange(F // 2 + 1)
        angles = 2.0 * np.pi * (step[:, None] * np.arange(F)[None, :] % F) / F
        rows.append(np.cos(angles) @ weights / F)
    return [[float(value) for value in row] for row in rows]


LAG_PROFILE = lag_profile()


def home_shift(diff):
    return jnp.where(diff <= 4, -(diff // 2), (9 - diff) // 2)


HOME = [0, 0, -1, -1, -2, 2, 1, 1]

PIECES = [(0, True, True), (0, True, False)]
for _step in range(1, NB // 2):
    PIECES += [
        (_step, True, True),
        (_step, True, False),
        (_step, False, False),
        (_step, False, True),
    ]
PIECES += [(NB // 2, True, True), (NB // 2, False, False)]
NPIECES = len(PIECES)


def pack_kernel(y_ref, out_ref):
    for part in range(GROUP):
        rows = jnp.concatenate([y_ref[line * GROUP + part] for line in range(GROUP)], axis=0)
        turned = rows.astype(jnp.float32).T.astype(jnp.bfloat16)
        both = jnp.concatenate([turned[:64], turned[64:]], axis=1)
        out_ref[part * 64 : (part + 1) * 64, :] = both


def write_coefs(offsets_ref, coefs_ref):
    piece = lax.axis_index("x") * GROUP + lax.axis_index("y")
    plane = lax.axis_index("zh") * 2 + lax.axis_index("zl")
    diff = piece // 2
    a = (plane + home_shift(diff) + NB) % NB
    b = (a + diff) % NB
    shift = (offsets_ref[a, b] + offsets_ref[b, a]) % NOFF
    for step in range(F // 2 + 1):
        value = jnp.float32(LAG_PROFILE[0][step])
        for offset in range(1, NOFF):
            value = jnp.where(shift == offset, jnp.float32(LAG_PROFILE[offset][step]), value)
        coefs_ref[step : step + 1, :] = jnp.full((1, HALF), value, jnp.float32)


def gram_kernel(diffs, single, pairs, *refs):
    count = len(single) + 2 * len(pairs)
    if len(refs) > count + 2:
        write_coefs(refs[count], refs[-1])
        refs = refs[:count] + refs[count + 1 : -1]
    first_core = lax.axis_index("core") == 0
    rights = {plane: refs[index][...] for index, plane in enumerate(single)}
    for index, plane in enumerate(pairs):
        behind = refs[len(single) + 2 * index][...]
        ahead = refs[len(single) + 2 * index + 1][...]
        rights[-plane] = jnp.where(first_core, behind, ahead)
        rights[plane] = jnp.where(first_core, ahead, behind)
    mine_ref, theirs_ref = refs[count:]
    lane = lax.broadcasted_iota(jnp.int32, (BLOCK, KK), 1)
    sign = jnp.where(lane < NK, -1.0, 1.0).astype(jnp.float32)
    scale = jnp.float32(1.0 / math.sqrt(RECORDS))
    lefts = {}
    for plane in sorted({HOME[diff] for diff in diffs}):
        top = rights[plane]
        bottom = (pltpu.roll(top.astype(jnp.float32), NK, 1) * sign).astype(jnp.bfloat16)
        lefts[plane] = jnp.concatenate([top, bottom], axis=0)
    for index, diff in enumerate(diffs):
        a = HOME[diff]
        b = (a + diff + 3) % NB - 3
        both = lax.dot_general(
            lefts[a], rights[b], (((1,), (1,)), ((), ())), preferred_element_type=jnp.float32
        )
        tile = (both[:BLOCK] + both[BLOCK:]) * scale
        mine = jnp.where(first_core, tile[:HALF], tile[HALF:])
        theirs = jnp.where(first_core, tile[HALF:], tile[:HALF]).astype(jnp.bfloat16)
        for side in range(2):
            columns = slice(side * HALF, (side + 1) * HALF)
            mine_ref[2 * index + side] = mine[:, columns]
            theirs_ref[2 * index + side] = theirs[:, columns]


def add_kernel(near_ref, near_other_ref, far_ref, far_other_ref, out_ref):
    for diffs, mine_ref, other_ref in (
        (NEAR_DIFFS, near_ref, near_other_ref),
        (FAR_DIFFS, far_ref, far_other_ref),
    ):
        for index, diff in enumerate(diffs):
            for side in range(2):
                total = mine_ref[2 * index + side] + other_ref[2 * index + side].astype(jnp.float32)
                out_ref[2 * diff + side] = total.astype(jnp.bfloat16)


def window_kernel(coefs_ref, in_ref, out_ref):
    coefs = [coefs_ref[step : step + 1, :] for step in range(F // 2 + 1)]

    def chunk(index, carry):
        rows = pl.ds(pl.multiple_of(index * 16, 16), 16)
        data = [in_ref[g, rows, :].astype(jnp.float32) for g in range(F)]
        for f in range(F):
            total = coefs[0] * data[f] + coefs[F // 2] * data[(f + F // 2) % F]
            for step in range(1, F // 2):
                total = total + coefs[step] * (data[(f + step) % F] + data[(f - step) % F])
            out_ref[f, rows, :] = total.astype(jnp.bfloat16)
        return carry

    lax.fori_loop(0, HALF // 16, chunk, 0)


def place():
    core = lax.axis_index("core")
    zh = lax.axis_index("zh")
    zl = lax.axis_index("zl")
    return core, 2 * zh + zl, 2 * zh + core, 4 * zl


def copy_in(entry, piece_ref, g_ref, sem):
    step, carried, own = entry
    core, here, _, _ = place()
    away = jnp.where(core == 0, -1, 1)
    plane = (here + (away if carried else -away) * step + NB) % NB
    half = core if own else 1 - core
    return pltpu.make_async_copy(piece_ref, g_ref.at[half, plane], sem)


def read_block(g_ref, a, diff):
    plane = (a - home_shift(diff) + NB) % NB
    halves = [
        jnp.concatenate([g_ref[h, plane, 2 * diff], g_ref[h, plane, 2 * diff + 1]], axis=1)
        for h in range(2)
    ]
    return jnp.concatenate(halves, axis=0)


def prepare_kernel(*refs):
    pieces = refs[: NPIECES - 2]
    g_ref, left_ref, sems = refs[NPIECES - 2 :]
    _, _, i, _ = place()
    copies = []
    for index, piece_ref in enumerate(pieces):
        copy = copy_in(PIECES[index], piece_ref, g_ref, sems.at[index])
        copy.start()
        copies.append(copy)
    for copy in copies:
        copy.wait()
    for step in range(NB):
        columns = pl.ds(step * BLOCK, BLOCK)
        left_ref[:BLOCK, columns] = read_block(g_ref, i, jnp.int32(step))
        k = (i + step) % NB
        across = read_block(g_ref, k, jnp.int32((NB - step) % NB))
        left_ref[BLOCK:, columns] = across.astype(jnp.float32).T.astype(jnp.bfloat16)


def panel(m, g_ref, left_ref, out_ref):
    core, _, i, first = place()
    y = lax.axis_index("y")
    aside = jnp.where(core == y // 2, 0, 2)
    j = first + (y + m + aside) % GROUP
    downs = []
    acrosses = []
    for step in range(NB):
        k = (i + step) % NB
        downs.append(read_block(g_ref, k, (j - k + NB) % NB))
        acrosses.append(read_block(g_ref, j, (k - j + NB) % NB))
    down = jnp.concatenate(downs, axis=0)
    across = jnp.concatenate(acrosses, axis=1)
    first = jnp.dot(left_ref[...], down, preferred_element_type=jnp.float32)
    second = lax.dot_general(
        left_ref[...], across, (((1,), (1,)), ((), ())), preferred_element_type=jnp.float32
    )
    scale = jnp.float32(0.5 / math.sqrt(S))
    out_ref[0] = ((second[:BLOCK] + first[BLOCK:]) * scale).astype(jnp.bfloat16)
    out_ref[1] = ((first[:BLOCK] - second[BLOCK:]) * scale).astype(jnp.bfloat16)


def panels_kernel(order, first, *refs):
    if first:
        left_ref, last_ref, last_swap_ref, g_ref = refs[1:5]
        out_refs = refs[5:-1]
        sems = refs[-1]
        copies = [
            copy_in(PIECES[-2], last_ref, g_ref, sems.at[0]),
            copy_in(PIECES[-1], last_swap_ref, g_ref, sems.at[1]),
        ]
        for copy in copies:
            copy.start()
        for copy in copies:
            copy.wait()
    else:
        left_ref, g_ref = refs[:2]
        out_refs = refs[2:]
    for m, out_ref in zip(order, out_refs):
        panel(m, g_ref, left_ref, out_ref)


def join_kernel(moved, *refs):
    pieces = refs[: len(moved)]
    out_ref, sems = refs[-2:]
    core = lax.axis_index("core")
    y = lax.axis_index("y")
    copies = []
    for index, m in enumerate(moved):
        source = (y - m + GROUP) % GROUP
        half = jnp.where(source // 2 == core, core, 1 - core)
        rows = pl.ds(pl.multiple_of(half * BLOCK, BLOCK), BLOCK)
        copies.append(
            pltpu.make_async_copy(
                pieces[index], out_ref.at[:, source % 2, rows, :], sems.at[index]
            )
        )
    for copy in copies:
        copy.start()
    for copy in copies:
        copy.wait()


def call(kernel, shapes, *args, spaces=None, out_space=pltpu.VMEM, scratch=(), aliases=None, flops=0, mib=16):
    shapes = [shape if isinstance(shape, jax.ShapeDtypeStruct) else bf16(shape) for shape in shapes]
    spaces = spaces or [pltpu.VMEM] * len(args)
    cost = None
    if flops is not None:
        moved = sum(arg.size * arg.dtype.itemsize for arg in args)
        moved += sum(math.prod(shape.shape) * shape.dtype.itemsize for shape in shapes)
        cost = pl.CostEstimate(flops=flops, bytes_accessed=moved, transcendentals=0)
    results = pl.pallas_call(
        kernel,
        out_shape=shapes,
        in_specs=[pl.BlockSpec(memory_space=space) for space in spaces],
        out_specs=[pl.BlockSpec(memory_space=out_space)] * len(shapes),
        scratch_shapes=list(scratch),
        input_output_aliases=aliases or {},
        cost_estimate=cost,
        compiler_params=pltpu.CompilerParams(vmem_limit_bytes=mib * 1024 * 1024),
    )(*args)
    return results[0] if len(shapes) == 1 else results


def bf16(shape):
    return jax.ShapeDtypeStruct(shape, jnp.bfloat16)


def carry(value, step=1):
    moves = [(z, (z + step) % NB) for z in range(NB)]
    moves += [(NB + z, NB + (z - step) % NB) for z in range(NB)]
    return lax.ppermute(value, ("core",) + Z, moves)


def other_core(value):
    return lax.ppermute(value, "core", [(0, 1), (1, 0)])


def panel_moves(m):
    moves = []
    for core in range(2):
        for y in range(GROUP):
            if core == y // 2:
                target = (core, (y + m) % GROUP)
            else:
                target = (1 - core, (y + m + 2) % GROUP)
            moves.append((core * GROUP + y, target[0] * GROUP + target[1]))
    return moves


def partial_gram(diffs, single, pairs, values, offsets=None):
    count = 2 * len(diffs)
    shapes = [jax.ShapeDtypeStruct((count, HALF, HALF), jnp.float32), bf16((count, HALF, HALF))]
    spaces = [pltpu.VMEM] * len(values)
    if offsets is not None:
        shapes.append(jax.ShapeDtypeStruct((F, HALF), jnp.float32))
        values = (*values, offsets)
        spaces.append(pltpu.SMEM)
    return call(
        functools.partial(gram_kernel, diffs, single, pairs),
        shapes,
        *values,
        spaces=spaces,
        flops=count * 2 * BLOCK * BLOCK * KK,
    )


def on_device(records, offsets):
    outgoing = records.transpose(2, 0, 1, 3).reshape(F, REC_DEV, 2 * 64)
    arrived = lax.all_to_all(outgoing, ("x", "y"), 0, 0, tiled=True)
    here = call(pack_kernel, [(BLOCK, KK)], arrived)
    behind = carry(here)
    ahead = carry(here, -1)
    behind2 = carry(behind)
    ahead2 = carry(ahead, -1)
    near, near_theirs, coefs = partial_gram(NEAR_DIFFS, (0,), (1,), (here, behind, ahead), offsets)
    near_other = other_core(near_theirs)
    far, far_theirs = partial_gram(FAR_DIFFS, (), (1, 2), (behind, ahead, behind2, ahead2))
    far_other = other_core(far_theirs)
    strip = call(add_kernel, [(F, HALF, HALF)], near, near_other, far, far_other)
    bins = lax.all_to_all(strip, ("x", "y"), 0, 0, tiled=True)
    windowed = call(window_kernel, [(F, HALF, HALF)], coefs, bins)
    mine = lax.all_to_all(windowed, ("x", "y"), 0, 0, tiled=True)
    own = {}
    other = {}
    own[0], own[1] = mine, carry(mine)
    other[0] = other_core(mine)
    pieces = {(0, True, True): own[0], (0, True, False): other[0]}
    for step in range(1, NB // 2 + 1):
        if step > 1:
            own[step] = carry(own[step - 1])
        pieces[(step, True, True)] = own[step]
        if step < NB // 2:
            other[step] = carry(other[step - 1])
            pieces[(step, True, False)] = other[step]
        pieces[(step, False, False)] = other_core(own[step])
        if step < NB // 2:
            pieces[(step, False, True)] = other_core(other[step])
    pieces = [pieces[key] for key in PIECES]
    whole_shape = (2, NB, F, HALF, HALF)
    whole, left = call(
        prepare_kernel,
        [whole_shape, (2 * BLOCK, S)],
        *pieces[:-2],
        spaces=[pl.ANY] * (NPIECES - 2),
        scratch=[pltpu.SemaphoreType.DMA((NPIECES - 2,))],
    )
    tile = (2, BLOCK, BLOCK)
    out_shape = (2, 2, 2 * BLOCK, BLOCK)
    joined = []
    for order in PANELS:
        first = order is PANELS[0]
        kernel = functools.partial(panels_kernel, order, first)
        shapes = [tile] * len(order)
        if first:
            whole, *panels = call(
                kernel,
                [whole_shape] + shapes,
                whole,
                left,
                *pieces[-2:],
                spaces=[pltpu.VMEM, pltpu.VMEM, pl.ANY, pl.ANY],
                scratch=[pltpu.SemaphoreType.DMA((2,))],
                aliases={0: 0},
                flops=None,
            )
        else:
            panels = call(kernel, shapes, left, whole, flops=None)
            panels = panels if len(order) > 1 else [panels]
        arrived = [
            lax.ppermute(value, ("core", "y"), panel_moves(m)) for m, value in zip(order, panels)
        ]
        joined = [
            call(
                functools.partial(join_kernel, order),
                [out_shape],
                *arrived,
                *joined,
                spaces=[pl.ANY] * (len(arrived) + len(joined)),
                out_space=pl.ANY,
                scratch=[pltpu.SemaphoreType.DMA((len(order),))],
                aliases={len(order): 0} if joined else None,
            )
        ]
    return joined[0]


def solution(mesh):
    fine = Mesh(mesh.devices.reshape(4, 2, 4, 2, 4), ("x", "core", "zh", "zl", "y"))
    return jax.shard_map(
        on_device,
        mesh=fine,
        in_specs=(P(("x", "core"), None, None, ("zh", "zl", "y")), P()),
        out_specs=P(None, ("x", "core"), "zh", ("zl", "y")),
        check_vma=False,
    )
```

```python
import functools
import math

import jax
import jax.numpy as jnp
import numpy as np
from jax import lax
from jax.experimental import pallas as pl
from jax.experimental.pallas import tpu as pltpu
from jax.sharding import Mesh, PartitionSpec as P

S = 2048
F = 16
RECORDS = 384
BLOCK = 256
HALF = 128
NOFF = 4
NB = 8
REC_DEV = 48
GROUP = 4
NK = GROUP * REC_DEV
KK = 2 * NK
NEAR_DIFFS = (0, 1, 7, 2, 6)
FAR_DIFFS = (3, 5, 4)
PANELS = ((2,), (0,), (1,), (3,))
Z = ("zh", "zl")


def lag_profile():
    lag = np.minimum(np.arange(F), F - np.arange(F))
    rows = []
    for offset in range(NOFF):
        inside = (lag >= offset + 2) & (lag < offset + 5)
        weights = np.where(inside, 1.0, 0.1)
        step = np.arange(F // 2 + 1)
        angles = 2.0 * np.pi * (step[:, None] * np.arange(F)[None, :] % F) / F
        rows.append(np.cos(angles) @ weights / F)
    return [[float(value) for value in row] for row in rows]


LAG_PROFILE = lag_profile()


def home_shift(diff):
    return jnp.where(diff <= 4, -(diff // 2), (9 - diff) // 2)


HOME = [0, 0, -1, -1, -2, 2, 1, 1]

PIECES = [(0, True, True), (0, True, False)]
for _step in range(1, NB // 2):
    PIECES += [
        (_step, True, True),
        (_step, True, False),
        (_step, False, False),
        (_step, False, True),
    ]
PIECES += [(NB // 2, True, True), (NB // 2, False, False)]
NPIECES = len(PIECES)


def pack_kernel(y_ref, out_ref):
    for part in range(GROUP):
        rows = jnp.concatenate([y_ref[line * GROUP + part] for line in range(GROUP)], axis=0)
        turned = rows.astype(jnp.float32).T.astype(jnp.bfloat16)
        both = jnp.concatenate([turned[:64], turned[64:]], axis=1)
        out_ref[part * 64 : (part + 1) * 64, :] = both


def write_coefs(offsets_ref, coefs_ref):
    piece = lax.axis_index("x") * GROUP + lax.axis_index("y")
    plane = lax.axis_index("zh") * 2 + lax.axis_index("zl")
    diff = piece // 2
    a = (plane + home_shift(diff) + NB) % NB
    b = (a + diff) % NB
    shift = (offsets_ref[a, b] + offsets_ref[b, a]) % NOFF
    for step in range(F // 2 + 1):
        value = jnp.float32(LAG_PROFILE[0][step])
        for offset in range(1, NOFF):
            value = jnp.where(shift == offset, jnp.float32(LAG_PROFILE[offset][step]), value)
        coefs_ref[step : step + 1, :] = jnp.full((1, HALF), value, jnp.float32)


def gram_kernel(diffs, single, pairs, *refs):
    count = len(single) + 2 * len(pairs)
    if len(refs) > count + 2:
        write_coefs(refs[count], refs[-1])
        refs = refs[:count] + refs[count + 1 : -1]
    first_core = lax.axis_index("core") == 0
    even = lax.axis_index("zl") == 0
    rights = {plane: refs[index][...] for index, plane in enumerate(single)}
    for index, plane in enumerate(pairs):
        first = refs[len(single) + 2 * index][...]
        second = refs[len(single) + 2 * index + 1][...]
        rights[-plane] = jnp.where(even, first, second)
        rights[plane] = jnp.where(even, second, first)
    mine_ref, theirs_ref = refs[count:]
    lane = lax.broadcasted_iota(jnp.int32, (BLOCK, KK), 1)
    sign = jnp.where(lane < NK, -1.0, 1.0).astype(jnp.float32)
    scale = jnp.float32(1.0 / math.sqrt(RECORDS))
    lefts = {}
    for plane in sorted({HOME[diff] for diff in diffs}):
        top = rights[plane]
        bottom = (pltpu.roll(top.astype(jnp.float32), NK, 1) * sign).astype(jnp.bfloat16)
        lefts[plane] = jnp.concatenate([top, bottom], axis=0)
    for index, diff in enumerate(diffs):
        a = HOME[diff]
        b = (a + diff + 3) % NB - 3
        both = lax.dot_general(
            lefts[a], rights[b], (((1,), (1,)), ((), ())), preferred_element_type=jnp.float32
        )
        tile = (both[:BLOCK] + both[BLOCK:]) * scale
        mine = jnp.where(first_core, tile[:HALF], tile[HALF:])
        theirs = jnp.where(first_core, tile[HALF:], tile[:HALF]).astype(jnp.bfloat16)
        for side in range(2):
            columns = slice(side * HALF, (side + 1) * HALF)
            mine_ref[2 * index + side] = mine[:, columns]
            theirs_ref[2 * index + side] = theirs[:, columns]


def add_kernel(near_ref, near_other_ref, far_ref, far_other_ref, out_ref):
    for diffs, mine_ref, other_ref in (
        (NEAR_DIFFS, near_ref, near_other_ref),
        (FAR_DIFFS, far_ref, far_other_ref),
    ):
        for index, diff in enumerate(diffs):
            for side in range(2):
                total = mine_ref[2 * index + side] + other_ref[2 * index + side].astype(jnp.float32)
                out_ref[2 * diff + side] = total.astype(jnp.bfloat16)


def window_kernel(coefs_ref, in_ref, out_ref):
    coefs = [coefs_ref[step : step + 1, :] for step in range(F // 2 + 1)]

    def chunk(index, carry):
        rows = pl.ds(pl.multiple_of(index * 16, 16), 16)
        data = [in_ref[g, rows, :].astype(jnp.float32) for g in range(F)]
        for f in range(F):
            total = coefs[0] * data[f] + coefs[F // 2] * data[(f + F // 2) % F]
            for step in range(1, F // 2):
                total = total + coefs[step] * (data[(f + step) % F] + data[(f - step) % F])
            out_ref[f, rows, :] = total.astype(jnp.bfloat16)
        return carry

    lax.fori_loop(0, HALF // 16, chunk, 0)


def place():
    core = lax.axis_index("core")
    zh = lax.axis_index("zh")
    zl = lax.axis_index("zl")
    return core, 2 * zh + zl, 2 * zh + core, 4 * zl


def copy_in(entry, piece_ref, g_ref, sem):
    step, carried, own = entry
    core, here, _, _ = place()
    away = jnp.where(core == 0, -1, 1)
    plane = (here + (away if carried else -away) * step + NB) % NB
    half = core if own else 1 - core
    return pltpu.make_async_copy(piece_ref, g_ref.at[half, plane], sem)


def read_block(g_ref, a, diff):
    plane = (a - home_shift(diff) + NB) % NB
    halves = [
        jnp.concatenate([g_ref[h, plane, 2 * diff], g_ref[h, plane, 2 * diff + 1]], axis=1)
        for h in range(2)
    ]
    return jnp.concatenate(halves, axis=0)


def prepare_kernel(*refs):
    pieces = refs[: NPIECES - 2]
    g_ref, left_ref, sems = refs[NPIECES - 2 :]
    _, _, i, _ = place()
    copies = []
    for index, piece_ref in enumerate(pieces):
        copy = copy_in(PIECES[index], piece_ref, g_ref, sems.at[index])
        copy.start()
        copies.append(copy)
    for copy in copies:
        copy.wait()
    for step in range(NB):
        columns = pl.ds(step * BLOCK, BLOCK)
        left_ref[:BLOCK, columns] = read_block(g_ref, i, jnp.int32(step))
        k = (i + step) % NB
        across = read_block(g_ref, k, jnp.int32((NB - step) % NB))
        left_ref[BLOCK:, columns] = across.astype(jnp.float32).T.astype(jnp.bfloat16)


def panel(m, g_ref, left_ref, out_ref):
    core, _, i, first = place()
    y = lax.axis_index("y")
    aside = jnp.where(core == y // 2, 0, 2)
    j = first + (y + m + aside) % GROUP
    downs = []
    acrosses = []
    for step in range(NB):
        k = (i + step) % NB
        downs.append(read_block(g_ref, k, (j - k + NB) % NB))
        acrosses.append(read_block(g_ref, j, (k - j + NB) % NB))
    down = jnp.concatenate(downs, axis=0)
    across = jnp.concatenate(acrosses, axis=1)
    first = jnp.dot(left_ref[...], down, preferred_element_type=jnp.float32)
    second = lax.dot_general(
        left_ref[...], across, (((1,), (1,)), ((), ())), preferred_element_type=jnp.float32
    )
    scale = jnp.float32(0.5 / math.sqrt(S))
    out_ref[0] = ((second[:BLOCK] + first[BLOCK:]) * scale).astype(jnp.bfloat16)
    out_ref[1] = ((first[:BLOCK] - second[BLOCK:]) * scale).astype(jnp.bfloat16)


def panels_kernel(order, first, *refs):
    if first:
        left_ref, last_ref, last_swap_ref, g_ref = refs[1:5]
        out_refs = refs[5:-1]
        sems = refs[-1]
        copies = [
            copy_in(PIECES[-2], last_ref, g_ref, sems.at[0]),
            copy_in(PIECES[-1], last_swap_ref, g_ref, sems.at[1]),
        ]
        for copy in copies:
            copy.start()
        for copy in copies:
            copy.wait()
    else:
        left_ref, g_ref = refs[:2]
        out_refs = refs[2:]
    for m, out_ref in zip(order, out_refs):
        panel(m, g_ref, left_ref, out_ref)


def join_kernel(moved, *refs):
    pieces = refs[: len(moved)]
    out_ref, sems = refs[-2:]
    core = lax.axis_index("core")
    y = lax.axis_index("y")
    copies = []
    for index, m in enumerate(moved):
        source = (y - m + GROUP) % GROUP
        half = jnp.where(source // 2 == core, core, 1 - core)
        rows = pl.ds(pl.multiple_of(half * BLOCK, BLOCK), BLOCK)
        copies.append(
            pltpu.make_async_copy(
                pieces[index], out_ref.at[:, source % 2, rows, :], sems.at[index]
            )
        )
    for copy in copies:
        copy.start()
    for copy in copies:
        copy.wait()


def call(kernel, shapes, *args, spaces=None, out_space=pltpu.VMEM, scratch=(), aliases=None, flops=0, mib=16):
    shapes = [shape if isinstance(shape, jax.ShapeDtypeStruct) else bf16(shape) for shape in shapes]
    spaces = spaces or [pltpu.VMEM] * len(args)
    cost = None
    if flops is not None:
        moved = sum(arg.size * arg.dtype.itemsize for arg in args)
        moved += sum(math.prod(shape.shape) * shape.dtype.itemsize for shape in shapes)
        cost = pl.CostEstimate(flops=flops, bytes_accessed=moved, transcendentals=0)
    results = pl.pallas_call(
        kernel,
        out_shape=shapes,
        in_specs=[pl.BlockSpec(memory_space=space) for space in spaces],
        out_specs=[pl.BlockSpec(memory_space=out_space)] * len(shapes),
        scratch_shapes=list(scratch),
        input_output_aliases=aliases or {},
        cost_estimate=cost,
        compiler_params=pltpu.CompilerParams(vmem_limit_bytes=mib * 1024 * 1024),
    )(*args)
    return results[0] if len(shapes) == 1 else results


def bf16(shape):
    return jax.ShapeDtypeStruct(shape, jnp.bfloat16)


def pair_z(value, first):
    moves = [(z, (z + (1 if (z % 2 == 1) == first else -1)) % NB) for z in range(NB)]
    return lax.ppermute(value, Z, moves)


def carry(value):
    moves = [(z, (z + 1) % NB) for z in range(NB)]
    moves += [(NB + z, NB + (z - 1) % NB) for z in range(NB)]
    return lax.ppermute(value, ("core",) + Z, moves)


def other_core(value):
    return lax.ppermute(value, "core", [(0, 1), (1, 0)])


def panel_moves(m):
    moves = []
    for core in range(2):
        for y in range(GROUP):
            if core == y // 2:
                target = (core, (y + m) % GROUP)
            else:
                target = (1 - core, (y + m + 2) % GROUP)
            moves.append((core * GROUP + y, target[0] * GROUP + target[1]))
    return moves


def partial_gram(diffs, single, pairs, values, offsets=None):
    count = 2 * len(diffs)
    shapes = [jax.ShapeDtypeStruct((count, HALF, HALF), jnp.float32), bf16((count, HALF, HALF))]
    spaces = [pltpu.VMEM] * len(values)
    if offsets is not None:
        shapes.append(jax.ShapeDtypeStruct((F, HALF), jnp.float32))
        values = (*values, offsets)
        spaces.append(pltpu.SMEM)
    return call(
        functools.partial(gram_kernel, diffs, single, pairs),
        shapes,
        *values,
        spaces=spaces,
        flops=count * 2 * BLOCK * BLOCK * KK,
    )


def on_device(records, offsets):
    outgoing = records.transpose(2, 0, 1, 3).reshape(F, REC_DEV, 2 * 64)
    arrived = lax.all_to_all(outgoing, ("x", "y"), 0, 0, tiled=True)
    here = call(pack_kernel, [(BLOCK, KK)], arrived)
    first = pair_z(here, True)
    second = pair_z(here, False)
    first2 = pair_z(second, True)
    second2 = pair_z(first, False)
    near, near_theirs, coefs = partial_gram(NEAR_DIFFS, (0,), (1,), (here, first, second), offsets)
    near_other = other_core(near_theirs)
    far, far_theirs = partial_gram(FAR_DIFFS, (), (1, 2), (first, second, first2, second2))
    far_other = other_core(far_theirs)
    strip = call(add_kernel, [(F, HALF, HALF)], near, near_other, far, far_other)
    bins = lax.all_to_all(strip, ("x", "y"), 0, 0, tiled=True)
    windowed = call(window_kernel, [(F, HALF, HALF)], coefs, bins)
    mine = lax.all_to_all(windowed, ("x", "y"), 0, 0, tiled=True)
    own = {}
    other = {}
    own[0], other[0] = mine, other_core(mine)
    pieces = {(0, True, True): own[0], (0, True, False): other[0]}
    for step in range(1, NB // 2 + 1):
        own[step] = carry(own[step - 1])
        pieces[(step, True, True)] = own[step]
        if step < NB // 2:
            other[step] = carry(other[step - 1])
            pieces[(step, True, False)] = other[step]
        pieces[(step, False, False)] = other_core(own[step])
        if step < NB // 2:
            pieces[(step, False, True)] = other_core(other[step])
    pieces = [pieces[key] for key in PIECES]
    whole_shape = (2, NB, F, HALF, HALF)
    whole, left = call(
        prepare_kernel,
        [whole_shape, (2 * BLOCK, S)],
        *pieces[:-2],
        spaces=[pl.ANY] * (NPIECES - 2),
        scratch=[pltpu.SemaphoreType.DMA((NPIECES - 2,))],
    )
    tile = (2, BLOCK, BLOCK)
    out_shape = (2, 2, 2 * BLOCK, BLOCK)
    joined = []
    for order in PANELS:
        first = order is PANELS[0]
        kernel = functools.partial(panels_kernel, order, first)
        shapes = [tile] * len(order)
        if first:
            whole, *panels = call(
                kernel,
                [whole_shape] + shapes,
                whole,
                left,
                *pieces[-2:],
                spaces=[pltpu.VMEM, pltpu.VMEM, pl.ANY, pl.ANY],
                scratch=[pltpu.SemaphoreType.DMA((2,))],
                aliases={0: 0},
                flops=None,
            )
        else:
            panels = call(kernel, shapes, left, whole, flops=None)
            panels = panels if len(order) > 1 else [panels]
        arrived = [
            lax.ppermute(value, ("core", "y"), panel_moves(m)) for m, value in zip(order, panels)
        ]
        joined = [
            call(
                functools.partial(join_kernel, order),
                [out_shape],
                *arrived,
                *joined,
                spaces=[pl.ANY] * (len(arrived) + len(joined)),
                out_space=pl.ANY,
                scratch=[pltpu.SemaphoreType.DMA((len(order),))],
                aliases={len(order): 0} if joined else None,
            )
        ]
    return joined[0]


def solution(mesh):
    fine = Mesh(mesh.devices.reshape(4, 2, 4, 2, 4), ("x", "core", "zh", "zl", "y"))
    return jax.shard_map(
        on_device,
        mesh=fine,
        in_specs=(P(("x", "core"), None, None, ("zh", "zl", "y")), P()),
        out_specs=P(None, ("x", "core"), "zh", ("zl", "y")),
        check_vma=False,
    )
```

```python
import functools
import math

import jax
import jax.numpy as jnp
import numpy as np
from jax import lax
from jax.experimental import pallas as pl
from jax.experimental.pallas import tpu as pltpu
from jax.sharding import Mesh, PartitionSpec as P

S = 2048
F = 16
RECORDS = 384
BLOCK = 256
HALF = 128
NOFF = 4
NB = 8
REC_DEV = 48
GROUP = 4
NK = GROUP * REC_DEV
KK = 2 * NK
NEAR_DIFFS = (0, 1, 7, 2, 6)
FAR_DIFFS = (3, 5, 4)
PANELS = ((2,), (0,), (1,), (3,))
Z = ("zh", "zl")


def lag_profile():
    lag = np.minimum(np.arange(F), F - np.arange(F))
    rows = []
    for offset in range(NOFF):
        inside = (lag >= offset + 2) & (lag < offset + 5)
        weights = np.where(inside, 1.0, 0.1)
        step = np.arange(F // 2 + 1)
        angles = 2.0 * np.pi * (step[:, None] * np.arange(F)[None, :] % F) / F
        rows.append(np.cos(angles) @ weights / F)
    return [[float(value) for value in row] for row in rows]


LAG_PROFILE = lag_profile()


def home_shift(diff):
    return jnp.where(diff <= 4, -(diff // 2), (9 - diff) // 2)


HOME = [0, 0, -1, -1, -2, 2, 1, 1]

PIECES = [(0, True, True), (0, True, False)]
for _step in range(1, NB // 2):
    PIECES += [
        (_step, True, True),
        (_step, True, False),
        (_step, False, False),
        (_step, False, True),
    ]
PIECES += [(NB // 2, True, True), (NB // 2, False, False)]
NPIECES = len(PIECES)


def pack_kernel(y_ref, out_ref):
    for part in range(GROUP):
        rows = jnp.concatenate([y_ref[line * GROUP + part] for line in range(GROUP)], axis=0)
        turned = rows.astype(jnp.float32).T.astype(jnp.bfloat16)
        both = jnp.concatenate([turned[:64], turned[64:]], axis=1)
        out_ref[part * 64 : (part + 1) * 64, :] = both


def write_coefs(offsets_ref, coefs_ref):
    piece = lax.axis_index("x") * GROUP + lax.axis_index("y")
    plane = lax.axis_index("zh") * 2 + lax.axis_index("zl")
    diff = piece // 2
    a = (plane + home_shift(diff) + NB) % NB
    b = (a + diff) % NB
    shift = (offsets_ref[a, b] + offsets_ref[b, a]) % NOFF
    for step in range(F // 2 + 1):
        value = jnp.float32(LAG_PROFILE[0][step])
        for offset in range(1, NOFF):
            value = jnp.where(shift == offset, jnp.float32(LAG_PROFILE[offset][step]), value)
        coefs_ref[step : step + 1, :] = jnp.full((1, HALF), value, jnp.float32)


def gram_kernel(diffs, single, pairs, *refs):
    count = len(single) + 2 * len(pairs)
    if len(refs) > count + 2:
        write_coefs(refs[count], refs[-1])
        refs = refs[:count] + refs[count + 1 : -1]
    first_core = lax.axis_index("core") == 0
    even = lax.axis_index("zl") == 0
    rights = {plane: refs[index][...] for index, plane in enumerate(single)}
    for index, plane in enumerate(pairs):
        second = refs[len(single) + 2 * index][...]
        first = refs[len(single) + 2 * index + 1][...]
        rights[-plane] = jnp.where(even, first, second)
        rights[plane] = jnp.where(even, second, first)
    mine_ref, theirs_ref = refs[count:]
    lane = lax.broadcasted_iota(jnp.int32, (BLOCK, KK), 1)
    sign = jnp.where(lane < NK, -1.0, 1.0).astype(jnp.float32)
    scale = jnp.float32(1.0 / math.sqrt(RECORDS))
    lefts = {}
    for plane in sorted({HOME[diff] for diff in diffs}):
        top = rights[plane]
        bottom = (pltpu.roll(top.astype(jnp.float32), NK, 1) * sign).astype(jnp.bfloat16)
        lefts[plane] = jnp.concatenate([top, bottom], axis=0)
    for index, diff in enumerate(diffs):
        a = HOME[diff]
        b = (a + diff + 3) % NB - 3
        both = lax.dot_general(
            lefts[a], rights[b], (((1,), (1,)), ((), ())), preferred_element_type=jnp.float32
        )
        tile = (both[:BLOCK] + both[BLOCK:]) * scale
        mine = jnp.where(first_core, tile[:HALF], tile[HALF:])
        theirs = jnp.where(first_core, tile[HALF:], tile[:HALF]).astype(jnp.bfloat16)
        for side in range(2):
            columns = slice(side * HALF, (side + 1) * HALF)
            mine_ref[2 * index + side] = mine[:, columns]
            theirs_ref[2 * index + side] = theirs[:, columns]


def add_kernel(near_ref, near_other_ref, far_ref, far_other_ref, out_ref):
    for diffs, mine_ref, other_ref in (
        (NEAR_DIFFS, near_ref, near_other_ref),
        (FAR_DIFFS, far_ref, far_other_ref),
    ):
        for index, diff in enumerate(diffs):
            for side in range(2):
                total = mine_ref[2 * index + side] + other_ref[2 * index + side].astype(jnp.float32)
                out_ref[2 * diff + side] = total.astype(jnp.bfloat16)


def window_kernel(coefs_ref, in_ref, out_ref):
    coefs = [coefs_ref[step : step + 1, :] for step in range(F // 2 + 1)]

    def chunk(index, carry):
        rows = pl.ds(pl.multiple_of(index * 16, 16), 16)
        data = [in_ref[g, rows, :].astype(jnp.float32) for g in range(F)]
        for f in range(F):
            total = coefs[0] * data[f] + coefs[F // 2] * data[(f + F // 2) % F]
            for step in range(1, F // 2):
                total = total + coefs[step] * (data[(f + step) % F] + data[(f - step) % F])
            out_ref[f, rows, :] = total.astype(jnp.bfloat16)
        return carry

    lax.fori_loop(0, HALF // 16, chunk, 0)


def place():
    core = lax.axis_index("core")
    zh = lax.axis_index("zh")
    zl = lax.axis_index("zl")
    return core, 2 * zh + zl, 2 * zh + core, 4 * zl


def copy_in(entry, piece_ref, g_ref, sem):
    step, carried, own = entry
    core, here, _, _ = place()
    away = jnp.where(core == 0, -1, 1)
    plane = (here + (away if carried else -away) * step + NB) % NB
    half = core if own else 1 - core
    return pltpu.make_async_copy(piece_ref, g_ref.at[half, plane], sem)


def read_block(g_ref, a, diff):
    plane = (a - home_shift(diff) + NB) % NB
    halves = [
        jnp.concatenate([g_ref[h, plane, 2 * diff], g_ref[h, plane, 2 * diff + 1]], axis=1)
        for h in range(2)
    ]
    return jnp.concatenate(halves, axis=0)


def prepare_kernel(*refs):
    pieces = refs[: NPIECES - 2]
    g_ref, left_ref, sems = refs[NPIECES - 2 :]
    _, _, i, _ = place()
    copies = []
    for index, piece_ref in enumerate(pieces):
        copy = copy_in(PIECES[index], piece_ref, g_ref, sems.at[index])
        copy.start()
        copies.append(copy)
    for copy in copies:
        copy.wait()
    for step in range(NB):
        columns = pl.ds(step * BLOCK, BLOCK)
        left_ref[:BLOCK, columns] = read_block(g_ref, i, jnp.int32(step))
        k = (i + step) % NB
        across = read_block(g_ref, k, jnp.int32((NB - step) % NB))
        left_ref[BLOCK:, columns] = across.astype(jnp.float32).T.astype(jnp.bfloat16)


def panel(m, g_ref, left_ref, out_ref):
    core, _, i, first = place()
    y = lax.axis_index("y")
    aside = jnp.where(core == y // 2, 0, 2)
    j = first + (y + m + aside) % GROUP
    downs = []
    acrosses = []
    for step in range(NB):
        k = (i + step) % NB
        downs.append(read_block(g_ref, k, (j - k + NB) % NB))
        acrosses.append(read_block(g_ref, j, (k - j + NB) % NB))
    down = jnp.concatenate(downs, axis=0)
    across = jnp.concatenate(acrosses, axis=1)
    first = jnp.dot(left_ref[...], down, preferred_element_type=jnp.float32)
    second = lax.dot_general(
        left_ref[...], across, (((1,), (1,)), ((), ())), preferred_element_type=jnp.float32
    )
    scale = jnp.float32(0.5 / math.sqrt(S))
    out_ref[0] = ((second[:BLOCK] + first[BLOCK:]) * scale).astype(jnp.bfloat16)
    out_ref[1] = ((first[:BLOCK] - second[BLOCK:]) * scale).astype(jnp.bfloat16)


def panels_kernel(order, first, *refs):
    if first:
        left_ref, last_ref, last_swap_ref, g_ref = refs[1:5]
        out_refs = refs[5:-1]
        sems = refs[-1]
        copies = [
            copy_in(PIECES[-2], last_ref, g_ref, sems.at[0]),
            copy_in(PIECES[-1], last_swap_ref, g_ref, sems.at[1]),
        ]
        for copy in copies:
            copy.start()
        for copy in copies:
            copy.wait()
    else:
        left_ref, g_ref = refs[:2]
        out_refs = refs[2:]
    for m, out_ref in zip(order, out_refs):
        panel(m, g_ref, left_ref, out_ref)


def join_kernel(moved, *refs):
    pieces = refs[: len(moved)]
    out_ref, sems = refs[-2:]
    core = lax.axis_index("core")
    y = lax.axis_index("y")
    copies = []
    for index, m in enumerate(moved):
        source = (y - m + GROUP) % GROUP
        half = jnp.where(source // 2 == core, core, 1 - core)
        rows = pl.ds(pl.multiple_of(half * BLOCK, BLOCK), BLOCK)
        copies.append(
            pltpu.make_async_copy(
                pieces[index], out_ref.at[:, source % 2, rows, :], sems.at[index]
            )
        )
    for copy in copies:
        copy.start()
    for copy in copies:
        copy.wait()


def call(kernel, shapes, *args, spaces=None, out_space=pltpu.VMEM, scratch=(), aliases=None, flops=0, mib=16):
    shapes = [shape if isinstance(shape, jax.ShapeDtypeStruct) else bf16(shape) for shape in shapes]
    spaces = spaces or [pltpu.VMEM] * len(args)
    cost = None
    if flops is not None:
        moved = sum(arg.size * arg.dtype.itemsize for arg in args)
        moved += sum(math.prod(shape.shape) * shape.dtype.itemsize for shape in shapes)
        cost = pl.CostEstimate(flops=flops, bytes_accessed=moved, transcendentals=0)
    results = pl.pallas_call(
        kernel,
        out_shape=shapes,
        in_specs=[pl.BlockSpec(memory_space=space) for space in spaces],
        out_specs=[pl.BlockSpec(memory_space=out_space)] * len(shapes),
        scratch_shapes=list(scratch),
        input_output_aliases=aliases or {},
        cost_estimate=cost,
        compiler_params=pltpu.CompilerParams(vmem_limit_bytes=mib * 1024 * 1024),
    )(*args)
    return results[0] if len(shapes) == 1 else results


def bf16(shape):
    return jax.ShapeDtypeStruct(shape, jnp.bfloat16)


def pair_z(value, first):
    moves = [(z, (z + (1 if (z % 2 == 1) == first else -1)) % NB) for z in range(NB)]
    return lax.ppermute(value, Z, moves)


def carry(value):
    moves = [(z, (z + 1) % NB) for z in range(NB)]
    moves += [(NB + z, NB + (z - 1) % NB) for z in range(NB)]
    return lax.ppermute(value, ("core",) + Z, moves)


def other_core(value):
    return lax.ppermute(value, "core", [(0, 1), (1, 0)])


def panel_moves(m):
    moves = []
    for core in range(2):
        for y in range(GROUP):
            if core == y // 2:
                target = (core, (y + m) % GROUP)
            else:
                target = (1 - core, (y + m + 2) % GROUP)
            moves.append((core * GROUP + y, target[0] * GROUP + target[1]))
    return moves


def partial_gram(diffs, single, pairs, values, offsets=None):
    count = 2 * len(diffs)
    shapes = [jax.ShapeDtypeStruct((count, HALF, HALF), jnp.float32), bf16((count, HALF, HALF))]
    spaces = [pltpu.VMEM] * len(values)
    if offsets is not None:
        shapes.append(jax.ShapeDtypeStruct((F, HALF), jnp.float32))
        values = (*values, offsets)
        spaces.append(pltpu.SMEM)
    return call(
        functools.partial(gram_kernel, diffs, single, pairs),
        shapes,
        *values,
        spaces=spaces,
        flops=count * 2 * BLOCK * BLOCK * KK,
    )


def on_device(records, offsets):
    outgoing = records.transpose(2, 0, 1, 3).reshape(F, REC_DEV, 2 * 64)
    arrived = lax.all_to_all(outgoing, ("x", "y"), 0, 0, tiled=True)
    here = call(pack_kernel, [(BLOCK, KK)], arrived)
    second = pair_z(here, False)
    first = pair_z(here, True)
    second2 = pair_z(first, False)
    first2 = pair_z(second, True)
    near, near_theirs, coefs = partial_gram(NEAR_DIFFS, (0,), (1,), (here, second, first), offsets)
    near_other = other_core(near_theirs)
    far, far_theirs = partial_gram(FAR_DIFFS, (), (1, 2), (second, first, second2, first2))
    far_other = other_core(far_theirs)
    strip = call(add_kernel, [(F, HALF, HALF)], near, near_other, far, far_other)
    bins = lax.all_to_all(strip, ("x", "y"), 0, 0, tiled=True)
    windowed = call(window_kernel, [(F, HALF, HALF)], coefs, bins)
    mine = lax.all_to_all(windowed, ("x", "y"), 0, 0, tiled=True)
    own = {}
    other = {}
    own[0], other[0] = mine, other_core(mine)
    pieces = {(0, True, True): own[0], (0, True, False): other[0]}
    for step in range(1, NB // 2 + 1):
        own[step] = carry(own[step - 1])
        pieces[(step, True, True)] = own[step]
        if step < NB // 2:
            other[step] = carry(other[step - 1])
            pieces[(step, True, False)] = other[step]
        pieces[(step, False, False)] = other_core(own[step])
        if step < NB // 2:
            pieces[(step, False, True)] = other_core(other[step])
    pieces = [pieces[key] for key in PIECES]
    whole_shape = (2, NB, F, HALF, HALF)
    whole, left = call(
        prepare_kernel,
        [whole_shape, (2 * BLOCK, S)],
        *pieces[:-2],
        spaces=[pl.ANY] * (NPIECES - 2),
        scratch=[pltpu.SemaphoreType.DMA((NPIECES - 2,))],
    )
    tile = (2, BLOCK, BLOCK)
    out_shape = (2, 2, 2 * BLOCK, BLOCK)
    joined = []
    for order in PANELS:
        first = order is PANELS[0]
        kernel = functools.partial(panels_kernel, order, first)
        shapes = [tile] * len(order)
        if first:
            whole, *panels = call(
                kernel,
                [whole_shape] + shapes,
                whole,
                left,
                *pieces[-2:],
                spaces=[pltpu.VMEM, pltpu.VMEM, pl.ANY, pl.ANY],
                scratch=[pltpu.SemaphoreType.DMA((2,))],
                aliases={0: 0},
                flops=None,
            )
        else:
            panels = call(kernel, shapes, left, whole, flops=None)
            panels = panels if len(order) > 1 else [panels]
        arrived = [
            lax.ppermute(value, ("core", "y"), panel_moves(m)) for m, value in zip(order, panels)
        ]
        joined = [
            call(
                functools.partial(join_kernel, order),
                [out_shape],
                *arrived,
                *joined,
                spaces=[pl.ANY] * (len(arrived) + len(joined)),
                out_space=pl.ANY,
                scratch=[pltpu.SemaphoreType.DMA((len(order),))],
                aliases={len(order): 0} if joined else None,
            )
        ]
    return joined[0]


def solution(mesh):
    fine = Mesh(mesh.devices.reshape(4, 2, 4, 2, 4), ("x", "core", "zh", "zl", "y"))
    return jax.shard_map(
        on_device,
        mesh=fine,
        in_specs=(P(("x", "core"), None, None, ("zh", "zl", "y")), P()),
        out_specs=P(None, ("x", "core"), "zh", ("zl", "y")),
        check_vma=False,
    )
```

```python
import functools
import math

import jax
import jax.numpy as jnp
import numpy as np
from jax import lax
from jax.experimental import pallas as pl
from jax.experimental.pallas import tpu as pltpu
from jax.sharding import Mesh, PartitionSpec as P

S = 2048
F = 16
RECORDS = 384
BLOCK = 256
HALF = 128
NOFF = 4
NB = 8
REC_DEV = 48
GROUP = 4
NK = GROUP * REC_DEV
KK = 2 * NK
NEAR_DIFFS = (0, 1, 7, 2, 6)
FAR_DIFFS = (3, 5, 4)
PANELS = ((2,), (0,), (1,), (3,))
Z = ("zh", "zl")


def lag_profile():
    lag = np.minimum(np.arange(F), F - np.arange(F))
    rows = []
    for offset in range(NOFF):
        inside = (lag >= offset + 2) & (lag < offset + 5)
        weights = np.where(inside, 1.0, 0.1)
        step = np.arange(F // 2 + 1)
        angles = 2.0 * np.pi * (step[:, None] * np.arange(F)[None, :] % F) / F
        rows.append(np.cos(angles) @ weights / F)
    return [[float(value) for value in row] for row in rows]


LAG_PROFILE = lag_profile()


def home_shift(diff):
    return jnp.where(diff <= 4, -(diff // 2), (9 - diff) // 2)


HOME = [0, 0, -1, -1, -2, 2, 1, 1]

PIECES = [(0, True, True), (0, True, False)]
for _step in range(1, NB // 2):
    PIECES += [
        (_step, True, True),
        (_step, True, False),
        (_step, False, False),
        (_step, False, True),
    ]
PIECES += [(NB // 2, True, True), (NB // 2, False, False)]
NPIECES = len(PIECES)


def pack_kernel(y_ref, out_ref):
    for part in range(GROUP):
        rows = jnp.concatenate([y_ref[line * GROUP + part] for line in range(GROUP)], axis=0)
        turned = rows.astype(jnp.float32).T.astype(jnp.bfloat16)
        both = jnp.concatenate([turned[:64], turned[64:]], axis=1)
        out_ref[part * 64 : (part + 1) * 64, :] = both


def write_coefs(offsets_ref, coefs_ref):
    piece = lax.axis_index("x") * GROUP + lax.axis_index("y")
    plane = lax.axis_index("zh") * 2 + lax.axis_index("zl")
    diff = piece // 2
    a = (plane + home_shift(diff) + NB) % NB
    b = (a + diff) % NB
    shift = (offsets_ref[a, b] + offsets_ref[b, a]) % NOFF
    for step in range(F // 2 + 1):
        value = jnp.float32(LAG_PROFILE[0][step])
        for offset in range(1, NOFF):
            value = jnp.where(shift == offset, jnp.float32(LAG_PROFILE[offset][step]), value)
        coefs_ref[step : step + 1, :] = jnp.full((1, HALF), value, jnp.float32)


def gram_kernel(diffs, single, pairs, *refs):
    count = len(single) + 2 * len(pairs)
    if len(refs) > count + 2:
        write_coefs(refs[count], refs[-1])
        refs = refs[:count] + refs[count + 1 : -1]
    first_core = lax.axis_index("core") == 0
    even = lax.axis_index("zl") == 0
    rights = {plane: refs[index][...] for index, plane in enumerate(single)}
    for index, plane in enumerate(pairs):
        first = refs[len(single) + 2 * index][...]
        second = refs[len(single) + 2 * index + 1][...]
        rights[-plane] = jnp.where(even, first, second)
        rights[plane] = jnp.where(even, second, first)
    mine_ref, theirs_ref = refs[count:]
    lane = lax.broadcasted_iota(jnp.int32, (BLOCK, KK), 1)
    sign = jnp.where(lane < NK, -1.0, 1.0).astype(jnp.float32)
    scale = jnp.float32(1.0 / math.sqrt(RECORDS))
    lefts = {}
    for plane in sorted({HOME[diff] for diff in diffs}):
        top = rights[plane]
        bottom = (pltpu.roll(top.astype(jnp.float32), NK, 1) * sign).astype(jnp.bfloat16)
        lefts[plane] = jnp.concatenate([top, bottom], axis=0)
    for index, diff in enumerate(diffs):
        a = HOME[diff]
        b = (a + diff + 3) % NB - 3
        both = lax.dot_general(
            lefts[a], rights[b], (((1,), (1,)), ((), ())), preferred_element_type=jnp.float32
        )
        tile = (both[:BLOCK] + both[BLOCK:]) * scale
        mine = jnp.where(first_core, tile[:HALF], tile[HALF:])
        theirs = jnp.where(first_core, tile[HALF:], tile[:HALF]).astype(jnp.bfloat16)
        for side in range(2):
            columns = slice(side * HALF, (side + 1) * HALF)
            mine_ref[2 * index + side] = mine[:, columns]
            theirs_ref[2 * index + side] = theirs[:, columns]


def add_kernel(near_ref, near_other_ref, far_ref, far_other_ref, out_ref):
    for diffs, mine_ref, other_ref in (
        (NEAR_DIFFS, near_ref, near_other_ref),
        (FAR_DIFFS, far_ref, far_other_ref),
    ):
        for index, diff in enumerate(diffs):
            for side in range(2):
                total = mine_ref[2 * index + side] + other_ref[2 * index + side].astype(jnp.float32)
                out_ref[2 * diff + side] = total.astype(jnp.bfloat16)


def window_kernel(coefs_ref, in_ref, out_ref):
    coefs = [coefs_ref[step : step + 1, :] for step in range(F // 2 + 1)]

    def chunk(index, carry):
        rows = pl.ds(pl.multiple_of(index * 16, 16), 16)
        data = [in_ref[g, rows, :].astype(jnp.float32) for g in range(F)]
        for f in range(F):
            total = coefs[0] * data[f] + coefs[F // 2] * data[(f + F // 2) % F]
            for step in range(1, F // 2):
                total = total + coefs[step] * (data[(f + step) % F] + data[(f - step) % F])
            out_ref[f, rows, :] = total.astype(jnp.bfloat16)
        return carry

    lax.fori_loop(0, HALF // 16, chunk, 0)


def place():
    core = lax.axis_index("core")
    zh = lax.axis_index("zh")
    zl = lax.axis_index("zl")
    return core, 2 * zh + zl, 2 * zh + core, 4 * zl


def copy_in(entry, piece_ref, g_ref, sem):
    step, carried, own = entry
    core, here, _, _ = place()
    away = jnp.where(core == 0, -1, 1)
    plane = (here + (away if carried else -away) * step + NB) % NB
    half = core if own else 1 - core
    return pltpu.make_async_copy(piece_ref, g_ref.at[half, plane], sem)


def read_block(g_ref, a, diff):
    plane = (a - home_shift(diff) + NB) % NB
    halves = [
        jnp.concatenate([g_ref[h, plane, 2 * diff], g_ref[h, plane, 2 * diff + 1]], axis=1)
        for h in range(2)
    ]
    return jnp.concatenate(halves, axis=0)


def prepare_kernel(*refs):
    pieces = refs[: NPIECES - 2]
    g_ref, left_ref, sems = refs[NPIECES - 2 :]
    _, _, i, _ = place()
    copies = []
    for index, piece_ref in enumerate(pieces):
        copy = copy_in(PIECES[index], piece_ref, g_ref, sems.at[index])
        copy.start()
        copies.append(copy)
    for copy in copies:
        copy.wait()
    for step in range(NB):
        columns = pl.ds(step * BLOCK, BLOCK)
        left_ref[:BLOCK, columns] = read_block(g_ref, i, jnp.int32(step))
        k = (i + step) % NB
        across = read_block(g_ref, k, jnp.int32((NB - step) % NB))
        left_ref[BLOCK:, columns] = across.astype(jnp.float32).T.astype(jnp.bfloat16)


def panel(m, g_ref, left_ref, out_ref):
    core, _, i, first = place()
    y = lax.axis_index("y")
    aside = jnp.where(core == y // 2, 0, 2)
    j = first + jnp.bitwise_xor(y, jnp.bitwise_xor(m, aside))
    downs = []
    acrosses = []
    for step in range(NB):
        k = (i + step) % NB
        downs.append(read_block(g_ref, k, (j - k + NB) % NB))
        acrosses.append(read_block(g_ref, j, (k - j + NB) % NB))
    down = jnp.concatenate(downs, axis=0)
    across = jnp.concatenate(acrosses, axis=1)
    first = jnp.dot(left_ref[...], down, preferred_element_type=jnp.float32)
    second = lax.dot_general(
        left_ref[...], across, (((1,), (1,)), ((), ())), preferred_element_type=jnp.float32
    )
    scale = jnp.float32(0.5 / math.sqrt(S))
    out_ref[0] = ((second[:BLOCK] + first[BLOCK:]) * scale).astype(jnp.bfloat16)
    out_ref[1] = ((first[:BLOCK] - second[BLOCK:]) * scale).astype(jnp.bfloat16)


def panels_kernel(order, first, *refs):
    if first:
        left_ref, last_ref, last_swap_ref, g_ref = refs[1:5]
        out_refs = refs[5:-1]
        sems = refs[-1]
        copies = [
            copy_in(PIECES[-2], last_ref, g_ref, sems.at[0]),
            copy_in(PIECES[-1], last_swap_ref, g_ref, sems.at[1]),
        ]
        for copy in copies:
            copy.start()
        for copy in copies:
            copy.wait()
    else:
        left_ref, g_ref = refs[:2]
        out_refs = refs[2:]
    for m, out_ref in zip(order, out_refs):
        panel(m, g_ref, left_ref, out_ref)


def join_kernel(moved, *refs):
    pieces = refs[: len(moved)]
    out_ref, sems = refs[-2:]
    core = lax.axis_index("core")
    y = lax.axis_index("y")
    copies = []
    for index, m in enumerate(moved):
        source = jnp.bitwise_xor(y, m)
        half = jnp.where(source // 2 == core, core, 1 - core)
        rows = pl.ds(pl.multiple_of(half * BLOCK, BLOCK), BLOCK)
        copies.append(
            pltpu.make_async_copy(
                pieces[index], out_ref.at[:, source % 2, rows, :], sems.at[index]
            )
        )
    for copy in copies:
        copy.start()
    for copy in copies:
        copy.wait()


def call(kernel, shapes, *args, spaces=None, out_space=pltpu.VMEM, scratch=(), aliases=None, flops=0, mib=16):
    shapes = [shape if isinstance(shape, jax.ShapeDtypeStruct) else bf16(shape) for shape in shapes]
    spaces = spaces or [pltpu.VMEM] * len(args)
    cost = None
    if flops is not None:
        moved = sum(arg.size * arg.dtype.itemsize for arg in args)
        moved += sum(math.prod(shape.shape) * shape.dtype.itemsize for shape in shapes)
        cost = pl.CostEstimate(flops=flops, bytes_accessed=moved, transcendentals=0)
    results = pl.pallas_call(
        kernel,
        out_shape=shapes,
        in_specs=[pl.BlockSpec(memory_space=space) for space in spaces],
        out_specs=[pl.BlockSpec(memory_space=out_space)] * len(shapes),
        scratch_shapes=list(scratch),
        input_output_aliases=aliases or {},
        cost_estimate=cost,
        compiler_params=pltpu.CompilerParams(vmem_limit_bytes=mib * 1024 * 1024),
    )(*args)
    return results[0] if len(shapes) == 1 else results


def bf16(shape):
    return jax.ShapeDtypeStruct(shape, jnp.bfloat16)


def pair_z(value, first):
    moves = [(z, (z + (1 if (z % 2 == 1) == first else -1)) % NB) for z in range(NB)]
    return lax.ppermute(value, Z, moves)


def carry(value):
    moves = [(z, (z + 1) % NB) for z in range(NB)]
    moves += [(NB + z, NB + (z - 1) % NB) for z in range(NB)]
    return lax.ppermute(value, ("core",) + Z, moves)


def other_core(value):
    return lax.ppermute(value, "core", [(0, 1), (1, 0)])


def panel_moves(m):
    moves = []
    for core in range(2):
        for y in range(GROUP):
            if core == y // 2:
                target = (core, y ^ m)
            else:
                target = (1 - core, y ^ m ^ 2)
            moves.append((core * GROUP + y, target[0] * GROUP + target[1]))
    return moves


def partial_gram(diffs, single, pairs, values, offsets=None):
    count = 2 * len(diffs)
    shapes = [jax.ShapeDtypeStruct((count, HALF, HALF), jnp.float32), bf16((count, HALF, HALF))]
    spaces = [pltpu.VMEM] * len(values)
    if offsets is not None:
        shapes.append(jax.ShapeDtypeStruct((F, HALF), jnp.float32))
        values = (*values, offsets)
        spaces.append(pltpu.SMEM)
    return call(
        functools.partial(gram_kernel, diffs, single, pairs),
        shapes,
        *values,
        spaces=spaces,
        flops=count * 2 * BLOCK * BLOCK * KK,
    )


def on_device(records, offsets):
    outgoing = records.transpose(2, 0, 1, 3).reshape(F, REC_DEV, 2 * 64)
    arrived = lax.all_to_all(outgoing, ("x", "y"), 0, 0, tiled=True)
    here = call(pack_kernel, [(BLOCK, KK)], arrived)
    first = pair_z(here, True)
    second = pair_z(here, False)
    first2 = pair_z(second, True)
    second2 = pair_z(first, False)
    near, near_theirs, coefs = partial_gram(NEAR_DIFFS, (0,), (1,), (here, first, second), offsets)
    near_other = other_core(near_theirs)
    far, far_theirs = partial_gram(FAR_DIFFS, (), (1, 2), (first, second, first2, second2))
    far_other = other_core(far_theirs)
    strip = call(add_kernel, [(F, HALF, HALF)], near, near_other, far, far_other)
    bins = lax.all_to_all(strip, ("x", "y"), 0, 0, tiled=True)
    windowed = call(window_kernel, [(F, HALF, HALF)], coefs, bins)
    mine = lax.all_to_all(windowed, ("x", "y"), 0, 0, tiled=True)
    own = {}
    other = {}
    own[0], other[0] = mine, other_core(mine)
    pieces = {(0, True, True): own[0], (0, True, False): other[0]}
    for step in range(1, NB // 2 + 1):
        own[step] = carry(own[step - 1])
        pieces[(step, True, True)] = own[step]
        if step < NB // 2:
            other[step] = carry(other[step - 1])
            pieces[(step, True, False)] = other[step]
        pieces[(step, False, False)] = other_core(own[step])
        if step < NB // 2:
            pieces[(step, False, True)] = other_core(other[step])
    pieces = [pieces[key] for key in PIECES]
    whole_shape = (2, NB, F, HALF, HALF)
    whole, left = call(
        prepare_kernel,
        [whole_shape, (2 * BLOCK, S)],
        *pieces[:-2],
        spaces=[pl.ANY] * (NPIECES - 2),
        scratch=[pltpu.SemaphoreType.DMA((NPIECES - 2,))],
    )
    tile = (2, BLOCK, BLOCK)
    out_shape = (2, 2, 2 * BLOCK, BLOCK)
    joined = []
    for order in PANELS:
        first = order is PANELS[0]
        kernel = functools.partial(panels_kernel, order, first)
        shapes = [tile] * len(order)
        if first:
            whole, *panels = call(
                kernel,
                [whole_shape] + shapes,
                whole,
                left,
                *pieces[-2:],
                spaces=[pltpu.VMEM, pltpu.VMEM, pl.ANY, pl.ANY],
                scratch=[pltpu.SemaphoreType.DMA((2,))],
                aliases={0: 0},
                flops=None,
            )
        else:
            panels = call(kernel, shapes, left, whole, flops=None)
            panels = panels if len(order) > 1 else [panels]
        arrived = [
            lax.ppermute(value, ("core", "y"), panel_moves(m)) for m, value in zip(order, panels)
        ]
        joined = [
            call(
                functools.partial(join_kernel, order),
                [out_shape],
                *arrived,
                *joined,
                spaces=[pl.ANY] * (len(arrived) + len(joined)),
                out_space=pl.ANY,
                scratch=[pltpu.SemaphoreType.DMA((len(order),))],
                aliases={len(order): 0} if joined else None,
            )
        ]
    return joined[0]


def solution(mesh):
    fine = Mesh(mesh.devices.reshape(4, 2, 4, 2, 4), ("x", "core", "zh", "zl", "y"))
    return jax.shard_map(
        on_device,
        mesh=fine,
        in_specs=(P(("x", "core"), None, None, ("zh", "zl", "y")), P()),
        out_specs=P(None, ("x", "core"), "zh", ("zl", "y")),
        check_vma=False,
    )
```

```python
import functools
import math

import jax
import jax.numpy as jnp
import numpy as np
from jax import lax
from jax.experimental import pallas as pl
from jax.experimental.pallas import tpu as pltpu
from jax.sharding import Mesh, PartitionSpec as P

S = 2048
F = 16
RECORDS = 384
BLOCK = 256
HALF = 128
NOFF = 4
NB = 8
REC_DEV = 48
GROUP = 4
NK = GROUP * REC_DEV
KK = 2 * NK
NEAR_DIFFS = (0, 1, 7, 2, 6)
FAR_DIFFS = (3, 5, 4)
PANELS = (2, 1, 3, 0)
Z = ("zh", "zl")


def lag_profile():
    lag = np.minimum(np.arange(F), F - np.arange(F))
    rows = []
    for offset in range(NOFF):
        inside = (lag >= offset + 2) & (lag < offset + 5)
        weights = np.where(inside, 1.0, 0.1)
        step = np.arange(F // 2 + 1)
        angles = 2.0 * np.pi * (step[:, None] * np.arange(F)[None, :] % F) / F
        rows.append(np.cos(angles) @ weights / F)
    return [[float(value) for value in row] for row in rows]


LAG_PROFILE = lag_profile()


def home_shift(diff):
    return jnp.where(diff <= 4, -(diff // 2), (9 - diff) // 2)


HOME = [0, 0, -1, -1, -2, 2, 1, 1]

PIECES = [(0, True, True), (0, True, False)]
for _step in range(1, NB // 2):
    PIECES += [
        (_step, True, True),
        (_step, True, False),
        (_step, False, False),
        (_step, False, True),
    ]
PIECES += [(NB // 2, True, True), (NB // 2, False, False)]
NPIECES = len(PIECES)


def pack_kernel(y_ref, out_ref):
    for part in range(GROUP):
        rows = jnp.concatenate([y_ref[line * GROUP + part] for line in range(GROUP)], axis=0)
        turned = rows.astype(jnp.float32).T.astype(jnp.bfloat16)
        both = jnp.concatenate([turned[:64], turned[64:]], axis=1)
        out_ref[part * 64 : (part + 1) * 64, :] = both


def write_coefs(offsets_ref, coefs_ref):
    piece = lax.axis_index("x") * GROUP + lax.axis_index("y")
    plane = lax.axis_index("zh") * 2 + lax.axis_index("zl")
    diff = piece // 2
    a = (plane + home_shift(diff) + NB) % NB
    b = (a + diff) % NB
    shift = (offsets_ref[a, b] + offsets_ref[b, a]) % NOFF
    for step in range(F // 2 + 1):
        value = jnp.float32(LAG_PROFILE[0][step])
        for offset in range(1, NOFF):
            value = jnp.where(shift == offset, jnp.float32(LAG_PROFILE[offset][step]), value)
        coefs_ref[step : step + 1, :] = jnp.full((1, HALF), value, jnp.float32)


def gram_kernel(diffs, single, pairs, *refs):
    count = len(single) + 2 * len(pairs)
    if len(refs) > count + 2:
        write_coefs(refs[count], refs[-1])
        refs = refs[:count] + refs[count + 1 : -1]
    first_core = lax.axis_index("core") == 0
    even = lax.axis_index("zl") == 0
    rights = {plane: refs[index][...] for index, plane in enumerate(single)}
    for index, plane in enumerate(pairs):
        first = refs[len(single) + 2 * index][...]
        second = refs[len(single) + 2 * index + 1][...]
        rights[-plane] = jnp.where(even, first, second)
        rights[plane] = jnp.where(even, second, first)
    mine_ref, theirs_ref = refs[count:]
    lane = lax.broadcasted_iota(jnp.int32, (BLOCK, KK), 1)
    sign = jnp.where(lane < NK, -1.0, 1.0).astype(jnp.float32)
    scale = jnp.float32(1.0 / math.sqrt(RECORDS))
    lefts = {}
    for plane in sorted({HOME[diff] for diff in diffs}):
        top = rights[plane]
        bottom = (pltpu.roll(top.astype(jnp.float32), NK, 1) * sign).astype(jnp.bfloat16)
        lefts[plane] = jnp.concatenate([top, bottom], axis=0)
    for index, diff in enumerate(diffs):
        a = HOME[diff]
        b = (a + diff + 3) % NB - 3
        both = lax.dot_general(
            lefts[a], rights[b], (((1,), (1,)), ((), ())), preferred_element_type=jnp.float32
        )
        tile = (both[:BLOCK] + both[BLOCK:]) * scale
        mine = jnp.where(first_core, tile[:HALF], tile[HALF:])
        theirs = jnp.where(first_core, tile[HALF:], tile[:HALF]).astype(jnp.bfloat16)
        for side in range(2):
            columns = slice(side * HALF, (side + 1) * HALF)
            mine_ref[2 * index + side] = mine[:, columns]
            theirs_ref[2 * index + side] = theirs[:, columns]


def add_kernel(near_ref, near_other_ref, far_ref, far_other_ref, out_ref):
    for diffs, mine_ref, other_ref in (
        (NEAR_DIFFS, near_ref, near_other_ref),
        (FAR_DIFFS, far_ref, far_other_ref),
    ):
        for index, diff in enumerate(diffs):
            for side in range(2):
                total = mine_ref[2 * index + side] + other_ref[2 * index + side].astype(jnp.float32)
                out_ref[2 * diff + side] = total.astype(jnp.bfloat16)


def window_kernel(coefs_ref, in_ref, out_ref):
    coefs = [coefs_ref[step : step + 1, :] for step in range(F // 2 + 1)]

    def chunk(index, carry):
        rows = pl.ds(pl.multiple_of(index * 16, 16), 16)
        data = [in_ref[g, rows, :].astype(jnp.float32) for g in range(F)]
        for f in range(F):
            total = coefs[0] * data[f] + coefs[F // 2] * data[(f + F // 2) % F]
            for step in range(1, F // 2):
                total = total + coefs[step] * (data[(f + step) % F] + data[(f - step) % F])
            out_ref[f, rows, :] = total.astype(jnp.bfloat16)
        return carry

    lax.fori_loop(0, HALF // 16, chunk, 0)


def place():
    core = lax.axis_index("core")
    zh = lax.axis_index("zh")
    zl = lax.axis_index("zl")
    return core, 2 * zh + zl, 2 * zh + core, 4 * zl


def copy_in(entry, piece_ref, g_ref, sem):
    step, carried, own = entry
    core, here, _, _ = place()
    away = jnp.where(core == 0, -1, 1)
    plane = (here + (away if carried else -away) * step + NB) % NB
    half = core if own else 1 - core
    return pltpu.make_async_copy(piece_ref, g_ref.at[half, plane], sem)


def read_block(g_ref, a, diff):
    plane = (a - home_shift(diff) + NB) % NB
    halves = [
        jnp.concatenate([g_ref[h, plane, 2 * diff], g_ref[h, plane, 2 * diff + 1]], axis=1)
        for h in range(2)
    ]
    return jnp.concatenate(halves, axis=0)


def prepare_kernel(*refs):
    pieces = refs[: NPIECES - 2]
    g_ref, left_ref, sems = refs[NPIECES - 2 :]
    _, _, i, _ = place()
    copies = []
    for index, piece_ref in enumerate(pieces):
        copy = copy_in(PIECES[index], piece_ref, g_ref, sems.at[index])
        copy.start()
        copies.append(copy)
    for copy in copies:
        copy.wait()
    for step in range(NB):
        columns = pl.ds(step * BLOCK, BLOCK)
        left_ref[:BLOCK, columns] = read_block(g_ref, i, jnp.int32(step))
        k = (i + step) % NB
        across = read_block(g_ref, k, jnp.int32((NB - step) % NB))
        left_ref[BLOCK:, columns] = across.astype(jnp.float32).T.astype(jnp.bfloat16)


def panel(m, g_ref, left_ref, out_ref):
    core, _, i, first = place()
    y = lax.axis_index("y")
    aside = jnp.where(core == y // 2, 0, 2) if m % 2 == 1 else 0
    j = first + jnp.bitwise_xor(y, jnp.bitwise_xor(m, aside))
    downs = []
    acrosses = []
    for step in range(NB):
        k = (i + step) % NB
        downs.append(read_block(g_ref, k, (j - k + NB) % NB))
        acrosses.append(read_block(g_ref, j, (k - j + NB) % NB))
    down = jnp.concatenate(downs, axis=0)
    across = jnp.concatenate(acrosses, axis=1)
    first = jnp.dot(left_ref[...], down, preferred_element_type=jnp.float32)
    second = lax.dot_general(
        left_ref[...], across, (((1,), (1,)), ((), ())), preferred_element_type=jnp.float32
    )
    scale = jnp.float32(0.5 / math.sqrt(S))
    out_ref[0] = ((second[:BLOCK] + first[BLOCK:]) * scale).astype(jnp.bfloat16)
    out_ref[1] = ((first[:BLOCK] - second[BLOCK:]) * scale).astype(jnp.bfloat16)


def first_panel_kernel(old_ref, left_ref, last_ref, last_swap_ref, g_ref, out_ref, sems):
    del old_ref
    copies = [
        copy_in(PIECES[-2], last_ref, g_ref, sems.at[0]),
        copy_in(PIECES[-1], last_swap_ref, g_ref, sems.at[1]),
    ]
    for copy in copies:
        copy.start()
    for copy in copies:
        copy.wait()
    panel(PANELS[0], g_ref, left_ref, out_ref)


def panels_kernel(left_ref, g_ref, *out_refs):
    for m, out_ref in zip(PANELS[1:], out_refs):
        panel(m, g_ref, left_ref, out_ref)


def select_kernel(own_ref, came_ref, keep_ref, give_ref):
    holder = lax.axis_index("core") == lax.axis_index("y") // 2
    own = own_ref[...]
    came = came_ref[...]
    keep_ref[...] = jnp.where(holder, own, came)
    give_ref[...] = jnp.where(holder, came, own)


def rows_of(half):
    return pl.ds(pl.multiple_of(half * BLOCK, BLOCK), BLOCK)


def join_kernel(m, piece_ref, *refs):
    out_ref, sem = refs[-2:]
    core = lax.axis_index("core")
    source = jnp.bitwise_xor(lax.axis_index("y"), m)
    half = jnp.where(source // 2 == core, core, 1 - core)
    copy = pltpu.make_async_copy(piece_ref, out_ref.at[:, source % 2, rows_of(half), :], sem)
    copy.start()
    copy.wait()


def last_join_kernel(kept_ref, swapped_ref, joined_ref, out_ref, sems):
    del joined_ref
    core = lax.axis_index("core")
    bin_index = lax.axis_index("y") % 2
    copies = [
        pltpu.make_async_copy(piece, out_ref.at[:, bin_index, rows_of(half), :], sems.at[index])
        for index, (piece, half) in enumerate(((kept_ref, core), (swapped_ref, 1 - core)))
    ]
    for copy in copies:
        copy.start()
    for copy in copies:
        copy.wait()


def call(kernel, shapes, *args, spaces=None, out_space=pltpu.VMEM, scratch=(), aliases=None, flops=0, mib=16):
    shapes = [shape if isinstance(shape, jax.ShapeDtypeStruct) else bf16(shape) for shape in shapes]
    spaces = spaces or [pltpu.VMEM] * len(args)
    cost = None
    if flops is not None:
        moved = sum(arg.size * arg.dtype.itemsize for arg in args)
        moved += sum(math.prod(shape.shape) * shape.dtype.itemsize for shape in shapes)
        cost = pl.CostEstimate(flops=flops, bytes_accessed=moved, transcendentals=0)
    results = pl.pallas_call(
        kernel,
        out_shape=shapes,
        in_specs=[pl.BlockSpec(memory_space=space) for space in spaces],
        out_specs=[pl.BlockSpec(memory_space=out_space)] * len(shapes),
        scratch_shapes=list(scratch),
        input_output_aliases=aliases or {},
        cost_estimate=cost,
        compiler_params=pltpu.CompilerParams(vmem_limit_bytes=mib * 1024 * 1024),
    )(*args)
    return results[0] if len(shapes) == 1 else results


def bf16(shape):
    return jax.ShapeDtypeStruct(shape, jnp.bfloat16)


def pair_z(value, first):
    moves = [(z, (z + (1 if (z % 2 == 1) == first else -1)) % NB) for z in range(NB)]
    return lax.ppermute(value, Z, moves)


def carry(value):
    moves = [(z, (z + 1) % NB) for z in range(NB)]
    moves += [(NB + z, NB + (z - 1) % NB) for z in range(NB)]
    return lax.ppermute(value, ("core",) + Z, moves)


def other_core(value):
    return lax.ppermute(value, "core", [(0, 1), (1, 0)])


def panel_moves(m):
    moves = []
    for core in range(2):
        for y in range(GROUP):
            if core == y // 2:
                target = (core, y ^ m)
            else:
                target = (1 - core, y ^ m ^ 2)
            moves.append((core * GROUP + y, target[0] * GROUP + target[1]))
    return moves


def partial_gram(diffs, single, pairs, values, offsets=None):
    count = 2 * len(diffs)
    shapes = [jax.ShapeDtypeStruct((count, HALF, HALF), jnp.float32), bf16((count, HALF, HALF))]
    spaces = [pltpu.VMEM] * len(values)
    if offsets is not None:
        shapes.append(jax.ShapeDtypeStruct((F, HALF), jnp.float32))
        values = (*values, offsets)
        spaces.append(pltpu.SMEM)
    return call(
        functools.partial(gram_kernel, diffs, single, pairs),
        shapes,
        *values,
        spaces=spaces,
        flops=count * 2 * BLOCK * BLOCK * KK,
    )


def on_device(records, offsets):
    outgoing = records.transpose(2, 0, 1, 3).reshape(F, REC_DEV, 2 * 64)
    arrived = lax.all_to_all(outgoing, ("x", "y"), 0, 0, tiled=True)
    here = call(pack_kernel, [(BLOCK, KK)], arrived)
    first = pair_z(here, True)
    second = pair_z(here, False)
    first2 = pair_z(second, True)
    second2 = pair_z(first, False)
    near, near_theirs, coefs = partial_gram(NEAR_DIFFS, (0,), (1,), (here, first, second), offsets)
    near_other = other_core(near_theirs)
    far, far_theirs = partial_gram(FAR_DIFFS, (), (1, 2), (first, second, first2, second2))
    far_other = other_core(far_theirs)
    strip = call(add_kernel, [(F, HALF, HALF)], near, near_other, far, far_other)
    bins = lax.all_to_all(strip, ("x", "y"), 0, 0, tiled=True)
    windowed = call(window_kernel, [(F, HALF, HALF)], coefs, bins)
    mine = lax.all_to_all(windowed, ("x", "y"), 0, 0, tiled=True)
    own = {}
    other = {}
    own[0], other[0] = mine, other_core(mine)
    pieces = {(0, True, True): own[0], (0, True, False): other[0]}
    for step in range(1, NB // 2 + 1):
        own[step] = carry(own[step - 1])
        pieces[(step, True, True)] = own[step]
        if step < NB // 2:
            other[step] = carry(other[step - 1])
            pieces[(step, True, False)] = other[step]
        pieces[(step, False, False)] = other_core(own[step])
        if step < NB // 2:
            pieces[(step, False, True)] = other_core(other[step])
    pieces = [pieces[key] for key in PIECES]
    whole_shape = (2, NB, F, HALF, HALF)
    whole, left = call(
        prepare_kernel,
        [whole_shape, (2 * BLOCK, S)],
        *pieces[:-2],
        spaces=[pl.ANY] * (NPIECES - 2),
        scratch=[pltpu.SemaphoreType.DMA((NPIECES - 2,))],
    )
    tile = (2, BLOCK, BLOCK)
    out_shape = (2, 2, 2 * BLOCK, BLOCK)
    panels = {}
    whole, panels[PANELS[0]] = call(
        first_panel_kernel,
        [whole_shape, tile],
        whole,
        left,
        *pieces[-2:],
        spaces=[pltpu.VMEM, pltpu.VMEM, pl.ANY, pl.ANY],
        scratch=[pltpu.SemaphoreType.DMA((2,))],
        aliases={0: 0},
        flops=None,
    )
    rest = call(panels_kernel, [tile] * (GROUP - 1), left, whole, flops=None)
    panels.update(zip(PANELS[1:], rest))
    arrived = {2: lax.ppermute(panels[2], "y", [(y, y ^ 2) for y in range(GROUP)])}
    for m in (1, 3):
        arrived[m] = lax.ppermute(panels[m], ("core", "y"), panel_moves(m))
    kept, given = call(select_kernel, [tile, tile], panels[0], arrived[2], flops=None)
    swapped = other_core(given)
    joined = []
    for m in (1, 3):
        joined = [
            call(
                functools.partial(join_kernel, m),
                [out_shape],
                arrived[m],
                *joined,
                spaces=[pl.ANY] * (1 + len(joined)),
                out_space=pl.ANY,
                scratch=[pltpu.SemaphoreType.DMA],
                aliases={1: 0} if joined else None,
                flops=None,
            )
        ]
    return call(
        last_join_kernel,
        [out_shape],
        kept,
        swapped,
        *joined,
        spaces=[pl.ANY] * 3,
        out_space=pl.ANY,
        scratch=[pltpu.SemaphoreType.DMA((2,))],
        aliases={2: 0},
        flops=None,
    )


def solution(mesh):
    fine = Mesh(mesh.devices.reshape(4, 2, 4, 2, 4), ("x", "core", "zh", "zl", "y"))
    return jax.shard_map(
        on_device,
        mesh=fine,
        in_specs=(P(("x", "core"), None, None, ("zh", "zl", "y")), P()),
        out_specs=P(None, ("x", "core"), "zh", ("zl", "y")),
        check_vma=False,
    )
```

```python
import functools
import math

import jax
import jax.numpy as jnp
import numpy as np
from jax import lax
from jax.experimental import pallas as pl
from jax.experimental.pallas import tpu as pltpu
from jax.sharding import Mesh, PartitionSpec as P

S = 2048
F = 16
RECORDS = 384
BLOCK = 256
HALF = 128
NOFF = 4
NB = 8
REC_DEV = 48
GROUP = 4
NK = GROUP * REC_DEV
KK = 2 * NK
NEAR_DIFFS = (0, 1, 7, 2, 6)
FAR_DIFFS = (3, 5, 4)
PANELS = (2, 1, 3, 0)
Z = ("zh", "zl")


def lag_profile():
    lag = np.minimum(np.arange(F), F - np.arange(F))
    rows = []
    for offset in range(NOFF):
        inside = (lag >= offset + 2) & (lag < offset + 5)
        weights = np.where(inside, 1.0, 0.1)
        step = np.arange(F // 2 + 1)
        angles = 2.0 * np.pi * (step[:, None] * np.arange(F)[None, :] % F) / F
        rows.append(np.cos(angles) @ weights / F)
    return [[float(value) for value in row] for row in rows]


LAG_PROFILE = lag_profile()


def home_shift(diff):
    return jnp.where(diff <= 4, -(diff // 2), (9 - diff) // 2)


HOME = [0, 0, -1, -1, -2, 2, 1, 1]

PIECES = [(0, True, True), (0, True, False)]
for _step in range(1, NB // 2):
    PIECES += [
        (_step, True, True),
        (_step, True, False),
        (_step, False, False),
        (_step, False, True),
    ]
PIECES += [(NB // 2, True, True), (NB // 2, False, False)]
NPIECES = len(PIECES)


def pack_kernel(y_ref, out_ref):
    for part in range(GROUP):
        rows = jnp.concatenate([y_ref[line * GROUP + part] for line in range(GROUP)], axis=0)
        turned = rows.astype(jnp.float32).T.astype(jnp.bfloat16)
        both = jnp.concatenate([turned[:64], turned[64:]], axis=1)
        out_ref[part * 64 : (part + 1) * 64, :] = both


def write_coefs(offsets_ref, coefs_ref):
    piece = lax.axis_index("x") * GROUP + lax.axis_index("y")
    plane = lax.axis_index("zh") * 2 + lax.axis_index("zl")
    diff = piece // 2
    a = (plane + home_shift(diff) + NB) % NB
    b = (a + diff) % NB
    shift = (offsets_ref[a, b] + offsets_ref[b, a]) % NOFF
    for step in range(F // 2 + 1):
        value = jnp.float32(LAG_PROFILE[0][step])
        for offset in range(1, NOFF):
            value = jnp.where(shift == offset, jnp.float32(LAG_PROFILE[offset][step]), value)
        coefs_ref[step : step + 1, :] = jnp.full((1, HALF), value, jnp.float32)


def gram_kernel(diffs, single, pairs, *refs):
    count = len(single) + 2 * len(pairs)
    if len(refs) > count + 2:
        write_coefs(refs[count], refs[-1])
        refs = refs[:count] + refs[count + 1 : -1]
    first_core = lax.axis_index("core") == 0
    even = lax.axis_index("zl") == 0
    rights = {plane: refs[index][...] for index, plane in enumerate(single)}
    for index, plane in enumerate(pairs):
        first = refs[len(single) + 2 * index][...]
        second = refs[len(single) + 2 * index + 1][...]
        rights[-plane] = jnp.where(even, first, second)
        rights[plane] = jnp.where(even, second, first)
    mine_ref, theirs_ref = refs[count:]
    lane = lax.broadcasted_iota(jnp.int32, (BLOCK, KK), 1)
    sign = jnp.where(lane < NK, -1.0, 1.0).astype(jnp.float32)
    scale = jnp.float32(1.0 / math.sqrt(RECORDS))
    lefts = {}
    for plane in sorted({HOME[diff] for diff in diffs}):
        top = rights[plane]
        bottom = (pltpu.roll(top.astype(jnp.float32), NK, 1) * sign).astype(jnp.bfloat16)
        lefts[plane] = jnp.concatenate([top, bottom], axis=0)
    for index, diff in enumerate(diffs):
        a = HOME[diff]
        b = (a + diff + 3) % NB - 3
        both = lax.dot_general(
            lefts[a], rights[b], (((1,), (1,)), ((), ())), preferred_element_type=jnp.float32
        )
        tile = (both[:BLOCK] + both[BLOCK:]) * scale
        mine = jnp.where(first_core, tile[:HALF], tile[HALF:])
        theirs = jnp.where(first_core, tile[HALF:], tile[:HALF]).astype(jnp.bfloat16)
        for side in range(2):
            columns = slice(side * HALF, (side + 1) * HALF)
            mine_ref[2 * index + side] = mine[:, columns]
            theirs_ref[2 * index + side] = theirs[:, columns]


def add_kernel(near_ref, near_other_ref, far_ref, far_other_ref, out_ref):
    for diffs, mine_ref, other_ref in (
        (NEAR_DIFFS, near_ref, near_other_ref),
        (FAR_DIFFS, far_ref, far_other_ref),
    ):
        for index, diff in enumerate(diffs):
            for side in range(2):
                total = mine_ref[2 * index + side] + other_ref[2 * index + side].astype(jnp.float32)
                out_ref[2 * diff + side] = total.astype(jnp.bfloat16)


def window_kernel(coefs_ref, in_ref, out_ref):
    coefs = [coefs_ref[step : step + 1, :] for step in range(F // 2 + 1)]

    def chunk(index, carry):
        rows = pl.ds(pl.multiple_of(index * 16, 16), 16)
        data = [in_ref[g, rows, :].astype(jnp.float32) for g in range(F)]
        for f in range(F):
            total = coefs[0] * data[f] + coefs[F // 2] * data[(f + F // 2) % F]
            for step in range(1, F // 2):
                total = total + coefs[step] * (data[(f + step) % F] + data[(f - step) % F])
            out_ref[f, rows, :] = total.astype(jnp.bfloat16)
        return carry

    lax.fori_loop(0, HALF // 16, chunk, 0)


def place():
    core = lax.axis_index("core")
    zh = lax.axis_index("zh")
    zl = lax.axis_index("zl")
    return core, 2 * zh + zl, 2 * zh + core, 4 * zl


def copy_in(entry, piece_ref, g_ref, sem):
    step, carried, own = entry
    core, here, _, _ = place()
    away = jnp.where(core == 0, -1, 1)
    plane = (here + (away if carried else -away) * step + NB) % NB
    half = core if own else 1 - core
    return pltpu.make_async_copy(piece_ref, g_ref.at[half, plane], sem)


def read_block(g_ref, a, diff):
    plane = (a - home_shift(diff) + NB) % NB
    halves = [
        jnp.concatenate([g_ref[h, plane, 2 * diff], g_ref[h, plane, 2 * diff + 1]], axis=1)
        for h in range(2)
    ]
    return jnp.concatenate(halves, axis=0)


def prepare_kernel(*refs):
    pieces = refs[: NPIECES - 2]
    g_ref, left_ref, sems = refs[NPIECES - 2 :]
    _, _, i, _ = place()
    copies = []
    for index, piece_ref in enumerate(pieces):
        copy = copy_in(PIECES[index], piece_ref, g_ref, sems.at[index])
        copy.start()
        copies.append(copy)
    for copy in copies:
        copy.wait()
    for step in range(NB):
        columns = pl.ds(step * BLOCK, BLOCK)
        left_ref[:BLOCK, columns] = read_block(g_ref, i, jnp.int32(step))
        k = (i + step) % NB
        across = read_block(g_ref, k, jnp.int32((NB - step) % NB))
        left_ref[BLOCK:, columns] = across.astype(jnp.float32).T.astype(jnp.bfloat16)


def panel(m, g_ref, left_ref, out_ref):
    core, _, i, first = place()
    y = lax.axis_index("y")
    aside = jnp.where(core == y // 2, 0, 2) if m % 2 == 1 else 0
    j = first + jnp.bitwise_xor(y, jnp.bitwise_xor(m, aside))
    downs = []
    acrosses = []
    for step in range(NB):
        k = (i + step) % NB
        downs.append(read_block(g_ref, k, (j - k + NB) % NB))
        acrosses.append(read_block(g_ref, j, (k - j + NB) % NB))
    down = jnp.concatenate(downs, axis=0)
    across = jnp.concatenate(acrosses, axis=1)
    first = jnp.dot(left_ref[...], down, preferred_element_type=jnp.float32)
    second = lax.dot_general(
        left_ref[...], across, (((1,), (1,)), ((), ())), preferred_element_type=jnp.float32
    )
    scale = jnp.float32(0.5 / math.sqrt(S))
    out_ref[0] = ((second[:BLOCK] + first[BLOCK:]) * scale).astype(jnp.bfloat16)
    out_ref[1] = ((first[:BLOCK] - second[BLOCK:]) * scale).astype(jnp.bfloat16)


def first_panel_kernel(old_ref, left_ref, last_ref, last_swap_ref, g_ref, out_ref, sems):
    del old_ref
    copies = [
        copy_in(PIECES[-2], last_ref, g_ref, sems.at[0]),
        copy_in(PIECES[-1], last_swap_ref, g_ref, sems.at[1]),
    ]
    for copy in copies:
        copy.start()
    for copy in copies:
        copy.wait()
    panel(PANELS[0], g_ref, left_ref, out_ref)


def panels_kernel(left_ref, g_ref, *out_refs):
    for m, out_ref in zip(PANELS[1:], out_refs):
        panel(m, g_ref, left_ref, out_ref)


def select_kernel(own_ref, came_ref, keep_ref, give_ref):
    holder = lax.axis_index("core") == lax.axis_index("y") // 2
    own = own_ref[...]
    came = came_ref[...]
    keep_ref[...] = jnp.where(holder, own, came)
    give_ref[...] = jnp.where(holder, came, own)


def rows_of(half):
    return pl.ds(pl.multiple_of(half * BLOCK, BLOCK), BLOCK)


def join_kernel(one_ref, three_ref, kept_ref, swapped_ref, out_ref, sems):
    core = lax.axis_index("core")
    y = lax.axis_index("y")
    pieces = [(kept_ref, y % 2, core), (swapped_ref, y % 2, 1 - core)]
    for m, piece_ref in ((1, one_ref), (3, three_ref)):
        source = jnp.bitwise_xor(y, m)
        half = jnp.where(source // 2 == core, core, 1 - core)
        pieces.append((piece_ref, source % 2, half))
    copies = [
        pltpu.make_async_copy(piece, out_ref.at[:, bin_index, rows_of(half), :], sems.at[index])
        for index, (piece, bin_index, half) in enumerate(pieces)
    ]
    for copy in copies:
        copy.start()
    for copy in copies:
        copy.wait()


def call(kernel, shapes, *args, spaces=None, out_space=pltpu.VMEM, scratch=(), aliases=None, flops=0, mib=16):
    shapes = [shape if isinstance(shape, jax.ShapeDtypeStruct) else bf16(shape) for shape in shapes]
    spaces = spaces or [pltpu.VMEM] * len(args)
    cost = None
    if flops is not None:
        moved = sum(arg.size * arg.dtype.itemsize for arg in args)
        moved += sum(math.prod(shape.shape) * shape.dtype.itemsize for shape in shapes)
        cost = pl.CostEstimate(flops=flops, bytes_accessed=moved, transcendentals=0)
    results = pl.pallas_call(
        kernel,
        out_shape=shapes,
        in_specs=[pl.BlockSpec(memory_space=space) for space in spaces],
        out_specs=[pl.BlockSpec(memory_space=out_space)] * len(shapes),
        scratch_shapes=list(scratch),
        input_output_aliases=aliases or {},
        cost_estimate=cost,
        compiler_params=pltpu.CompilerParams(vmem_limit_bytes=mib * 1024 * 1024),
    )(*args)
    return results[0] if len(shapes) == 1 else results


def bf16(shape):
    return jax.ShapeDtypeStruct(shape, jnp.bfloat16)


def pair_z(value, first):
    moves = [(z, (z + (1 if (z % 2 == 1) == first else -1)) % NB) for z in range(NB)]
    return lax.ppermute(value, Z, moves)


def carry(value):
    moves = [(z, (z + 1) % NB) for z in range(NB)]
    moves += [(NB + z, NB + (z - 1) % NB) for z in range(NB)]
    return lax.ppermute(value, ("core",) + Z, moves)


def other_core(value):
    return lax.ppermute(value, "core", [(0, 1), (1, 0)])


def panel_moves(m):
    moves = []
    for core in range(2):
        for y in range(GROUP):
            if core == y // 2:
                target = (core, y ^ m)
            else:
                target = (1 - core, y ^ m ^ 2)
            moves.append((core * GROUP + y, target[0] * GROUP + target[1]))
    return moves


def partial_gram(diffs, single, pairs, values, offsets=None):
    count = 2 * len(diffs)
    shapes = [jax.ShapeDtypeStruct((count, HALF, HALF), jnp.float32), bf16((count, HALF, HALF))]
    spaces = [pltpu.VMEM] * len(values)
    if offsets is not None:
        shapes.append(jax.ShapeDtypeStruct((F, HALF), jnp.float32))
        values = (*values, offsets)
        spaces.append(pltpu.SMEM)
    return call(
        functools.partial(gram_kernel, diffs, single, pairs),
        shapes,
        *values,
        spaces=spaces,
        flops=count * 2 * BLOCK * BLOCK * KK,
    )


def on_device(records, offsets):
    outgoing = records.transpose(2, 0, 1, 3).reshape(F, REC_DEV, 2 * 64)
    arrived = lax.all_to_all(outgoing, ("x", "y"), 0, 0, tiled=True)
    here = call(pack_kernel, [(BLOCK, KK)], arrived)
    first = pair_z(here, True)
    second = pair_z(here, False)
    first2 = pair_z(second, True)
    second2 = pair_z(first, False)
    near, near_theirs, coefs = partial_gram(NEAR_DIFFS, (0,), (1,), (here, first, second), offsets)
    near_other = other_core(near_theirs)
    far, far_theirs = partial_gram(FAR_DIFFS, (), (1, 2), (first, second, first2, second2))
    far_other = other_core(far_theirs)
    strip = call(add_kernel, [(F, HALF, HALF)], near, near_other, far, far_other)
    bins = lax.all_to_all(strip, ("x", "y"), 0, 0, tiled=True)
    windowed = call(window_kernel, [(F, HALF, HALF)], coefs, bins)
    mine = lax.all_to_all(windowed, ("x", "y"), 0, 0, tiled=True)
    own = {}
    other = {}
    own[0], other[0] = mine, other_core(mine)
    pieces = {(0, True, True): own[0], (0, True, False): other[0]}
    for step in range(1, NB // 2 + 1):
        own[step] = carry(own[step - 1])
        pieces[(step, True, True)] = own[step]
        if step < NB // 2:
            other[step] = carry(other[step - 1])
            pieces[(step, True, False)] = other[step]
        pieces[(step, False, False)] = other_core(own[step])
        if step < NB // 2:
            pieces[(step, False, True)] = other_core(other[step])
    pieces = [pieces[key] for key in PIECES]
    whole_shape = (2, NB, F, HALF, HALF)
    whole, left = call(
        prepare_kernel,
        [whole_shape, (2 * BLOCK, S)],
        *pieces[:-2],
        spaces=[pl.ANY] * (NPIECES - 2),
        scratch=[pltpu.SemaphoreType.DMA((NPIECES - 2,))],
    )
    tile = (2, BLOCK, BLOCK)
    out_shape = (2, 2, 2 * BLOCK, BLOCK)
    panels = {}
    whole, panels[PANELS[0]] = call(
        first_panel_kernel,
        [whole_shape, tile],
        whole,
        left,
        *pieces[-2:],
        spaces=[pltpu.VMEM, pltpu.VMEM, pl.ANY, pl.ANY],
        scratch=[pltpu.SemaphoreType.DMA((2,))],
        aliases={0: 0},
        flops=None,
    )
    rest = call(panels_kernel, [tile] * (GROUP - 1), left, whole, flops=None)
    panels.update(zip(PANELS[1:], rest))
    arrived = {2: lax.ppermute(panels[2], "y", [(y, y ^ 2) for y in range(GROUP)])}
    for m in (1, 3):
        arrived[m] = lax.ppermute(panels[m], ("core", "y"), panel_moves(m))
    kept, given = call(select_kernel, [tile, tile], panels[0], arrived[2], flops=None)
    swapped = other_core(given)
    return call(
        join_kernel,
        [out_shape],
        arrived[1],
        arrived[3],
        kept,
        swapped,
        spaces=[pl.ANY] * GROUP,
        out_space=pl.ANY,
        scratch=[pltpu.SemaphoreType.DMA((GROUP,))],
        flops=None,
    )


def solution(mesh):
    fine = Mesh(mesh.devices.reshape(4, 2, 4, 2, 4), ("x", "core", "zh", "zl", "y"))
    return jax.shard_map(
        on_device,
        mesh=fine,
        in_specs=(P(("x", "core"), None, None, ("zh", "zl", "y")), P()),
        out_specs=P(None, ("x", "core"), "zh", ("zl", "y")),
        check_vma=False,
    )
```

```python
import functools
import math

import jax
import jax.numpy as jnp
import numpy as np
from jax import lax
from jax.experimental import pallas as pl
from jax.experimental.pallas import tpu as pltpu
from jax.sharding import Mesh, PartitionSpec as P

S = 2048
F = 16
RECORDS = 384
BLOCK = 256
HALF = 128
NOFF = 4
NB = 8
REC_DEV = 48
GROUP = 4
NK = GROUP * REC_DEV
KK = 2 * NK
NEAR_DIFFS = (0, 1, 7, 2, 6)
FAR_DIFFS = (3, 5, 4)
PANELS = (2, 1, 3, 0)
Z = ("zh", "zl")


def lag_profile():
    lag = np.minimum(np.arange(F), F - np.arange(F))
    rows = []
    for offset in range(NOFF):
        inside = (lag >= offset + 2) & (lag < offset + 5)
        weights = np.where(inside, 1.0, 0.1)
        step = np.arange(F // 2 + 1)
        angles = 2.0 * np.pi * (step[:, None] * np.arange(F)[None, :] % F) / F
        rows.append(np.cos(angles) @ weights / F)
    return [[float(value) for value in row] for row in rows]


LAG_PROFILE = lag_profile()


def home_shift(diff):
    return jnp.where(diff <= 4, -(diff // 2), (9 - diff) // 2)


HOME = [0, 0, -1, -1, -2, 2, 1, 1]

PIECES = [(0, True, True), (0, True, False)]
for _step in range(1, NB // 2):
    PIECES += [
        (_step, True, True),
        (_step, True, False),
        (_step, False, False),
        (_step, False, True),
    ]
PIECES += [(NB // 2, True, True), (NB // 2, False, False)]
NPIECES = len(PIECES)


def pack_kernel(y_ref, out_ref):
    for part in range(GROUP):
        rows = jnp.concatenate([y_ref[line * GROUP + part] for line in range(GROUP)], axis=0)
        turned = rows.astype(jnp.float32).T.astype(jnp.bfloat16)
        both = jnp.concatenate([turned[:64], turned[64:]], axis=1)
        out_ref[part * 64 : (part + 1) * 64, :] = both


def write_coefs(offsets_ref, coefs_ref):
    piece = lax.axis_index("x") * GROUP + lax.axis_index("y")
    plane = lax.axis_index("zh") * 2 + lax.axis_index("zl")
    diff = piece // 2
    a = (plane + home_shift(diff) + NB) % NB
    b = (a + diff) % NB
    shift = (offsets_ref[a, b] + offsets_ref[b, a]) % NOFF
    for step in range(F // 2 + 1):
        value = jnp.float32(LAG_PROFILE[0][step])
        for offset in range(1, NOFF):
            value = jnp.where(shift == offset, jnp.float32(LAG_PROFILE[offset][step]), value)
        coefs_ref[step : step + 1, :] = jnp.full((1, HALF), value, jnp.float32)


def gram_kernel(diffs, single, pairs, *refs):
    count = len(single) + 2 * len(pairs)
    if len(refs) > count + 2:
        write_coefs(refs[count], refs[-1])
        refs = refs[:count] + refs[count + 1 : -1]
    first_core = lax.axis_index("core") == 0
    even = lax.axis_index("zl") == 0
    rights = {plane: refs[index][...] for index, plane in enumerate(single)}
    for index, plane in enumerate(pairs):
        first = refs[len(single) + 2 * index][...]
        second = refs[len(single) + 2 * index + 1][...]
        rights[-plane] = jnp.where(even, first, second)
        rights[plane] = jnp.where(even, second, first)
    mine_ref, theirs_ref = refs[count:]
    lane = lax.broadcasted_iota(jnp.int32, (BLOCK, KK), 1)
    sign = jnp.where(lane < NK, -1.0, 1.0).astype(jnp.float32)
    scale = jnp.float32(1.0 / math.sqrt(RECORDS))
    lefts = {}
    for plane in sorted({HOME[diff] for diff in diffs}):
        top = rights[plane]
        bottom = (pltpu.roll(top.astype(jnp.float32), NK, 1) * sign).astype(jnp.bfloat16)
        lefts[plane] = jnp.concatenate([top, bottom], axis=0)
    for index, diff in enumerate(diffs):
        a = HOME[diff]
        b = (a + diff + 3) % NB - 3
        both = lax.dot_general(
            lefts[a], rights[b], (((1,), (1,)), ((), ())), preferred_element_type=jnp.float32
        )
        tile = (both[:BLOCK] + both[BLOCK:]) * scale
        mine = jnp.where(first_core, tile[:HALF], tile[HALF:])
        theirs = jnp.where(first_core, tile[HALF:], tile[:HALF]).astype(jnp.bfloat16)
        for side in range(2):
            columns = slice(side * HALF, (side + 1) * HALF)
            mine_ref[2 * index + side] = mine[:, columns]
            theirs_ref[2 * index + side] = theirs[:, columns]


def add_kernel(near_ref, near_other_ref, far_ref, far_other_ref, out_ref):
    for diffs, mine_ref, other_ref in (
        (NEAR_DIFFS, near_ref, near_other_ref),
        (FAR_DIFFS, far_ref, far_other_ref),
    ):
        for index, diff in enumerate(diffs):
            for side in range(2):
                total = mine_ref[2 * index + side] + other_ref[2 * index + side].astype(jnp.float32)
                out_ref[2 * diff + side] = total.astype(jnp.bfloat16)


def window_kernel(coefs_ref, in_ref, out_ref):
    coefs = [coefs_ref[step : step + 1, :] for step in range(F // 2 + 1)]

    def chunk(index, carry):
        rows = pl.ds(pl.multiple_of(index * 16, 16), 16)
        data = [in_ref[g, rows, :].astype(jnp.float32) for g in range(F)]
        for f in range(F):
            total = coefs[0] * data[f] + coefs[F // 2] * data[(f + F // 2) % F]
            for step in range(1, F // 2):
                total = total + coefs[step] * (data[(f + step) % F] + data[(f - step) % F])
            out_ref[f, rows, :] = total.astype(jnp.bfloat16)
        return carry

    lax.fori_loop(0, HALF // 16, chunk, 0)


def place():
    core = lax.axis_index("core")
    zh = lax.axis_index("zh")
    zl = lax.axis_index("zl")
    return core, 2 * zh + zl, 2 * zh + core, 4 * zl


def copy_in(entry, piece_ref, g_ref, sem):
    step, carried, own = entry
    core, here, _, _ = place()
    away = jnp.where(core == 0, -1, 1)
    plane = (here + (away if carried else -away) * step + NB) % NB
    half = core if own else 1 - core
    return pltpu.make_async_copy(piece_ref, g_ref.at[half, plane], sem)


def read_block(g_ref, a, diff):
    plane = (a - home_shift(diff) + NB) % NB
    halves = [
        jnp.concatenate([g_ref[h, plane, 2 * diff], g_ref[h, plane, 2 * diff + 1]], axis=1)
        for h in range(2)
    ]
    return jnp.concatenate(halves, axis=0)


def prepare_kernel(*refs):
    pieces = refs[: NPIECES - 2]
    g_ref, left_ref, sems = refs[NPIECES - 2 :]
    _, _, i, _ = place()
    copies = []
    for index, piece_ref in enumerate(pieces):
        copy = copy_in(PIECES[index], piece_ref, g_ref, sems.at[index])
        copy.start()
        copies.append(copy)
    for copy in copies:
        copy.wait()
    for step in range(NB):
        columns = pl.ds(step * BLOCK, BLOCK)
        left_ref[:BLOCK, columns] = read_block(g_ref, i, jnp.int32(step))
        k = (i + step) % NB
        across = read_block(g_ref, k, jnp.int32((NB - step) % NB))
        left_ref[BLOCK:, columns] = across.astype(jnp.float32).T.astype(jnp.bfloat16)


def panel(m, g_ref, left_ref, out_ref):
    core, _, i, first = place()
    y = lax.axis_index("y")
    aside = jnp.where(core == y // 2, 0, 2) if m % 2 == 1 else 0
    j = first + jnp.bitwise_xor(y, jnp.bitwise_xor(m, aside))
    downs = []
    acrosses = []
    for step in range(NB):
        k = (i + step) % NB
        downs.append(read_block(g_ref, k, (j - k + NB) % NB))
        acrosses.append(read_block(g_ref, j, (k - j + NB) % NB))
    down = jnp.concatenate(downs, axis=0)
    across = jnp.concatenate(acrosses, axis=1)
    first = jnp.dot(left_ref[...], down, preferred_element_type=jnp.float32)
    second = lax.dot_general(
        left_ref[...], across, (((1,), (1,)), ((), ())), preferred_element_type=jnp.float32
    )
    scale = jnp.float32(0.5 / math.sqrt(S))
    out_ref[0] = ((second[:BLOCK] + first[BLOCK:]) * scale).astype(jnp.bfloat16)
    out_ref[1] = ((first[:BLOCK] - second[BLOCK:]) * scale).astype(jnp.bfloat16)


def first_panel_kernel(old_ref, left_ref, last_ref, last_swap_ref, g_ref, out_ref, sems):
    del old_ref
    copies = [
        copy_in(PIECES[-2], last_ref, g_ref, sems.at[0]),
        copy_in(PIECES[-1], last_swap_ref, g_ref, sems.at[1]),
    ]
    for copy in copies:
        copy.start()
    for copy in copies:
        copy.wait()
    panel(PANELS[0], g_ref, left_ref, out_ref)


def panels_kernel(left_ref, g_ref, *out_refs):
    for m, out_ref in zip(PANELS[1:-1], out_refs):
        panel(m, g_ref, left_ref, out_ref)


def last_panel_kernel(left_ref, g_ref, came_ref, keep_ref, give_ref, own_ref):
    panel(PANELS[-1], g_ref, left_ref, own_ref)
    holder = lax.axis_index("core") == lax.axis_index("y") // 2
    own = own_ref[...]
    came = came_ref[...]
    keep_ref[...] = jnp.where(holder, own, came)
    give_ref[...] = jnp.where(holder, came, own)


def rows_of(half):
    return pl.ds(pl.multiple_of(half * BLOCK, BLOCK), BLOCK)


def join_kernel(one_ref, three_ref, kept_ref, swapped_ref, out_ref, sems):
    core = lax.axis_index("core")
    y = lax.axis_index("y")
    pieces = [(kept_ref, y % 2, core), (swapped_ref, y % 2, 1 - core)]
    for m, piece_ref in ((1, one_ref), (3, three_ref)):
        source = jnp.bitwise_xor(y, m)
        half = jnp.where(source // 2 == core, core, 1 - core)
        pieces.append((piece_ref, source % 2, half))
    copies = [
        pltpu.make_async_copy(piece, out_ref.at[:, bin_index, rows_of(half), :], sems.at[index])
        for index, (piece, bin_index, half) in enumerate(pieces)
    ]
    for copy in copies:
        copy.start()
    for copy in copies:
        copy.wait()


def call(kernel, shapes, *args, spaces=None, out_space=pltpu.VMEM, scratch=(), aliases=None, flops=0, mib=16):
    shapes = [shape if isinstance(shape, jax.ShapeDtypeStruct) else bf16(shape) for shape in shapes]
    spaces = spaces or [pltpu.VMEM] * len(args)
    cost = None
    if flops is not None:
        moved = sum(arg.size * arg.dtype.itemsize for arg in args)
        moved += sum(math.prod(shape.shape) * shape.dtype.itemsize for shape in shapes)
        cost = pl.CostEstimate(flops=flops, bytes_accessed=moved, transcendentals=0)
    results = pl.pallas_call(
        kernel,
        out_shape=shapes,
        in_specs=[pl.BlockSpec(memory_space=space) for space in spaces],
        out_specs=[pl.BlockSpec(memory_space=out_space)] * len(shapes),
        scratch_shapes=list(scratch),
        input_output_aliases=aliases or {},
        cost_estimate=cost,
        compiler_params=pltpu.CompilerParams(vmem_limit_bytes=mib * 1024 * 1024),
    )(*args)
    return results[0] if len(shapes) == 1 else results


def bf16(shape):
    return jax.ShapeDtypeStruct(shape, jnp.bfloat16)


def pair_z(value, first):
    moves = [(z, (z + (1 if (z % 2 == 1) == first else -1)) % NB) for z in range(NB)]
    return lax.ppermute(value, Z, moves)


def carry(value):
    moves = [(z, (z + 1) % NB) for z in range(NB)]
    moves += [(NB + z, NB + (z - 1) % NB) for z in range(NB)]
    return lax.ppermute(value, ("core",) + Z, moves)


def other_core(value):
    return lax.ppermute(value, "core", [(0, 1), (1, 0)])


def panel_moves(m):
    moves = []
    for core in range(2):
        for y in range(GROUP):
            if core == y // 2:
                target = (core, y ^ m)
            else:
                target = (1 - core, y ^ m ^ 2)
            moves.append((core * GROUP + y, target[0] * GROUP + target[1]))
    return moves


def partial_gram(diffs, single, pairs, values, offsets=None):
    count = 2 * len(diffs)
    shapes = [jax.ShapeDtypeStruct((count, HALF, HALF), jnp.float32), bf16((count, HALF, HALF))]
    spaces = [pltpu.VMEM] * len(values)
    if offsets is not None:
        shapes.append(jax.ShapeDtypeStruct((F, HALF), jnp.float32))
        values = (*values, offsets)
        spaces.append(pltpu.SMEM)
    return call(
        functools.partial(gram_kernel, diffs, single, pairs),
        shapes,
        *values,
        spaces=spaces,
        flops=count * 2 * BLOCK * BLOCK * KK,
    )


def on_device(records, offsets):
    outgoing = records.transpose(2, 0, 1, 3).reshape(F, REC_DEV, 2 * 64)
    arrived = lax.all_to_all(outgoing, ("x", "y"), 0, 0, tiled=True)
    here = call(pack_kernel, [(BLOCK, KK)], arrived)
    first = pair_z(here, True)
    second = pair_z(here, False)
    first2 = pair_z(second, True)
    second2 = pair_z(first, False)
    near, near_theirs, coefs = partial_gram(NEAR_DIFFS, (0,), (1,), (here, first, second), offsets)
    near_other = other_core(near_theirs)
    far, far_theirs = partial_gram(FAR_DIFFS, (), (1, 2), (first, second, first2, second2))
    far_other = other_core(far_theirs)
    strip = call(add_kernel, [(F, HALF, HALF)], near, near_other, far, far_other)
    bins = lax.all_to_all(strip, ("x", "y"), 0, 0, tiled=True)
    windowed = call(window_kernel, [(F, HALF, HALF)], coefs, bins)
    mine = lax.all_to_all(windowed, ("x", "y"), 0, 0, tiled=True)
    own = {}
    other = {}
    own[0], other[0] = mine, other_core(mine)
    pieces = {(0, True, True): own[0], (0, True, False): other[0]}
    for step in range(1, NB // 2 + 1):
        own[step] = carry(own[step - 1])
        pieces[(step, True, True)] = own[step]
        if step < NB // 2:
            other[step] = carry(other[step - 1])
            pieces[(step, True, False)] = other[step]
        pieces[(step, False, False)] = other_core(own[step])
        if step < NB // 2:
            pieces[(step, False, True)] = other_core(other[step])
    pieces = [pieces[key] for key in PIECES]
    whole_shape = (2, NB, F, HALF, HALF)
    whole, left = call(
        prepare_kernel,
        [whole_shape, (2 * BLOCK, S)],
        *pieces[:-2],
        spaces=[pl.ANY] * (NPIECES - 2),
        scratch=[pltpu.SemaphoreType.DMA((NPIECES - 2,))],
    )
    tile = (2, BLOCK, BLOCK)
    out_shape = (2, 2, 2 * BLOCK, BLOCK)
    panels = {}
    whole, panels[PANELS[0]] = call(
        first_panel_kernel,
        [whole_shape, tile],
        whole,
        left,
        *pieces[-2:],
        spaces=[pltpu.VMEM, pltpu.VMEM, pl.ANY, pl.ANY],
        scratch=[pltpu.SemaphoreType.DMA((2,))],
        aliases={0: 0},
        flops=None,
    )
    rest = call(panels_kernel, [tile] * (GROUP - 2), left, whole, flops=None)
    panels.update(zip(PANELS[1:-1], rest))
    arrived = {2: lax.ppermute(panels[2], "y", [(y, y ^ 2) for y in range(GROUP)])}
    for m in (1, 3):
        arrived[m] = lax.ppermute(panels[m], ("core", "y"), panel_moves(m))
    kept, given = call(
        last_panel_kernel,
        [tile, tile],
        left,
        whole,
        arrived[2],
        scratch=[pltpu.VMEM(tile, jnp.bfloat16)],
        flops=None,
    )
    swapped = other_core(given)
    return call(
        join_kernel,
        [out_shape],
        arrived[1],
        arrived[3],
        kept,
        swapped,
        spaces=[pl.ANY] * GROUP,
        out_space=pl.ANY,
        scratch=[pltpu.SemaphoreType.DMA((GROUP,))],
        flops=None,
    )


def solution(mesh):
    fine = Mesh(mesh.devices.reshape(4, 2, 4, 2, 4), ("x", "core", "zh", "zl", "y"))
    return jax.shard_map(
        on_device,
        mesh=fine,
        in_specs=(P(("x", "core"), None, None, ("zh", "zl", "y")), P()),
        out_specs=P(None, ("x", "core"), "zh", ("zl", "y")),
        check_vma=False,
    )
```

```python
import functools
import math

import jax
import jax.numpy as jnp
import numpy as np
from jax import lax
from jax.experimental import pallas as pl
from jax.experimental.pallas import tpu as pltpu
from jax.sharding import Mesh, PartitionSpec as P

S = 2048
F = 16
RECORDS = 384
BLOCK = 256
HALF = 128
NOFF = 4
NB = 8
REC_DEV = 48
GROUP = 4
NK = GROUP * REC_DEV
KK = 2 * NK
NEAR_DIFFS = (0, 1, 7, 2, 6)
FAR_DIFFS = (3, 5, 4)
PANELS = (2, 1, 3, 0)
Z = ("zh", "zl")


def lag_profile():
    lag = np.minimum(np.arange(F), F - np.arange(F))
    rows = []
    for offset in range(NOFF):
        inside = (lag >= offset + 2) & (lag < offset + 5)
        weights = np.where(inside, 1.0, 0.1)
        step = np.arange(F // 2 + 1)
        angles = 2.0 * np.pi * (step[:, None] * np.arange(F)[None, :] % F) / F
        rows.append(np.cos(angles) @ weights / F)
    return [[float(value) for value in row] for row in rows]


LAG_PROFILE = lag_profile()


def home_shift(diff):
    return jnp.where(diff <= 4, -(diff // 2), (9 - diff) // 2)


HOME = [0, 0, -1, -1, -2, 2, 1, 1]

PIECES = [(0, True, True), (0, True, False)]
for _step in range(1, NB // 2):
    PIECES += [
        (_step, True, True),
        (_step, True, False),
        (_step, False, False),
        (_step, False, True),
    ]
PIECES += [(NB // 2, True, True), (NB // 2, False, False)]
NPIECES = len(PIECES)


def turn_kernel(records_ref, out_ref, rows_ref):
    for record in range(REC_DEV):
        both = jnp.concatenate([records_ref[record, 0], records_ref[record, 1]], axis=1)
        rows_ref[record * F : (record + 1) * F, :] = both.astype(jnp.float32)
    for f in range(F):
        out_ref[f] = rows_ref[pl.ds(f, REC_DEV, stride=F), :].astype(jnp.bfloat16)


def pack_kernel(y_ref, out_ref):
    for part in range(GROUP):
        rows = jnp.concatenate([y_ref[line * GROUP + part] for line in range(GROUP)], axis=0)
        turned = rows.astype(jnp.float32).T.astype(jnp.bfloat16)
        both = jnp.concatenate([turned[:64], turned[64:]], axis=1)
        out_ref[part * 64 : (part + 1) * 64, :] = both


def write_coefs(offsets_ref, coefs_ref):
    piece = lax.axis_index("x") * GROUP + lax.axis_index("y")
    plane = lax.axis_index("zh") * 2 + lax.axis_index("zl")
    diff = piece // 2
    a = (plane + home_shift(diff) + NB) % NB
    b = (a + diff) % NB
    shift = (offsets_ref[a, b] + offsets_ref[b, a]) % NOFF
    for step in range(F // 2 + 1):
        value = jnp.float32(LAG_PROFILE[0][step])
        for offset in range(1, NOFF):
            value = jnp.where(shift == offset, jnp.float32(LAG_PROFILE[offset][step]), value)
        coefs_ref[step : step + 1, :] = jnp.full((1, HALF), value, jnp.float32)


def gram_kernel(diffs, single, pairs, *refs):
    count = len(single) + 2 * len(pairs)
    if len(refs) > count + 2:
        write_coefs(refs[count], refs[-1])
        refs = refs[:count] + refs[count + 1 : -1]
    first_core = lax.axis_index("core") == 0
    even = lax.axis_index("zl") == 0
    rights = {plane: refs[index][...] for index, plane in enumerate(single)}
    for index, plane in enumerate(pairs):
        first = refs[len(single) + 2 * index][...]
        second = refs[len(single) + 2 * index + 1][...]
        rights[-plane] = jnp.where(even, first, second)
        rights[plane] = jnp.where(even, second, first)
    mine_ref, theirs_ref = refs[count:]
    lane = lax.broadcasted_iota(jnp.int32, (BLOCK, KK), 1)
    sign = jnp.where(lane < NK, -1.0, 1.0).astype(jnp.float32)
    scale = jnp.float32(1.0 / math.sqrt(RECORDS))
    lefts = {}
    for plane in sorted({HOME[diff] for diff in diffs}):
        top = rights[plane]
        bottom = (pltpu.roll(top.astype(jnp.float32), NK, 1) * sign).astype(jnp.bfloat16)
        lefts[plane] = jnp.concatenate([top, bottom], axis=0)
    for index, diff in enumerate(diffs):
        a = HOME[diff]
        b = (a + diff + 3) % NB - 3
        both = lax.dot_general(
            lefts[a], rights[b], (((1,), (1,)), ((), ())), preferred_element_type=jnp.float32
        )
        tile = (both[:BLOCK] + both[BLOCK:]) * scale
        mine = jnp.where(first_core, tile[:HALF], tile[HALF:])
        theirs = jnp.where(first_core, tile[HALF:], tile[:HALF]).astype(jnp.bfloat16)
        for side in range(2):
            columns = slice(side * HALF, (side + 1) * HALF)
            mine_ref[2 * index + side] = mine[:, columns]
            theirs_ref[2 * index + side] = theirs[:, columns]


def add_kernel(near_ref, near_other_ref, far_ref, far_other_ref, out_ref):
    for diffs, mine_ref, other_ref in (
        (NEAR_DIFFS, near_ref, near_other_ref),
        (FAR_DIFFS, far_ref, far_other_ref),
    ):
        for index, diff in enumerate(diffs):
            for side in range(2):
                total = mine_ref[2 * index + side] + other_ref[2 * index + side].astype(jnp.float32)
                out_ref[2 * diff + side] = total.astype(jnp.bfloat16)


def window_kernel(coefs_ref, in_ref, out_ref):
    coefs = [coefs_ref[step : step + 1, :] for step in range(F // 2 + 1)]

    def chunk(index, carry):
        rows = pl.ds(pl.multiple_of(index * 16, 16), 16)
        data = [in_ref[g, rows, :].astype(jnp.float32) for g in range(F)]
        for f in range(F):
            total = coefs[0] * data[f] + coefs[F // 2] * data[(f + F // 2) % F]
            for step in range(1, F // 2):
                total = total + coefs[step] * (data[(f + step) % F] + data[(f - step) % F])
            out_ref[f, rows, :] = total.astype(jnp.bfloat16)
        return carry

    lax.fori_loop(0, HALF // 16, chunk, 0)


def place():
    core = lax.axis_index("core")
    zh = lax.axis_index("zh")
    zl = lax.axis_index("zl")
    return core, 2 * zh + zl, 2 * zh + core, 4 * zl


def copy_in(entry, piece_ref, g_ref, sem):
    step, carried, own = entry
    core, here, _, _ = place()
    away = jnp.where(core == 0, 1, -1)
    plane = (here + (away if carried else -away) * step + NB) % NB
    half = core if own else 1 - core
    return pltpu.make_async_copy(piece_ref, g_ref.at[half, plane], sem)


def read_block(g_ref, a, diff):
    plane = (a - home_shift(diff) + NB) % NB
    halves = [
        jnp.concatenate([g_ref[h, plane, 2 * diff], g_ref[h, plane, 2 * diff + 1]], axis=1)
        for h in range(2)
    ]
    return jnp.concatenate(halves, axis=0)


def prepare_kernel(*refs):
    pieces = refs[: NPIECES - 2]
    g_ref, left_ref, sems = refs[NPIECES - 2 :]
    _, _, i, _ = place()
    copies = []
    for index, piece_ref in enumerate(pieces):
        copy = copy_in(PIECES[index], piece_ref, g_ref, sems.at[index])
        copy.start()
        copies.append(copy)
    for copy in copies:
        copy.wait()
    for step in range(NB):
        columns = pl.ds(step * BLOCK, BLOCK)
        left_ref[:BLOCK, columns] = read_block(g_ref, i, jnp.int32(step))
        k = (i + step) % NB
        across = read_block(g_ref, k, jnp.int32((NB - step) % NB))
        left_ref[BLOCK:, columns] = across.astype(jnp.float32).T.astype(jnp.bfloat16)


def panel(m, g_ref, left_ref, out_ref):
    core, _, i, first = place()
    y = lax.axis_index("y")
    aside = jnp.where(core == y // 2, 0, 2) if m % 2 == 1 else 0
    j = first + jnp.bitwise_xor(y, jnp.bitwise_xor(m, aside))
    downs = []
    acrosses = []
    for step in range(NB):
        k = (i + step) % NB
        downs.append(read_block(g_ref, k, (j - k + NB) % NB))
        acrosses.append(read_block(g_ref, j, (k - j + NB) % NB))
    down = jnp.concatenate(downs, axis=0)
    across = jnp.concatenate(acrosses, axis=1)
    first = jnp.dot(left_ref[...], down, preferred_element_type=jnp.float32)
    second = lax.dot_general(
        left_ref[...], across, (((1,), (1,)), ((), ())), preferred_element_type=jnp.float32
    )
    scale = jnp.float32(0.5 / math.sqrt(S))
    out_ref[0] = ((second[:BLOCK] + first[BLOCK:]) * scale).astype(jnp.bfloat16)
    out_ref[1] = ((first[:BLOCK] - second[BLOCK:]) * scale).astype(jnp.bfloat16)


def first_panel_kernel(old_ref, left_ref, last_ref, last_swap_ref, g_ref, out_ref, sems):
    del old_ref
    copies = [
        copy_in(PIECES[-2], last_ref, g_ref, sems.at[0]),
        copy_in(PIECES[-1], last_swap_ref, g_ref, sems.at[1]),
    ]
    for copy in copies:
        copy.start()
    for copy in copies:
        copy.wait()
    panel(PANELS[0], g_ref, left_ref, out_ref)


def panels_kernel(left_ref, g_ref, *out_refs):
    for m, out_ref in zip(PANELS[1:], out_refs):
        panel(m, g_ref, left_ref, out_ref)


def select_kernel(own_ref, came_ref, keep_ref, give_ref):
    holder = lax.axis_index("core") == lax.axis_index("y") // 2
    own = own_ref[...]
    came = came_ref[...]
    keep_ref[...] = jnp.where(holder, own, came)
    give_ref[...] = jnp.where(holder, came, own)


def rows_of(half):
    return pl.ds(pl.multiple_of(half * BLOCK, BLOCK), BLOCK)


def join_kernel(one_ref, three_ref, kept_ref, swapped_ref, out_ref, sems):
    core = lax.axis_index("core")
    y = lax.axis_index("y")
    pieces = [(kept_ref, y % 2, core), (swapped_ref, y % 2, 1 - core)]
    for m, piece_ref in ((1, one_ref), (3, three_ref)):
        source = jnp.bitwise_xor(y, m)
        half = jnp.where(source // 2 == core, core, 1 - core)
        pieces.append((piece_ref, source % 2, half))
    copies = [
        pltpu.make_async_copy(piece, out_ref.at[:, bin_index, rows_of(half), :], sems.at[index])
        for index, (piece, bin_index, half) in enumerate(pieces)
    ]
    for copy in copies:
        copy.start()
    for copy in copies:
        copy.wait()


def call(kernel, shapes, *args, spaces=None, out_space=pltpu.VMEM, scratch=(), aliases=None, flops=0, mib=16):
    shapes = [shape if isinstance(shape, jax.ShapeDtypeStruct) else bf16(shape) for shape in shapes]
    spaces = spaces or [pltpu.VMEM] * len(args)
    cost = None
    if flops is not None:
        moved = sum(arg.size * arg.dtype.itemsize for arg in args)
        moved += sum(math.prod(shape.shape) * shape.dtype.itemsize for shape in shapes)
        cost = pl.CostEstimate(flops=flops, bytes_accessed=moved, transcendentals=0)
    results = pl.pallas_call(
        kernel,
        out_shape=shapes,
        in_specs=[pl.BlockSpec(memory_space=space) for space in spaces],
        out_specs=[pl.BlockSpec(memory_space=out_space)] * len(shapes),
        scratch_shapes=list(scratch),
        input_output_aliases=aliases or {},
        cost_estimate=cost,
        compiler_params=pltpu.CompilerParams(vmem_limit_bytes=mib * 1024 * 1024),
    )(*args)
    return results[0] if len(shapes) == 1 else results


def bf16(shape):
    return jax.ShapeDtypeStruct(shape, jnp.bfloat16)


def pair_z(value, first):
    moves = [(z, (z + (1 if (z % 2 == 1) == first else -1)) % NB) for z in range(NB)]
    return lax.ppermute(value, Z, moves)


def carry(value):
    moves = [(z, (z - 1) % NB) for z in range(NB)]
    moves += [(NB + z, NB + (z + 1) % NB) for z in range(NB)]
    return lax.ppermute(value, ("core",) + Z, moves)


def other_core(value):
    return lax.ppermute(value, "core", [(0, 1), (1, 0)])


def panel_moves(m):
    moves = []
    for core in range(2):
        for y in range(GROUP):
            if core == y // 2:
                target = (core, y ^ m)
            else:
                target = (1 - core, y ^ m ^ 2)
            moves.append((core * GROUP + y, target[0] * GROUP + target[1]))
    return moves


def partial_gram(diffs, single, pairs, values, offsets=None):
    count = 2 * len(diffs)
    shapes = [jax.ShapeDtypeStruct((count, HALF, HALF), jnp.float32), bf16((count, HALF, HALF))]
    spaces = [pltpu.VMEM] * len(values)
    if offsets is not None:
        shapes.append(jax.ShapeDtypeStruct((F, HALF), jnp.float32))
        values = (*values, offsets)
        spaces.append(pltpu.SMEM)
    return call(
        functools.partial(gram_kernel, diffs, single, pairs),
        shapes,
        *values,
        spaces=spaces,
        flops=count * 2 * BLOCK * BLOCK * KK,
    )


def on_device(records, offsets):
    outgoing = call(
        turn_kernel,
        [(F, REC_DEV, HALF)],
        records,
        scratch=[pltpu.VMEM((REC_DEV * F, HALF), jnp.float32)],
    )
    arrived = lax.all_to_all(outgoing, ("x", "y"), 0, 0, tiled=True)
    here = call(pack_kernel, [(BLOCK, KK)], arrived)
    first = pair_z(here, True)
    second = pair_z(here, False)
    first2 = pair_z(second, True)
    second2 = pair_z(first, False)
    near, near_theirs, coefs = partial_gram(NEAR_DIFFS, (0,), (1,), (here, first, second), offsets)
    near_other = other_core(near_theirs)
    far, far_theirs = partial_gram(FAR_DIFFS, (), (1, 2), (first, second, first2, second2))
    far_other = other_core(far_theirs)
    strip = call(add_kernel, [(F, HALF, HALF)], near, near_other, far, far_other)
    bins = lax.all_to_all(strip, ("x", "y"), 0, 0, tiled=True)
    windowed = call(window_kernel, [(F, HALF, HALF)], coefs, bins)
    mine = lax.all_to_all(windowed, ("x", "y"), 0, 0, tiled=True)
    own = {}
    other = {}
    own[0], other[0] = mine, other_core(mine)
    pieces = {(0, True, True): own[0], (0, True, False): other[0]}
    for step in range(1, NB // 2 + 1):
        own[step] = carry(own[step - 1])
        pieces[(step, True, True)] = own[step]
        if step < NB // 2:
            other[step] = carry(other[step - 1])
            pieces[(step, True, False)] = other[step]
        pieces[(step, False, False)] = other_core(own[step])
        if step < NB // 2:
            pieces[(step, False, True)] = other_core(other[step])
    pieces = [pieces[key] for key in PIECES]
    whole_shape = (2, NB, F, HALF, HALF)
    whole, left = call(
        prepare_kernel,
        [whole_shape, (2 * BLOCK, S)],
        *pieces[:-2],
        spaces=[pl.ANY] * (NPIECES - 2),
        scratch=[pltpu.SemaphoreType.DMA((NPIECES - 2,))],
    )
    tile = (2, BLOCK, BLOCK)
    out_shape = (2, 2, 2 * BLOCK, BLOCK)
    panels = {}
    whole, panels[PANELS[0]] = call(
        first_panel_kernel,
        [whole_shape, tile],
        whole,
        left,
        *pieces[-2:],
        spaces=[pltpu.VMEM, pltpu.VMEM, pl.ANY, pl.ANY],
        scratch=[pltpu.SemaphoreType.DMA((2,))],
        aliases={0: 0},
        flops=None,
    )
    rest = call(panels_kernel, [tile] * (GROUP - 1), left, whole, flops=None)
    panels.update(zip(PANELS[1:], rest))
    arrived = {2: lax.ppermute(panels[2], "y", [(y, y ^ 2) for y in range(GROUP)])}
    for m in (1, 3):
        arrived[m] = lax.ppermute(panels[m], ("core", "y"), panel_moves(m))
    kept, given = call(select_kernel, [tile, tile], panels[0], arrived[2], flops=None)
    swapped = other_core(given)
    return call(
        join_kernel,
        [out_shape],
        arrived[1],
        arrived[3],
        kept,
        swapped,
        spaces=[pl.ANY] * GROUP,
        out_space=pl.ANY,
        scratch=[pltpu.SemaphoreType.DMA((GROUP,))],
        flops=None,
    )


def solution(mesh):
    fine = Mesh(mesh.devices.reshape(4, 2, 4, 2, 4), ("x", "core", "zh", "zl", "y"))
    return jax.shard_map(
        on_device,
        mesh=fine,
        in_specs=(P(("x", "core"), None, None, ("zh", "zl", "y")), P()),
        out_specs=P(None, ("x", "core"), "zh", ("zl", "y")),
        check_vma=False,
    )
```

```python
import functools
import math

import jax
import jax.numpy as jnp
import numpy as np
from jax import lax
from jax.experimental import pallas as pl
from jax.experimental.pallas import tpu as pltpu
from jax.sharding import Mesh, PartitionSpec as P

S = 2048
F = 16
RECORDS = 384
BLOCK = 256
HALF = 128
NOFF = 4
NB = 8
REC_DEV = 48
GROUP = 4
NK = GROUP * REC_DEV
KK = 2 * NK
NEAR_DIFFS = (0, 1, 7, 2, 6)
FAR_DIFFS = (3, 5, 4)
PANELS = (2, 1, 3, 0)
Z = ("zh", "zl")


def lag_profile():
    lag = np.minimum(np.arange(F), F - np.arange(F))
    rows = []
    for offset in range(NOFF):
        inside = (lag >= offset + 2) & (lag < offset + 5)
        weights = np.where(inside, 1.0, 0.1)
        step = np.arange(F // 2 + 1)
        angles = 2.0 * np.pi * (step[:, None] * np.arange(F)[None, :] % F) / F
        rows.append(np.cos(angles) @ weights / F)
    return [[float(value) for value in row] for row in rows]


LAG_PROFILE = lag_profile()


def home_shift(diff):
    return jnp.where(diff <= 4, -(diff // 2), (9 - diff) // 2)


HOME = [0, 0, -1, -1, -2, 2, 1, 1]

PIECES = [(0, True, True), (0, True, False)]
for _step in range(1, NB // 2):
    PIECES += [
        (_step, True, True),
        (_step, True, False),
        (_step, False, False),
        (_step, False, True),
    ]
PIECES += [(NB // 2, True, True), (NB // 2, False, False)]
NPIECES = len(PIECES)


def turn_kernel(records_ref, out_ref, rows_ref):
    for record in range(REC_DEV):
        both = jnp.concatenate([records_ref[record, 0], records_ref[record, 1]], axis=1)
        rows_ref[record * F : (record + 1) * F, :] = both.astype(jnp.float32)
    for f in range(F):
        out_ref[f] = rows_ref[pl.ds(f, REC_DEV, stride=F), :].astype(jnp.bfloat16)


def pack_kernel(y_ref, out_ref):
    for part in range(GROUP):
        rows = jnp.concatenate([y_ref[line * GROUP + part] for line in range(GROUP)], axis=0)
        turned = rows.astype(jnp.float32).T.astype(jnp.bfloat16)
        both = jnp.concatenate([turned[:64], turned[64:]], axis=1)
        out_ref[part * 64 : (part + 1) * 64, :] = both


def write_coefs(offsets_ref, coefs_ref):
    piece = lax.axis_index("x") * GROUP + lax.axis_index("y")
    plane = lax.axis_index("zh") * 2 + lax.axis_index("zl")
    diff = piece // 2
    a = (plane + home_shift(diff) + NB) % NB
    b = (a + diff) % NB
    shift = (offsets_ref[a, b] + offsets_ref[b, a]) % NOFF
    for step in range(F // 2 + 1):
        value = jnp.float32(LAG_PROFILE[0][step])
        for offset in range(1, NOFF):
            value = jnp.where(shift == offset, jnp.float32(LAG_PROFILE[offset][step]), value)
        coefs_ref[step : step + 1, :] = jnp.full((1, HALF), value, jnp.float32)


def gram_kernel(diffs, single, pairs, *refs):
    count = len(single) + 2 * len(pairs)
    if len(refs) > count + 2:
        write_coefs(refs[count], refs[-1])
        refs = refs[:count] + refs[count + 1 : -1]
    first_core = lax.axis_index("core") == 0
    even = lax.axis_index("zl") == 0
    rights = {plane: refs[index][...] for index, plane in enumerate(single)}
    for index, plane in enumerate(pairs):
        first = refs[len(single) + 2 * index][...]
        second = refs[len(single) + 2 * index + 1][...]
        rights[-plane] = jnp.where(even, first, second)
        rights[plane] = jnp.where(even, second, first)
    mine_ref, theirs_ref = refs[count:]
    lane = lax.broadcasted_iota(jnp.int32, (BLOCK, KK), 1)
    sign = jnp.where(lane < NK, -1.0, 1.0).astype(jnp.float32)
    scale = jnp.float32(1.0 / math.sqrt(RECORDS))
    lefts = {}
    for plane in sorted({HOME[diff] for diff in diffs}):
        top = rights[plane]
        bottom = (pltpu.roll(top.astype(jnp.float32), NK, 1) * sign).astype(jnp.bfloat16)
        lefts[plane] = jnp.concatenate([top, bottom], axis=0)
    for index, diff in enumerate(diffs):
        a = HOME[diff]
        b = (a + diff + 3) % NB - 3
        both = lax.dot_general(
            lefts[a], rights[b], (((1,), (1,)), ((), ())), preferred_element_type=jnp.float32
        )
        tile = (both[:BLOCK] + both[BLOCK:]) * scale
        mine = jnp.where(first_core, tile[:HALF], tile[HALF:])
        theirs = jnp.where(first_core, tile[HALF:], tile[:HALF]).astype(jnp.bfloat16)
        for side in range(2):
            columns = slice(side * HALF, (side + 1) * HALF)
            mine_ref[2 * index + side] = mine[:, columns]
            theirs_ref[2 * index + side] = theirs[:, columns]


def add_kernel(near_ref, near_other_ref, far_ref, far_other_ref, out_ref):
    for diffs, mine_ref, other_ref in (
        (NEAR_DIFFS, near_ref, near_other_ref),
        (FAR_DIFFS, far_ref, far_other_ref),
    ):
        for index, diff in enumerate(diffs):
            for side in range(2):
                total = mine_ref[2 * index + side] + other_ref[2 * index + side].astype(jnp.float32)
                out_ref[2 * diff + side] = total.astype(jnp.bfloat16)


def window_kernel(coefs_ref, in_ref, out_ref):
    half = F // 2
    coefs = [coefs_ref[step : step + 1, :] for step in range(half + 1)]
    even = [0.5 * (coefs[step] + coefs[half - step]) for step in range(half // 2 + 1)]
    odd = [0.5 * (coefs[step] - coefs[half - step]) for step in range(half // 2)]

    def chunk(index, carry):
        rows = pl.ds(pl.multiple_of(index * 16, 16), 16)
        data = [in_ref[g, rows, :].astype(jnp.float32) for g in range(F)]
        sums = [data[f] + data[f + half] for f in range(half)]
        differences = [data[f] - data[f + half] for f in range(half)]
        differences += [data[f + half] - data[f] for f in range(half)]
        for f in range(half):
            plus = even[0] * sums[f] + even[half // 2] * sums[(f + half // 2) % half]
            minus = odd[0] * differences[f]
            for step in range(1, half // 2):
                plus = plus + even[step] * (sums[(f + step) % half] + sums[(f - step) % half])
                pair = differences[(f + step) % F] + differences[(f - step) % F]
                minus = minus + odd[step] * pair
            out_ref[f, rows, :] = (plus + minus).astype(jnp.bfloat16)
            out_ref[f + half, rows, :] = (plus - minus).astype(jnp.bfloat16)
        return carry

    lax.fori_loop(0, HALF // 16, chunk, 0)


def place():
    core = lax.axis_index("core")
    zh = lax.axis_index("zh")
    zl = lax.axis_index("zl")
    return core, 2 * zh + zl, 2 * zh + core, 4 * zl


def copy_in(entry, piece_ref, g_ref, sem):
    step, carried, own = entry
    core, here, _, _ = place()
    away = jnp.where(core == 0, 1, -1)
    plane = (here + (away if carried else -away) * step + NB) % NB
    half = core if own else 1 - core
    return pltpu.make_async_copy(piece_ref, g_ref.at[half, plane], sem)


def read_block(g_ref, a, diff):
    plane = (a - home_shift(diff) + NB) % NB
    halves = [
        jnp.concatenate([g_ref[h, plane, 2 * diff], g_ref[h, plane, 2 * diff + 1]], axis=1)
        for h in range(2)
    ]
    return jnp.concatenate(halves, axis=0)


def prepare_kernel(*refs):
    pieces = refs[: NPIECES - 2]
    g_ref, left_ref, sems = refs[NPIECES - 2 :]
    _, _, i, _ = place()
    copies = []
    for index, piece_ref in enumerate(pieces):
        copy = copy_in(PIECES[index], piece_ref, g_ref, sems.at[index])
        copy.start()
        copies.append(copy)
    for copy in copies:
        copy.wait()
    for step in range(NB):
        columns = pl.ds(step * BLOCK, BLOCK)
        left_ref[:BLOCK, columns] = read_block(g_ref, i, jnp.int32(step))
        k = (i + step) % NB
        across = read_block(g_ref, k, jnp.int32((NB - step) % NB))
        left_ref[BLOCK:, columns] = across.astype(jnp.float32).T.astype(jnp.bfloat16)


def panel(m, g_ref, left_ref, out_ref):
    core, _, i, first = place()
    y = lax.axis_index("y")
    aside = jnp.where(core == y // 2, 0, 2) if m % 2 == 1 else 0
    j = first + jnp.bitwise_xor(y, jnp.bitwise_xor(m, aside))
    downs = []
    acrosses = []
    for step in range(NB):
        k = (i + step) % NB
        downs.append(read_block(g_ref, k, (j - k + NB) % NB))
        acrosses.append(read_block(g_ref, j, (k - j + NB) % NB))
    down = jnp.concatenate(downs, axis=0)
    across = jnp.concatenate(acrosses, axis=1)
    first = jnp.dot(left_ref[...], down, preferred_element_type=jnp.float32)
    second = lax.dot_general(
        left_ref[...], across, (((1,), (1,)), ((), ())), preferred_element_type=jnp.float32
    )
    scale = jnp.float32(0.5 / math.sqrt(S))
    out_ref[0] = ((second[:BLOCK] + first[BLOCK:]) * scale).astype(jnp.bfloat16)
    out_ref[1] = ((first[:BLOCK] - second[BLOCK:]) * scale).astype(jnp.bfloat16)


def first_panel_kernel(old_ref, left_ref, last_ref, last_swap_ref, g_ref, out_ref, sems):
    del old_ref
    copies = [
        copy_in(PIECES[-2], last_ref, g_ref, sems.at[0]),
        copy_in(PIECES[-1], last_swap_ref, g_ref, sems.at[1]),
    ]
    for copy in copies:
        copy.start()
    for copy in copies:
        copy.wait()
    panel(PANELS[0], g_ref, left_ref, out_ref)


def panels_kernel(left_ref, g_ref, *out_refs):
    for m, out_ref in zip(PANELS[1:], out_refs):
        panel(m, g_ref, left_ref, out_ref)


def select_kernel(own_ref, came_ref, keep_ref, give_ref):
    holder = lax.axis_index("core") == lax.axis_index("y") // 2
    own = own_ref[...]
    came = came_ref[...]
    keep_ref[...] = jnp.where(holder, own, came)
    give_ref[...] = jnp.where(holder, came, own)


def rows_of(half):
    return pl.ds(pl.multiple_of(half * BLOCK, BLOCK), BLOCK)


def join_kernel(one_ref, three_ref, kept_ref, swapped_ref, out_ref, sems):
    core = lax.axis_index("core")
    y = lax.axis_index("y")
    pieces = [(kept_ref, y % 2, core), (swapped_ref, y % 2, 1 - core)]
    for m, piece_ref in ((1, one_ref), (3, three_ref)):
        source = jnp.bitwise_xor(y, m)
        half = jnp.where(source // 2 == core, core, 1 - core)
        pieces.append((piece_ref, source % 2, half))
    copies = [
        pltpu.make_async_copy(piece, out_ref.at[:, bin_index, rows_of(half), :], sems.at[index])
        for index, (piece, bin_index, half) in enumerate(pieces)
    ]
    for copy in copies:
        copy.start()
    for copy in copies:
        copy.wait()


def call(kernel, shapes, *args, spaces=None, out_space=pltpu.VMEM, scratch=(), aliases=None, flops=0, mib=16):
    shapes = [shape if isinstance(shape, jax.ShapeDtypeStruct) else bf16(shape) for shape in shapes]
    spaces = spaces or [pltpu.VMEM] * len(args)
    cost = None
    if flops is not None:
        moved = sum(arg.size * arg.dtype.itemsize for arg in args)
        moved += sum(math.prod(shape.shape) * shape.dtype.itemsize for shape in shapes)
        cost = pl.CostEstimate(flops=flops, bytes_accessed=moved, transcendentals=0)
    results = pl.pallas_call(
        kernel,
        out_shape=shapes,
        in_specs=[pl.BlockSpec(memory_space=space) for space in spaces],
        out_specs=[pl.BlockSpec(memory_space=out_space)] * len(shapes),
        scratch_shapes=list(scratch),
        input_output_aliases=aliases or {},
        cost_estimate=cost,
        compiler_params=pltpu.CompilerParams(vmem_limit_bytes=mib * 1024 * 1024),
    )(*args)
    return results[0] if len(shapes) == 1 else results


def bf16(shape):
    return jax.ShapeDtypeStruct(shape, jnp.bfloat16)


def pair_z(value, first):
    moves = [(z, (z + (1 if (z % 2 == 1) == first else -1)) % NB) for z in range(NB)]
    return lax.ppermute(value, Z, moves)


def carry(value):
    moves = [(z, (z - 1) % NB) for z in range(NB)]
    moves += [(NB + z, NB + (z + 1) % NB) for z in range(NB)]
    return lax.ppermute(value, ("core",) + Z, moves)


def other_core(value):
    return lax.ppermute(value, "core", [(0, 1), (1, 0)])


def panel_moves(m):
    moves = []
    for core in range(2):
        for y in range(GROUP):
            if core == y // 2:
                target = (core, y ^ m)
            else:
                target = (1 - core, y ^ m ^ 2)
            moves.append((core * GROUP + y, target[0] * GROUP + target[1]))
    return moves


def partial_gram(diffs, single, pairs, values, offsets=None):
    count = 2 * len(diffs)
    shapes = [jax.ShapeDtypeStruct((count, HALF, HALF), jnp.float32), bf16((count, HALF, HALF))]
    spaces = [pltpu.VMEM] * len(values)
    if offsets is not None:
        shapes.append(jax.ShapeDtypeStruct((F, HALF), jnp.float32))
        values = (*values, offsets)
        spaces.append(pltpu.SMEM)
    return call(
        functools.partial(gram_kernel, diffs, single, pairs),
        shapes,
        *values,
        spaces=spaces,
        flops=count * 2 * BLOCK * BLOCK * KK,
    )


def on_device(records, offsets):
    outgoing = call(
        turn_kernel,
        [(F, REC_DEV, HALF)],
        records,
        scratch=[pltpu.VMEM((REC_DEV * F, HALF), jnp.float32)],
    )
    arrived = lax.all_to_all(outgoing, ("x", "y"), 0, 0, tiled=True)
    here = call(pack_kernel, [(BLOCK, KK)], arrived)
    first = pair_z(here, True)
    second = pair_z(here, False)
    first2 = pair_z(second, True)
    second2 = pair_z(first, False)
    near, near_theirs, coefs = partial_gram(NEAR_DIFFS, (0,), (1,), (here, first, second), offsets)
    near_other = other_core(near_theirs)
    far, far_theirs = partial_gram(FAR_DIFFS, (), (1, 2), (first, second, first2, second2))
    far_other = other_core(far_theirs)
    strip = call(add_kernel, [(F, HALF, HALF)], near, near_other, far, far_other)
    bins = lax.all_to_all(strip, ("x", "y"), 0, 0, tiled=True)
    windowed = call(window_kernel, [(F, HALF, HALF)], coefs, bins)
    mine = lax.all_to_all(windowed, ("x", "y"), 0, 0, tiled=True)
    own = {}
    other = {}
    own[0], other[0] = mine, other_core(mine)
    pieces = {(0, True, True): own[0], (0, True, False): other[0]}
    for step in range(1, NB // 2 + 1):
        own[step] = carry(own[step - 1])
        pieces[(step, True, True)] = own[step]
        if step < NB // 2:
            other[step] = carry(other[step - 1])
            pieces[(step, True, False)] = other[step]
        pieces[(step, False, False)] = other_core(own[step])
        if step < NB // 2:
            pieces[(step, False, True)] = other_core(other[step])
    pieces = [pieces[key] for key in PIECES]
    whole_shape = (2, NB, F, HALF, HALF)
    whole, left = call(
        prepare_kernel,
        [whole_shape, (2 * BLOCK, S)],
        *pieces[:-2],
        spaces=[pl.ANY] * (NPIECES - 2),
        scratch=[pltpu.SemaphoreType.DMA((NPIECES - 2,))],
    )
    tile = (2, BLOCK, BLOCK)
    out_shape = (2, 2, 2 * BLOCK, BLOCK)
    panels = {}
    whole, panels[PANELS[0]] = call(
        first_panel_kernel,
        [whole_shape, tile],
        whole,
        left,
        *pieces[-2:],
        spaces=[pltpu.VMEM, pltpu.VMEM, pl.ANY, pl.ANY],
        scratch=[pltpu.SemaphoreType.DMA((2,))],
        aliases={0: 0},
        flops=None,
    )
    rest = call(panels_kernel, [tile] * (GROUP - 1), left, whole, flops=None)
    panels.update(zip(PANELS[1:], rest))
    arrived = {2: lax.ppermute(panels[2], "y", [(y, y ^ 2) for y in range(GROUP)])}
    for m in (1, 3):
        arrived[m] = lax.ppermute(panels[m], ("core", "y"), panel_moves(m))
    kept, given = call(select_kernel, [tile, tile], panels[0], arrived[2], flops=None)
    swapped = other_core(given)
    return call(
        join_kernel,
        [out_shape],
        arrived[1],
        arrived[3],
        kept,
        swapped,
        spaces=[pl.ANY] * GROUP,
        out_space=pl.ANY,
        scratch=[pltpu.SemaphoreType.DMA((GROUP,))],
        flops=None,
    )


def solution(mesh):
    fine = Mesh(mesh.devices.reshape(4, 2, 4, 2, 4), ("x", "core", "zh", "zl", "y"))
    return jax.shard_map(
        on_device,
        mesh=fine,
        in_specs=(P(("x", "core"), None, None, ("zh", "zl", "y")), P()),
        out_specs=P(None, ("x", "core"), "zh", ("zl", "y")),
        check_vma=False,
    )
```

```python
import functools
import math

import jax
import jax.numpy as jnp
import numpy as np
from jax import lax
from jax.experimental import pallas as pl
from jax.experimental.pallas import tpu as pltpu
from jax.sharding import Mesh, PartitionSpec as P

S = 2048
F = 16
RECORDS = 384
BLOCK = 256
HALF = 128
NOFF = 4
NB = 8
REC_DEV = 48
GROUP = 4
NK = GROUP * REC_DEV
KK = 2 * NK
NEAR_DIFFS = (0, 1, 7, 2, 6)
FAR_DIFFS = (3, 5, 4)
PANELS = (2, 1, 3, 0)
Z = ("zh", "zl")


def lag_profile():
    lag = np.minimum(np.arange(F), F - np.arange(F))
    rows = []
    for offset in range(NOFF):
        inside = (lag >= offset + 2) & (lag < offset + 5)
        weights = np.where(inside, 1.0, 0.1)
        step = np.arange(F // 2 + 1)
        angles = 2.0 * np.pi * (step[:, None] * np.arange(F)[None, :] % F) / F
        rows.append(np.cos(angles) @ weights / F)
    return [[float(value) for value in row] for row in rows]


LAG_PROFILE = lag_profile()


def home_shift(diff):
    return jnp.where(diff <= 4, -(diff // 2), (9 - diff) // 2)


HOME = [0, 0, -1, -1, -2, 2, 1, 1]

PIECES = [(0, True, True), (0, True, False)]
for _step in range(1, NB // 2):
    PIECES += [
        (_step, True, True),
        (_step, True, False),
        (_step, False, False),
        (_step, False, True),
    ]
PIECES += [(NB // 2, True, True), (NB // 2, False, False)]
NPIECES = len(PIECES)


def turn_kernel(records_ref, out_ref, rows_ref):
    for record in range(REC_DEV):
        both = jnp.concatenate([records_ref[record, 0], records_ref[record, 1]], axis=1)
        rows_ref[record * F : (record + 1) * F, :] = both.astype(jnp.float32)
    for f in range(F):
        out_ref[f] = rows_ref[pl.ds(f, REC_DEV, stride=F), :].astype(jnp.bfloat16)


def pack_kernel(y_ref, out_ref):
    for part in range(GROUP):
        rows = jnp.concatenate([y_ref[line * GROUP + part] for line in range(GROUP)], axis=0)
        turned = rows.astype(jnp.float32).T.astype(jnp.bfloat16)
        both = jnp.concatenate([turned[:64], turned[64:]], axis=1)
        out_ref[part * 64 : (part + 1) * 64, :] = both


def write_coefs(offsets_ref, coefs_ref):
    piece = lax.axis_index("x") * GROUP + lax.axis_index("y")
    plane = lax.axis_index("zh") * 2 + lax.axis_index("zl")
    diff = piece // 2
    a = (plane + home_shift(diff) + NB) % NB
    b = (a + diff) % NB
    shift = (offsets_ref[a, b] + offsets_ref[b, a]) % NOFF
    for step in range(F // 2 + 1):
        value = jnp.float32(LAG_PROFILE[0][step])
        for offset in range(1, NOFF):
            value = jnp.where(shift == offset, jnp.float32(LAG_PROFILE[offset][step]), value)
        coefs_ref[step : step + 1, :] = jnp.full((1, HALF), value, jnp.float32)


def gram_kernel(diffs, single, pairs, *refs):
    count = len(single) + 2 * len(pairs)
    if len(refs) > count + 2:
        write_coefs(refs[count], refs[-1])
        refs = refs[:count] + refs[count + 1 : -1]
    first_core = lax.axis_index("core") == 0
    even = lax.axis_index("zl") == 0
    rights = {plane: refs[index][...] for index, plane in enumerate(single)}
    for index, plane in enumerate(pairs):
        first = refs[len(single) + 2 * index][...]
        second = refs[len(single) + 2 * index + 1][...]
        rights[-plane] = jnp.where(even, first, second)
        rights[plane] = jnp.where(even, second, first)
    mine_ref, theirs_ref = refs[count:]
    lane = lax.broadcasted_iota(jnp.int32, (BLOCK, KK), 1)
    sign = jnp.where(lane < NK, -1.0, 1.0).astype(jnp.float32)
    scale = jnp.float32(1.0 / math.sqrt(RECORDS))
    lefts = {}
    for plane in sorted({HOME[diff] for diff in diffs}):
        top = rights[plane]
        bottom = (pltpu.roll(top.astype(jnp.float32), NK, 1) * sign).astype(jnp.bfloat16)
        lefts[plane] = jnp.concatenate([top, bottom], axis=0)
    for index, diff in enumerate(diffs):
        a = HOME[diff]
        b = (a + diff + 3) % NB - 3
        both = lax.dot_general(
            lefts[a], rights[b], (((1,), (1,)), ((), ())), preferred_element_type=jnp.float32
        )
        tile = (both[:BLOCK] + both[BLOCK:]) * scale
        mine = jnp.where(first_core, tile[:HALF], tile[HALF:])
        theirs = jnp.where(first_core, tile[HALF:], tile[:HALF]).astype(jnp.bfloat16)
        for side in range(2):
            columns = slice(side * HALF, (side + 1) * HALF)
            mine_ref[2 * index + side] = mine[:, columns]
            theirs_ref[2 * index + side] = theirs[:, columns]


def add_kernel(near_ref, near_other_ref, far_ref, far_other_ref, out_ref):
    for diffs, mine_ref, other_ref in (
        (NEAR_DIFFS, near_ref, near_other_ref),
        (FAR_DIFFS, far_ref, far_other_ref),
    ):
        for index, diff in enumerate(diffs):
            for side in range(2):
                total = mine_ref[2 * index + side] + other_ref[2 * index + side].astype(jnp.float32)
                out_ref[2 * diff + side] = total.astype(jnp.bfloat16)


def window_kernel(coefs_ref, in_ref, out_ref):
    half = F // 2
    coefs = [coefs_ref[step : step + 1, :] for step in range(half + 1)]
    even = [0.5 * (coefs[step] + coefs[half - step]) for step in range(half // 2 + 1)]
    odd = [0.5 * (coefs[step] - coefs[half - step]) for step in range(half // 2)]

    def chunk(index, carry):
        rows = pl.ds(pl.multiple_of(index * 16, 16), 16)
        data = [in_ref[g, rows, :].astype(jnp.float32) for g in range(F)]
        sums = [data[f] + data[f + half] for f in range(half)]
        differences = [data[f] - data[f + half] for f in range(half)]
        differences += [data[f + half] - data[f] for f in range(half)]
        for f in range(half):
            plus = even[0] * sums[f] + even[half // 2] * sums[(f + half // 2) % half]
            minus = odd[0] * differences[f]
            for step in range(1, half // 2):
                plus = plus + even[step] * (sums[(f + step) % half] + sums[(f - step) % half])
                pair = differences[(f + step) % F] + differences[(f - step) % F]
                minus = minus + odd[step] * pair
            out_ref[f, rows, :] = (plus + minus).astype(jnp.bfloat16)
            out_ref[f + half, rows, :] = (plus - minus).astype(jnp.bfloat16)
        return carry

    lax.fori_loop(0, HALF // 16, chunk, 0, unroll=True)


def place():
    core = lax.axis_index("core")
    zh = lax.axis_index("zh")
    zl = lax.axis_index("zl")
    return core, 2 * zh + zl, 2 * zh + core, 4 * zl


def copy_in(entry, piece_ref, g_ref, sem):
    step, carried, own = entry
    core, here, _, _ = place()
    away = jnp.where(core == 0, 1, -1)
    plane = (here + (away if carried else -away) * step + NB) % NB
    half = core if own else 1 - core
    return pltpu.make_async_copy(piece_ref, g_ref.at[half, plane], sem)


def read_block(g_ref, a, diff):
    plane = (a - home_shift(diff) + NB) % NB
    halves = [
        jnp.concatenate([g_ref[h, plane, 2 * diff], g_ref[h, plane, 2 * diff + 1]], axis=1)
        for h in range(2)
    ]
    return jnp.concatenate(halves, axis=0)


def prepare_kernel(*refs):
    pieces = refs[: NPIECES - 2]
    g_ref, left_ref, sems = refs[NPIECES - 2 :]
    _, _, i, _ = place()
    copies = []
    for index, piece_ref in enumerate(pieces):
        copy = copy_in(PIECES[index], piece_ref, g_ref, sems.at[index])
        copy.start()
        copies.append(copy)
    for copy in copies:
        copy.wait()
    for step in range(NB):
        columns = pl.ds(step * BLOCK, BLOCK)
        left_ref[:BLOCK, columns] = read_block(g_ref, i, jnp.int32(step))
        k = (i + step) % NB
        across = read_block(g_ref, k, jnp.int32((NB - step) % NB))
        left_ref[BLOCK:, columns] = across.astype(jnp.float32).T.astype(jnp.bfloat16)


def panel(m, g_ref, left_ref, out_ref):
    core, _, i, first = place()
    y = lax.axis_index("y")
    aside = jnp.where(core == y // 2, 0, 2) if m % 2 == 1 else 0
    j = first + jnp.bitwise_xor(y, jnp.bitwise_xor(m, aside))
    downs = []
    acrosses = []
    for step in range(NB):
        k = (i + step) % NB
        downs.append(read_block(g_ref, k, (j - k + NB) % NB))
        acrosses.append(read_block(g_ref, j, (k - j + NB) % NB))
    down = jnp.concatenate(downs, axis=0)
    across = jnp.concatenate(acrosses, axis=1)
    first = jnp.dot(left_ref[...], down, preferred_element_type=jnp.float32)
    second = lax.dot_general(
        left_ref[...], across, (((1,), (1,)), ((), ())), preferred_element_type=jnp.float32
    )
    scale = jnp.float32(0.5 / math.sqrt(S))
    out_ref[0] = ((second[:BLOCK] + first[BLOCK:]) * scale).astype(jnp.bfloat16)
    out_ref[1] = ((first[:BLOCK] - second[BLOCK:]) * scale).astype(jnp.bfloat16)


def first_panel_kernel(old_ref, left_ref, last_ref, last_swap_ref, g_ref, out_ref, sems):
    del old_ref
    copies = [
        copy_in(PIECES[-2], last_ref, g_ref, sems.at[0]),
        copy_in(PIECES[-1], last_swap_ref, g_ref, sems.at[1]),
    ]
    for copy in copies:
        copy.start()
    for copy in copies:
        copy.wait()
    panel(PANELS[0], g_ref, left_ref, out_ref)


def panels_kernel(left_ref, g_ref, *out_refs):
    for m, out_ref in zip(PANELS[1:], out_refs):
        panel(m, g_ref, left_ref, out_ref)


def select_kernel(own_ref, came_ref, keep_ref, give_ref):
    holder = lax.axis_index("core") == lax.axis_index("y") // 2
    own = own_ref[...]
    came = came_ref[...]
    keep_ref[...] = jnp.where(holder, own, came)
    give_ref[...] = jnp.where(holder, came, own)


def rows_of(half):
    return pl.ds(pl.multiple_of(half * BLOCK, BLOCK), BLOCK)


def join_kernel(one_ref, three_ref, kept_ref, swapped_ref, out_ref, sems):
    core = lax.axis_index("core")
    y = lax.axis_index("y")
    pieces = [(kept_ref, y % 2, core), (swapped_ref, y % 2, 1 - core)]
    for m, piece_ref in ((1, one_ref), (3, three_ref)):
        source = jnp.bitwise_xor(y, m)
        half = jnp.where(source // 2 == core, core, 1 - core)
        pieces.append((piece_ref, source % 2, half))
    copies = [
        pltpu.make_async_copy(piece, out_ref.at[:, bin_index, rows_of(half), :], sems.at[index])
        for index, (piece, bin_index, half) in enumerate(pieces)
    ]
    for copy in copies:
        copy.start()
    for copy in copies:
        copy.wait()


def call(kernel, shapes, *args, spaces=None, out_space=pltpu.VMEM, scratch=(), aliases=None, flops=0, mib=16):
    shapes = [shape if isinstance(shape, jax.ShapeDtypeStruct) else bf16(shape) for shape in shapes]
    spaces = spaces or [pltpu.VMEM] * len(args)
    cost = None
    if flops is not None:
        moved = sum(arg.size * arg.dtype.itemsize for arg in args)
        moved += sum(math.prod(shape.shape) * shape.dtype.itemsize for shape in shapes)
        cost = pl.CostEstimate(flops=flops, bytes_accessed=moved, transcendentals=0)
    results = pl.pallas_call(
        kernel,
        out_shape=shapes,
        in_specs=[pl.BlockSpec(memory_space=space) for space in spaces],
        out_specs=[pl.BlockSpec(memory_space=out_space)] * len(shapes),
        scratch_shapes=list(scratch),
        input_output_aliases=aliases or {},
        cost_estimate=cost,
        compiler_params=pltpu.CompilerParams(vmem_limit_bytes=mib * 1024 * 1024),
    )(*args)
    return results[0] if len(shapes) == 1 else results


def bf16(shape):
    return jax.ShapeDtypeStruct(shape, jnp.bfloat16)


def pair_z(value, first):
    moves = [(z, (z + (1 if (z % 2 == 1) == first else -1)) % NB) for z in range(NB)]
    return lax.ppermute(value, Z, moves)


def carry(value):
    moves = [(z, (z - 1) % NB) for z in range(NB)]
    moves += [(NB + z, NB + (z + 1) % NB) for z in range(NB)]
    return lax.ppermute(value, ("core",) + Z, moves)


def other_core(value):
    return lax.ppermute(value, "core", [(0, 1), (1, 0)])


def panel_moves(m):
    moves = []
    for core in range(2):
        for y in range(GROUP):
            if core == y // 2:
                target = (core, y ^ m)
            else:
                target = (1 - core, y ^ m ^ 2)
            moves.append((core * GROUP + y, target[0] * GROUP + target[1]))
    return moves


def partial_gram(diffs, single, pairs, values, offsets=None):
    count = 2 * len(diffs)
    shapes = [jax.ShapeDtypeStruct((count, HALF, HALF), jnp.float32), bf16((count, HALF, HALF))]
    spaces = [pltpu.VMEM] * len(values)
    if offsets is not None:
        shapes.append(jax.ShapeDtypeStruct((F, HALF), jnp.float32))
        values = (*values, offsets)
        spaces.append(pltpu.SMEM)
    return call(
        functools.partial(gram_kernel, diffs, single, pairs),
        shapes,
        *values,
        spaces=spaces,
        flops=count * 2 * BLOCK * BLOCK * KK,
    )


def on_device(records, offsets):
    outgoing = call(
        turn_kernel,
        [(F, REC_DEV, HALF)],
        records,
        scratch=[pltpu.VMEM((REC_DEV * F, HALF), jnp.float32)],
    )
    arrived = lax.all_to_all(outgoing, ("x", "y"), 0, 0, tiled=True)
    here = call(pack_kernel, [(BLOCK, KK)], arrived)
    first = pair_z(here, True)
    second = pair_z(here, False)
    first2 = pair_z(second, True)
    second2 = pair_z(first, False)
    near, near_theirs, coefs = partial_gram(NEAR_DIFFS, (0,), (1,), (here, first, second), offsets)
    near_other = other_core(near_theirs)
    far, far_theirs = partial_gram(FAR_DIFFS, (), (1, 2), (first, second, first2, second2))
    far_other = other_core(far_theirs)
    strip = call(add_kernel, [(F, HALF, HALF)], near, near_other, far, far_other)
    bins = lax.all_to_all(strip, ("x", "y"), 0, 0, tiled=True)
    windowed = call(window_kernel, [(F, HALF, HALF)], coefs, bins)
    mine = lax.all_to_all(windowed, ("x", "y"), 0, 0, tiled=True)
    own = {}
    other = {}
    own[0], other[0] = mine, other_core(mine)
    pieces = {(0, True, True): own[0], (0, True, False): other[0]}
    for step in range(1, NB // 2 + 1):
        own[step] = carry(own[step - 1])
        pieces[(step, True, True)] = own[step]
        if step < NB // 2:
            other[step] = carry(other[step - 1])
            pieces[(step, True, False)] = other[step]
        pieces[(step, False, False)] = other_core(own[step])
        if step < NB // 2:
            pieces[(step, False, True)] = other_core(other[step])
    pieces = [pieces[key] for key in PIECES]
    whole_shape = (2, NB, F, HALF, HALF)
    whole, left = call(
        prepare_kernel,
        [whole_shape, (2 * BLOCK, S)],
        *pieces[:-2],
        spaces=[pl.ANY] * (NPIECES - 2),
        scratch=[pltpu.SemaphoreType.DMA((NPIECES - 2,))],
    )
    tile = (2, BLOCK, BLOCK)
    out_shape = (2, 2, 2 * BLOCK, BLOCK)
    panels = {}
    whole, panels[PANELS[0]] = call(
        first_panel_kernel,
        [whole_shape, tile],
        whole,
        left,
        *pieces[-2:],
        spaces=[pltpu.VMEM, pltpu.VMEM, pl.ANY, pl.ANY],
        scratch=[pltpu.SemaphoreType.DMA((2,))],
        aliases={0: 0},
        flops=None,
    )
    rest = call(panels_kernel, [tile] * (GROUP - 1), left, whole, flops=None)
    panels.update(zip(PANELS[1:], rest))
    arrived = {2: lax.ppermute(panels[2], "y", [(y, y ^ 2) for y in range(GROUP)])}
    for m in (1, 3):
        arrived[m] = lax.ppermute(panels[m], ("core", "y"), panel_moves(m))
    kept, given = call(select_kernel, [tile, tile], panels[0], arrived[2], flops=None)
    swapped = other_core(given)
    return call(
        join_kernel,
        [out_shape],
        arrived[1],
        arrived[3],
        kept,
        swapped,
        spaces=[pl.ANY] * GROUP,
        out_space=pl.ANY,
        scratch=[pltpu.SemaphoreType.DMA((GROUP,))],
        flops=None,
    )


def solution(mesh):
    fine = Mesh(mesh.devices.reshape(4, 2, 4, 2, 4), ("x", "core", "zh", "zl", "y"))
    return jax.shard_map(
        on_device,
        mesh=fine,
        in_specs=(P(("x", "core"), None, None, ("zh", "zl", "y")), P()),
        out_specs=P(None, ("x", "core"), "zh", ("zl", "y")),
        check_vma=False,
    )
```

```python
import functools
import math

import jax
import jax.numpy as jnp
import numpy as np
from jax import lax
from jax.experimental import pallas as pl
from jax.experimental.pallas import tpu as pltpu
from jax.sharding import Mesh, PartitionSpec as P

S = 2048
F = 16
RECORDS = 384
BLOCK = 256
HALF = 128
NOFF = 4
NB = 8
REC_DEV = 48
GROUP = 4
NK = GROUP * REC_DEV
KK = 2 * NK
NEAR_DIFFS = (0, 1, 7, 2, 6)
FAR_DIFFS = (3, 5, 4)
PANELS = (2, 1, 3, 0)
Z = ("zh", "zl")


def lag_profile():
    lag = np.minimum(np.arange(F), F - np.arange(F))
    rows = []
    for offset in range(NOFF):
        inside = (lag >= offset + 2) & (lag < offset + 5)
        weights = np.where(inside, 1.0, 0.1)
        step = np.arange(F // 2 + 1)
        angles = 2.0 * np.pi * (step[:, None] * np.arange(F)[None, :] % F) / F
        rows.append(np.cos(angles) @ weights / F)
    return [[float(value) for value in row] for row in rows]


LAG_PROFILE = lag_profile()


def home_shift(diff):
    return jnp.where(diff <= 4, -(diff // 2), (9 - diff) // 2)


HOME = [0, 0, -1, -1, -2, 2, 1, 1]

PIECES = [(0, True, True), (0, True, False)]
for _step in range(1, NB // 2):
    PIECES += [
        (_step, True, True),
        (_step, True, False),
        (_step, False, False),
        (_step, False, True),
    ]
PIECES += [(NB // 2, True, True), (NB // 2, False, False)]
NPIECES = len(PIECES)
EARLY = 10


def turn_kernel(records_ref, out_ref, rows_ref):
    for record in range(REC_DEV):
        both = jnp.concatenate([records_ref[record, 0], records_ref[record, 1]], axis=1)
        rows_ref[record * F : (record + 1) * F, :] = both.astype(jnp.float32)
    for f in range(F):
        out_ref[f] = rows_ref[pl.ds(f, REC_DEV, stride=F), :].astype(jnp.bfloat16)


def pack_kernel(y_ref, out_ref):
    for part in range(GROUP):
        rows = jnp.concatenate([y_ref[line * GROUP + part] for line in range(GROUP)], axis=0)
        turned = rows.astype(jnp.float32).T.astype(jnp.bfloat16)
        both = jnp.concatenate([turned[:64], turned[64:]], axis=1)
        out_ref[part * 64 : (part + 1) * 64, :] = both


def write_coefs(offsets_ref, coefs_ref):
    piece = lax.axis_index("x") * GROUP + lax.axis_index("y")
    plane = lax.axis_index("zh") * 2 + lax.axis_index("zl")
    diff = piece // 2
    a = (plane + home_shift(diff) + NB) % NB
    b = (a + diff) % NB
    shift = (offsets_ref[a, b] + offsets_ref[b, a]) % NOFF
    for step in range(F // 2 + 1):
        value = jnp.float32(LAG_PROFILE[0][step])
        for offset in range(1, NOFF):
            value = jnp.where(shift == offset, jnp.float32(LAG_PROFILE[offset][step]), value)
        coefs_ref[step : step + 1, :] = jnp.full((1, HALF), value, jnp.float32)


def gram_kernel(diffs, single, pairs, *refs):
    count = len(single) + 2 * len(pairs)
    if len(refs) > count + 2:
        write_coefs(refs[count], refs[-1])
        refs = refs[:count] + refs[count + 1 : -1]
    first_core = lax.axis_index("core") == 0
    even = lax.axis_index("zl") == 0
    rights = {plane: refs[index][...] for index, plane in enumerate(single)}
    for index, plane in enumerate(pairs):
        first = refs[len(single) + 2 * index][...]
        second = refs[len(single) + 2 * index + 1][...]
        rights[-plane] = jnp.where(even, first, second)
        rights[plane] = jnp.where(even, second, first)
    mine_ref, theirs_ref = refs[count:]
    lane = lax.broadcasted_iota(jnp.int32, (BLOCK, KK), 1)
    sign = jnp.where(lane < NK, -1.0, 1.0).astype(jnp.float32)
    scale = jnp.float32(1.0 / math.sqrt(RECORDS))
    lefts = {}
    for plane in sorted({HOME[diff] for diff in diffs}):
        top = rights[plane]
        bottom = (pltpu.roll(top.astype(jnp.float32), NK, 1) * sign).astype(jnp.bfloat16)
        lefts[plane] = jnp.concatenate([top, bottom], axis=0)
    for index, diff in enumerate(diffs):
        a = HOME[diff]
        b = (a + diff + 3) % NB - 3
        both = lax.dot_general(
            lefts[a], rights[b], (((1,), (1,)), ((), ())), preferred_element_type=jnp.float32
        )
        tile = (both[:BLOCK] + both[BLOCK:]) * scale
        mine = jnp.where(first_core, tile[:HALF], tile[HALF:])
        theirs = jnp.where(first_core, tile[HALF:], tile[:HALF]).astype(jnp.bfloat16)
        for side in range(2):
            columns = slice(side * HALF, (side + 1) * HALF)
            mine_ref[2 * index + side] = mine[:, columns]
            theirs_ref[2 * index + side] = theirs[:, columns]


def add_kernel(near_ref, near_other_ref, far_ref, far_other_ref, out_ref):
    for diffs, mine_ref, other_ref in (
        (NEAR_DIFFS, near_ref, near_other_ref),
        (FAR_DIFFS, far_ref, far_other_ref),
    ):
        for index, diff in enumerate(diffs):
            for side in range(2):
                total = mine_ref[2 * index + side] + other_ref[2 * index + side].astype(jnp.float32)
                out_ref[2 * diff + side] = total.astype(jnp.bfloat16)


def window_kernel(coefs_ref, in_ref, out_ref):
    half = F // 2
    coefs = [coefs_ref[step : step + 1, :] for step in range(half + 1)]
    even = [0.5 * (coefs[step] + coefs[half - step]) for step in range(half // 2 + 1)]
    odd = [0.5 * (coefs[step] - coefs[half - step]) for step in range(half // 2)]

    def chunk(index, carry):
        rows = pl.ds(pl.multiple_of(index * 16, 16), 16)
        data = [in_ref[g, rows, :].astype(jnp.float32) for g in range(F)]
        sums = [data[f] + data[f + half] for f in range(half)]
        differences = [data[f] - data[f + half] for f in range(half)]
        differences += [data[f + half] - data[f] for f in range(half)]
        for f in range(half):
            plus = even[0] * sums[f] + even[half // 2] * sums[(f + half // 2) % half]
            minus = odd[0] * differences[f]
            for step in range(1, half // 2):
                plus = plus + even[step] * (sums[(f + step) % half] + sums[(f - step) % half])
                pair = differences[(f + step) % F] + differences[(f - step) % F]
                minus = minus + odd[step] * pair
            out_ref[f, rows, :] = (plus + minus).astype(jnp.bfloat16)
            out_ref[f + half, rows, :] = (plus - minus).astype(jnp.bfloat16)
        return carry

    lax.fori_loop(0, HALF // 16, chunk, 0, unroll=True)


def place():
    core = lax.axis_index("core")
    zh = lax.axis_index("zh")
    zl = lax.axis_index("zl")
    return core, 2 * zh + zl, 2 * zh + core, 4 * zl


def copy_in(entry, piece_ref, g_ref, sem):
    step, carried, own = entry
    core, here, _, _ = place()
    away = jnp.where(core == 0, 1, -1)
    plane = (here + (away if carried else -away) * step + NB) % NB
    half = core if own else 1 - core
    return pltpu.make_async_copy(piece_ref, g_ref.at[half, plane], sem)


def read_block(g_ref, a, diff):
    plane = (a - home_shift(diff) + NB) % NB
    halves = [
        jnp.concatenate([g_ref[h, plane, 2 * diff], g_ref[h, plane, 2 * diff + 1]], axis=1)
        for h in range(2)
    ]
    return jnp.concatenate(halves, axis=0)


def gather_kernel(*refs):
    pieces = refs[:EARLY]
    g_ref, sems = refs[EARLY:]
    copies = [copy_in(PIECES[i], piece_ref, g_ref, sems.at[i]) for i, piece_ref in enumerate(pieces)]
    for copy in copies:
        copy.start()
    for copy in copies:
        copy.wait()


def prepare_kernel(old_ref, *refs):
    del old_ref
    count = NPIECES - 1 - EARLY
    pieces = refs[:count]
    g_ref, left_ref, sems = refs[count:]
    _, _, i, _ = place()
    copies = []
    for index, piece_ref in enumerate(pieces):
        copy = copy_in(PIECES[EARLY + index], piece_ref, g_ref, sems.at[index])
        copy.start()
        copies.append(copy)
    for copy in copies:
        copy.wait()
    for step in range(NB):
        columns = pl.ds(step * BLOCK, BLOCK)
        left_ref[:BLOCK, columns] = read_block(g_ref, i, jnp.int32(step))
        k = (i + step) % NB
        across = read_block(g_ref, k, jnp.int32((NB - step) % NB))
        left_ref[BLOCK:, columns] = across.astype(jnp.float32).T.astype(jnp.bfloat16)


def panel(m, g_ref, left_ref, out_ref):
    core, _, i, first = place()
    y = lax.axis_index("y")
    aside = jnp.where(core == y // 2, 0, 2) if m % 2 == 1 else 0
    j = first + jnp.bitwise_xor(y, jnp.bitwise_xor(m, aside))
    downs = []
    acrosses = []
    for step in range(NB):
        k = (i + step) % NB
        downs.append(read_block(g_ref, k, (j - k + NB) % NB))
        acrosses.append(read_block(g_ref, j, (k - j + NB) % NB))
    down = jnp.concatenate(downs, axis=0)
    across = jnp.concatenate(acrosses, axis=1)
    first = jnp.dot(left_ref[...], down, preferred_element_type=jnp.float32)
    second = lax.dot_general(
        left_ref[...], across, (((1,), (1,)), ((), ())), preferred_element_type=jnp.float32
    )
    scale = jnp.float32(0.5 / math.sqrt(S))
    out_ref[0] = ((second[:BLOCK] + first[BLOCK:]) * scale).astype(jnp.bfloat16)
    out_ref[1] = ((first[:BLOCK] - second[BLOCK:]) * scale).astype(jnp.bfloat16)


def first_panel_kernel(old_ref, left_ref, last_swap_ref, g_ref, out_ref, sem):
    del old_ref
    copy = copy_in(PIECES[-1], last_swap_ref, g_ref, sem)
    copy.start()
    copy.wait()
    panel(PANELS[0], g_ref, left_ref, out_ref)


def panels_kernel(left_ref, g_ref, *out_refs):
    for m, out_ref in zip(PANELS[1:], out_refs):
        panel(m, g_ref, left_ref, out_ref)


def select_kernel(own_ref, came_ref, keep_ref, give_ref):
    holder = lax.axis_index("core") == lax.axis_index("y") // 2
    own = own_ref[...]
    came = came_ref[...]
    keep_ref[...] = jnp.where(holder, own, came)
    give_ref[...] = jnp.where(holder, came, own)


def rows_of(half):
    return pl.ds(pl.multiple_of(half * BLOCK, BLOCK), BLOCK)


def join_kernel(one_ref, three_ref, kept_ref, swapped_ref, out_ref, sems):
    core = lax.axis_index("core")
    y = lax.axis_index("y")
    pieces = [(kept_ref, y % 2, core), (swapped_ref, y % 2, 1 - core)]
    for m, piece_ref in ((1, one_ref), (3, three_ref)):
        source = jnp.bitwise_xor(y, m)
        half = jnp.where(source // 2 == core, core, 1 - core)
        pieces.append((piece_ref, source % 2, half))
    copies = [
        pltpu.make_async_copy(piece, out_ref.at[:, bin_index, rows_of(half), :], sems.at[index])
        for index, (piece, bin_index, half) in enumerate(pieces)
    ]
    for copy in copies:
        copy.start()
    for copy in copies:
        copy.wait()


def call(kernel, shapes, *args, spaces=None, out_space=pltpu.VMEM, scratch=(), aliases=None, flops=0, mib=16):
    shapes = [shape if isinstance(shape, jax.ShapeDtypeStruct) else bf16(shape) for shape in shapes]
    spaces = spaces or [pltpu.VMEM] * len(args)
    cost = None
    if flops is not None:
        moved = sum(arg.size * arg.dtype.itemsize for arg in args)
        moved += sum(math.prod(shape.shape) * shape.dtype.itemsize for shape in shapes)
        cost = pl.CostEstimate(flops=flops, bytes_accessed=moved, transcendentals=0)
    results = pl.pallas_call(
        kernel,
        out_shape=shapes,
        in_specs=[pl.BlockSpec(memory_space=space) for space in spaces],
        out_specs=[pl.BlockSpec(memory_space=out_space)] * len(shapes),
        scratch_shapes=list(scratch),
        input_output_aliases=aliases or {},
        cost_estimate=cost,
        compiler_params=pltpu.CompilerParams(vmem_limit_bytes=mib * 1024 * 1024),
    )(*args)
    return results[0] if len(shapes) == 1 else results


def bf16(shape):
    return jax.ShapeDtypeStruct(shape, jnp.bfloat16)


def pair_z(value, first):
    moves = [(z, (z + (1 if (z % 2 == 1) == first else -1)) % NB) for z in range(NB)]
    return lax.ppermute(value, Z, moves)


def carry(value):
    moves = [(z, (z - 1) % NB) for z in range(NB)]
    moves += [(NB + z, NB + (z + 1) % NB) for z in range(NB)]
    return lax.ppermute(value, ("core",) + Z, moves)


def other_core(value):
    return lax.ppermute(value, "core", [(0, 1), (1, 0)])


def panel_moves(m):
    moves = []
    for core in range(2):
        for y in range(GROUP):
            if core == y // 2:
                target = (core, y ^ m)
            else:
                target = (1 - core, y ^ m ^ 2)
            moves.append((core * GROUP + y, target[0] * GROUP + target[1]))
    return moves


def partial_gram(diffs, single, pairs, values, offsets=None):
    count = 2 * len(diffs)
    shapes = [jax.ShapeDtypeStruct((count, HALF, HALF), jnp.float32), bf16((count, HALF, HALF))]
    spaces = [pltpu.VMEM] * len(values)
    if offsets is not None:
        shapes.append(jax.ShapeDtypeStruct((F, HALF), jnp.float32))
        values = (*values, offsets)
        spaces.append(pltpu.SMEM)
    return call(
        functools.partial(gram_kernel, diffs, single, pairs),
        shapes,
        *values,
        spaces=spaces,
        flops=count * 2 * BLOCK * BLOCK * KK,
    )


def on_device(records, offsets):
    outgoing = call(
        turn_kernel,
        [(F, REC_DEV, HALF)],
        records,
        scratch=[pltpu.VMEM((REC_DEV * F, HALF), jnp.float32)],
    )
    arrived = lax.all_to_all(outgoing, ("x", "y"), 0, 0, tiled=True)
    here = call(pack_kernel, [(BLOCK, KK)], arrived)
    first = pair_z(here, True)
    second = pair_z(here, False)
    first2 = pair_z(second, True)
    second2 = pair_z(first, False)
    near, near_theirs, coefs = partial_gram(NEAR_DIFFS, (0,), (1,), (here, first, second), offsets)
    near_other = other_core(near_theirs)
    far, far_theirs = partial_gram(FAR_DIFFS, (), (1, 2), (first, second, first2, second2))
    far_other = other_core(far_theirs)
    strip = call(add_kernel, [(F, HALF, HALF)], near, near_other, far, far_other)
    bins = lax.all_to_all(strip, ("x", "y"), 0, 0, tiled=True)
    windowed = call(window_kernel, [(F, HALF, HALF)], coefs, bins)
    mine = lax.all_to_all(windowed, ("x", "y"), 0, 0, tiled=True)
    own = {}
    other = {}
    own[0], other[0] = mine, other_core(mine)
    pieces = {(0, True, True): own[0], (0, True, False): other[0]}
    for step in range(1, NB // 2 + 1):
        own[step] = carry(own[step - 1])
        pieces[(step, True, True)] = own[step]
        if step < NB // 2:
            other[step] = carry(other[step - 1])
            pieces[(step, True, False)] = other[step]
        pieces[(step, False, False)] = other_core(own[step])
        if step < NB // 2:
            pieces[(step, False, True)] = other_core(other[step])
    pieces = [pieces[key] for key in PIECES]
    whole_shape = (2, NB, F, HALF, HALF)
    whole = call(
        gather_kernel,
        [whole_shape],
        *pieces[:EARLY],
        spaces=[pl.ANY] * EARLY,
        scratch=[pltpu.SemaphoreType.DMA((EARLY,))],
    )
    whole, left = call(
        prepare_kernel,
        [whole_shape, (2 * BLOCK, S)],
        whole,
        *pieces[EARLY:-1],
        spaces=[pltpu.VMEM] + [pl.ANY] * (NPIECES - 1 - EARLY),
        scratch=[pltpu.SemaphoreType.DMA((NPIECES - 1 - EARLY,))],
        aliases={0: 0},
    )
    tile = (2, BLOCK, BLOCK)
    out_shape = (2, 2, 2 * BLOCK, BLOCK)
    panels = {}
    whole, panels[PANELS[0]] = call(
        first_panel_kernel,
        [whole_shape, tile],
        whole,
        left,
        pieces[-1],
        spaces=[pltpu.VMEM, pltpu.VMEM, pl.ANY],
        scratch=[pltpu.SemaphoreType.DMA],
        aliases={0: 0},
        flops=None,
    )
    rest = call(panels_kernel, [tile] * (GROUP - 1), left, whole, flops=None)
    panels.update(zip(PANELS[1:], rest))
    arrived = {2: lax.ppermute(panels[2], "y", [(y, y ^ 2) for y in range(GROUP)])}
    for m in (1, 3):
        arrived[m] = lax.ppermute(panels[m], ("core", "y"), panel_moves(m))
    kept, given = call(select_kernel, [tile, tile], panels[0], arrived[2], flops=None)
    swapped = other_core(given)
    return call(
        join_kernel,
        [out_shape],
        arrived[1],
        arrived[3],
        kept,
        swapped,
        spaces=[pl.ANY] * GROUP,
        out_space=pl.ANY,
        scratch=[pltpu.SemaphoreType.DMA((GROUP,))],
        flops=None,
    )


def solution(mesh):
    fine = Mesh(mesh.devices.reshape(4, 2, 4, 2, 4), ("x", "core", "zh", "zl", "y"))
    return jax.shard_map(
        on_device,
        mesh=fine,
        in_specs=(P(("x", "core"), None, None, ("zh", "zl", "y")), P()),
        out_specs=P(None, ("x", "core"), "zh", ("zl", "y")),
        check_vma=False,
    )
```
